32 devices in a mesh: wide: 16 (over z, y, x), narrow: 2 (over core).
Axes of the slice: x: 2, y: 2, z: 4, core: 2. Of those that a mesh axis runs over, the one named last changes fastest.
Arguments:
- inputs: bfloat16 [32768, 768], P('wide'), may hold values from -6 to 6
- segments: int32 [32768], P('wide'), may hold values from 0 to 3, as said below
- valid: int32 [32768], P('wide'), may hold values from 0 to 1, as said below
- w_query: bfloat16 [768, 768], P(None, 'narrow'), may hold values from -0.21875 to 0.21875
- w_key: bfloat16 [768, 768], P(None, 'narrow'), may hold values from -0.21875 to 0.21875
- w_value: bfloat16 [768, 768], P(None, 'narrow'), may hold values from -0.21875 to 0.21875
- b_query: bfloat16 [768], P('narrow'), may hold values from -3 to 3
- b_value: bfloat16 [768], P('narrow'), may hold values from -3 to 3
- w_attn_out: bfloat16 [768, 768], P('narrow'), may hold values from -1.75 to 1.75
- b_attn_out: bfloat16 [768], replicated, may hold values from -3 to 3
- gain_one: bfloat16 [768], replicated, may hold values from 0.099609375 to 1.8984375
- shift_one: bfloat16 [768], replicated, may hold values from -3 to 3
- w_ffn_in: bfloat16 [768, 3072], P(None, 'narrow'), may hold values from -0.21875 to 0.21875
- b_ffn_in: bfloat16 [3072], P('narrow'), may hold values from -3 to 3
- w_ffn_out: bfloat16 [3072, 768], P('narrow'), may hold values from -0.109375 to 0.109375
- b_ffn_out: bfloat16 [768], replicated, may hold values from -3 to 3
- gain_two: bfloat16 [768], replicated, may hold values from 0.099609375 to 1.8984375
- shift_two: bfloat16 [768], replicated, may hold values from -3 to 3
- out_grad: bfloat16 [32768, 768], P('wide'), may hold values from -18 to 18
Outputs:
- output: bfloat16 [32768, 768], P('wide')
- input_grad: bfloat16 [32768, 768], P('wide')
- grad_w_query: float32 [768, 768], P(None, 'narrow')
- grad_w_key: float32 [768, 768], P(None, 'narrow')
- grad_w_value: float32 [768, 768], P(None, 'narrow')
- grad_b_query: float32 [768], P('narrow')
- grad_b_value: float32 [768], P('narrow')
- grad_w_attn_out: float32 [768, 768], P('narrow')
- grad_b_attn_out: float32 [768], replicated
- grad_gain_one: float32 [768], replicated
- grad_shift_one: float32 [768], replicated
- grad_w_ffn_in: float32 [768, 3072], P(None, 'narrow')
- grad_b_ffn_in: float32 [3072], P('narrow')
- grad_w_ffn_out: float32 [3072, 768], P('narrow')
- grad_b_ffn_out: float32 [768], replicated
- grad_gain_two: float32 [768], replicated
- grad_shift_two: float32 [768], replicated
- rms: float32 [4], replicated
The draws below stay inside these ranges and needn't reach their ends.
Inputs may be any that keep to these rules, and one draw needn't show every extreme that they name: `segments`: each packed row of 512 tokens holds exactly four documents: the segment numbers start at 0 and rise by one at each new document; no document starts in the last quarter of a row. In each packed row the valid tokens are a prefix; fewer than 64 slots at the end of a row are padding.
All inputs are finite; a program needn't handle non-finite values.
Results may differ from the reference program's by a relative error of at most 0.015.
Values may be sent and summed in bfloat16 or wider, within the bound.
No kernel may reach another device: no remote copies, remote signals or barrier semaphores. Data moves between devices by JAX's collectives and lax.ppermute only.
A program may use at most 192 MiB of HBM per device.

```python
import math
import jax
import jax.numpy as jnp
from jax import lax

D = 768
HEADS = 12
HEAD_DIM = 64
FF = 3072
SEQ_LEN = 512
SEQ_DEV = 4
TOKENS = 32768


def draw_segments(key, part):
    row_total = TOKENS // SEQ_LEN
    span = SEQ_LEN * 3 // 4 - 1
    row_keys = jax.random.split(key, row_total)

    def row_starts(row_key):
        return jax.random.permutation(row_key, span)[:3].astype(jnp.int32) + 1
    starts = jax.vmap(row_starts)(row_keys)
    position = jnp.arange(SEQ_LEN, dtype=jnp.int32)
    begins = jnp.sum((position[None, :, None] == starts[:, None, :]).astype(jnp.int32), axis=-1)
    counts = jnp.cumsum(begins, axis=1)
    return counts.reshape(TOKENS).astype(jnp.int32)


def draw_valid(key, part):
    position = jnp.arange(TOKENS, dtype=jnp.int32).reshape(-1, SEQ_LEN) % SEQ_LEN
    padding = jax.random.randint(key, (TOKENS // SEQ_LEN, 1), 0, SEQ_LEN // 8)
    kept_mask = position < SEQ_LEN - padding
    return kept_mask.astype(jnp.int32).reshape(TOKENS)


def draw_out_grad(key, part):
    row_ramp = jnp.arange(TOKENS, dtype=jnp.float32) / max(TOKENS - 1, 1)
    base_draw = jnp.clip(jax.random.normal(key, (TOKENS, D), jnp.float32), -6.0, 6.0)
    row_scale = jnp.exp(row_ramp * math.log(3.0))
    return (base_draw * row_scale[:, None]).astype(jnp.bfloat16)


def levels(stream_key, dims, cuts, low, largest):
    def one(dim, blocks):
        heights = jax.random.uniform(jax.random.fold_in(jax.random.fold_in(stream_key, 6), dim), (blocks,), jnp.float32, low / len(cuts), largest / len(cuts))
        return jnp.repeat(jnp.exp(heights), dims[dim] // blocks).reshape((-1,) + (1,) * (len(dims) - dim - 1))

    level = one(*cuts[0])
    for cut in cuts[1:]:
        level = level * one(*cut)
    return level


def noise(key, extent, deviation, most, cuts=(), held_as=jnp.bfloat16):
    factor_of = levels(key, extent, cuts, -0.22, 0.18) if cuts else 1.0
    entries = jax.random.normal(key, extent, jnp.float32) * deviation * factor_of
    return jnp.minimum(jnp.maximum(entries, -most), most).astype(held_as)


def setup_inputs(seed: int = 0) -> dict:
    splits = jax.random.split(jax.random.key(seed), 20)
    inputs = noise(splits[0], (TOKENS, D), 1.0, 6.0, ((0, 16),))
    segments = draw_segments(jax.random.fold_in(splits[19], 71), 0)
    valid = draw_valid(jax.random.fold_in(splits[19], 71), 0)
    w_query = noise(splits[3], (D, D), D ** -0.5, 0.21875, ((1, 2),))
    w_key = noise(splits[4], (D, D), D ** -0.5, 0.21875, ((1, 2),))
    w_value = noise(splits[5], (D, D), D ** -0.5, 0.21875, ((1, 2),))
    b_query = noise(splits[6], (D,), 0.5, 3.0, ((0, 2),))
    b_value = noise(splits[7], (D,), 0.5, 3.0, ((0, 2),))
    w_attn_out = noise(splits[8], (D, D), (D // 64) ** -0.5, 1.75, ((0, 2),))
    b_attn_out = noise(splits[9], (D,), 0.5, 3.0)
    gain_one = jnp.clip(1.0 + 0.18 * jax.random.normal(splits[10], (D,), jnp.float32), 0.099609375, 1.8984375).astype(jnp.bfloat16)
    shift_one = noise(splits[11], (D,), 0.5, 3.0)
    w_ffn_in = noise(splits[12], (D, FF), D ** -0.5, 0.21875, ((1, 2),))
    b_ffn_in = noise(splits[13], (FF,), 0.5, 3.0, ((0, 2),))
    w_ffn_out = noise(splits[14], (FF, D), FF ** -0.5, 0.109375, ((0, 2),))
    b_ffn_out = noise(splits[15], (D,), 0.5, 3.0)
    gain_two = jnp.clip(1.0 + 0.18 * jax.random.normal(splits[16], (D,), jnp.float32), 0.099609375, 1.8984375).astype(jnp.bfloat16)
    shift_two = noise(splits[17], (D,), 0.5, 3.0)
    out_grad = draw_out_grad(jax.random.fold_in(splits[19], 71), 0)
    return dict(inputs=inputs, segments=segments, valid=valid, w_query=w_query, w_key=w_key, w_value=w_value, b_query=b_query, b_value=b_value, w_attn_out=w_attn_out, b_attn_out=b_attn_out, gain_one=gain_one, shift_one=shift_one, w_ffn_in=w_ffn_in, b_ffn_in=b_ffn_in, w_ffn_out=w_ffn_out, b_ffn_out=b_ffn_out, gain_two=gain_two, shift_two=shift_two, out_grad=out_grad)


@jax.custom_vjp
def low(v):
    return lax.optimization_barrier(v.astype(jnp.bfloat16)).astype(jnp.float32)

@jax.custom_vjp
def low_back(v):
    return v

def low_keep(v):
    return (low(v), None)

def low_pass(kept, grad):
    return (grad,)

def back_keep(v):
    return (v, None)

def back_low(kept, grad):
    return (low(grad),)
low.defvjp(low_keep, low_pass)
low_back.defvjp(back_keep, back_low)
norm_eps = 1e-06

def product(left, right):
    return jnp.dot(left, right, precision=lax.Precision.HIGHEST)

def layer_norm(values, gain, shift):
    centred = values - lax.optimization_barrier(jnp.mean(values, axis=-1, keepdims=True))
    variance = lax.optimization_barrier(jnp.mean(centred * centred, axis=-1, keepdims=True))
    return centred * lax.rsqrt(variance + norm_eps) * gain + shift

def attend(packed):
    queries, key_rows, value_rows, seg_row, valid_row = packed
    scores = jnp.einsum('qhd,khd->hqk', queries, key_rows, precision=lax.Precision.HIGHEST) * HEAD_DIM ** (-0.5)
    scores = low_back(scores)
    allowed = (seg_row[:, None] == seg_row[None, :]) & (valid_row[None, :] == 1)
    scores = jnp.where(allowed[None], scores, -1e+30)
    shifted = jnp.exp(scores - lax.optimization_barrier(jnp.max(scores, axis=-1, keepdims=True)))
    weights = low(shifted / lax.optimization_barrier(jnp.sum(shifted, axis=-1, keepdims=True)))
    return jnp.einsum('hqk,khd->qhd', weights, value_rows, precision=lax.Precision.HIGHEST)

def layer(params, hidden, extra_mixed, extra_first, extra_second, segments, valid):
    w_query, w_key, w_value, b_query, b_value, w_attn_out, b_attn_out, gain_one, shift_one, w_ffn_in, b_ffn_in, w_ffn_out, b_ffn_out, gain_two, shift_two = params
    queries = low_back(low(product(hidden, w_query) + b_query))
    key_rows = low_back(low(product(hidden, w_key)))
    value_rows = low_back(low(product(hidden, w_value) + b_value))
    head_shape = (-1, SEQ_LEN, HEADS, HEAD_DIM)
    context = lax.map(jax.checkpoint(attend), (queries.reshape(head_shape), key_rows.reshape(head_shape), value_rows.reshape(head_shape), segments.reshape(-1, SEQ_LEN), valid.reshape(-1, SEQ_LEN)))
    context = low_back(low(context.reshape(hidden.shape[0], D)))
    mixed = hidden + low_back(product(context, w_attn_out)) + b_attn_out + extra_mixed
    first = layer_norm(mixed, gain_one, shift_one) + extra_first
    pre_act = low_back(product(low(first), w_ffn_in) + b_ffn_in)
    activated = low(jax.nn.gelu(pre_act, approximate=False))
    second = first + low_back(product(activated, w_ffn_out)) + b_ffn_out + extra_second
    return layer_norm(second, gain_two, shift_two)

def reference(inputs, segments, valid, w_query, w_key, w_value, b_query, b_value, w_attn_out, b_attn_out, gain_one, shift_one, w_ffn_in, b_ffn_in, w_ffn_out, b_ffn_out, gain_two, shift_two, out_grad):
    params = tuple((p.astype(jnp.float32) for p in (w_query, w_key, w_value, b_query, b_value, w_attn_out, b_attn_out, gain_one, shift_one, w_ffn_in, b_ffn_in, w_ffn_out, b_ffn_out, gain_two, shift_two)))
    group_rows = SEQ_DEV * SEQ_LEN
    group_count = TOKENS // group_rows

    def regroup(array):
        return array.reshape((group_count, group_rows) + array.shape[1:])

    def group_step(carry, item):
        grads_acc, stats_acc = carry
        hidden, seg_rows, valid_rows, cotangent = item
        zeros = jnp.zeros_like(hidden)

        def forward(weights, hidden_in, extra_mixed, extra_first, extra_second):
            return layer(weights, hidden_in, extra_mixed, extra_first, extra_second, seg_rows, valid_rows)
        result, pullback = jax.vjp(forward, params, hidden, zeros, zeros, zeros)
        weight_rows = valid_rows.astype(jnp.float32)
        grad_params, grad_in, grad_mixed, grad_first, grad_second = pullback(cotangent * weight_rows[:, None])
        sums = jnp.stack([jnp.sum(weight_rows * lax.optimization_barrier(jnp.sum(g * g, axis=-1))) for g in (grad_in, grad_second, grad_first, grad_mixed)] + [jnp.sum(weight_rows)])
        updated = jax.tree.map(jnp.add, grads_acc, grad_params)
        return ((updated, stats_acc + sums), (result.astype(jnp.bfloat16), grad_in.astype(jnp.bfloat16)))
    start = (jax.tree.map(jnp.zeros_like, params), jnp.zeros((5,), jnp.float32))
    (grads, stats), (outputs, input_grads) = lax.scan(group_step, start, (regroup(inputs.astype(jnp.float32)), regroup(segments), regroup(valid), regroup(out_grad.astype(jnp.float32))))
    rms = jnp.sqrt(stats[:4] / (stats[4] * D))
    return (outputs.reshape(TOKENS, D), input_grads.reshape(TOKENS, D), grads[0], grads[1], grads[2], grads[3], grads[4], grads[5], grads[6], grads[7], grads[8], grads[9], grads[10], grads[11], grads[12], grads[13], grads[14], rms)
```

```python
from functools import partial

import jax
import jax.numpy as jnp
from jax import lax
from jax.sharding import PartitionSpec as P

D = 768
HEAD_DIM = 64
SEQ_LEN = 512
norm_eps = 1e-06
f32 = jnp.float32
bf16 = jnp.bfloat16


def left_contract(left, right):
    return lax.dot_general(
        left, right, (((0,), (0,)), ((), ())), preferred_element_type=f32
    )


def right_contract(left, right):
    return lax.dot_general(
        left, right, (((1,), (1,)), ((), ())), preferred_element_type=f32
    )


def layer_norm(values, gain, shift):
    centred = values - jnp.mean(values, axis=-1, keepdims=True)
    inverse = lax.rsqrt(jnp.mean(centred * centred, axis=-1, keepdims=True) + norm_eps)
    normed = centred * inverse
    return (normed * gain + shift, normed, inverse)


def norm_back(grad_rows, normed, inverse, gain):
    inner = grad_rows * gain
    centre_part = jnp.mean(inner, axis=-1, keepdims=True)
    slope_part = jnp.mean(inner * normed, axis=-1, keepdims=True)
    return inverse * (inner - centre_part - normed * slope_part)


def masked_scores(queries, key_rows, seg_row, valid_row, scale):
    scores = (
        jnp.einsum("qhd,khd->hqk", queries, key_rows, preferred_element_type=f32) * scale
    )
    allowed = (seg_row[:, None] == seg_row[None, :]) & (valid_row[None, :] == 1)
    return jnp.where(allowed[None], scores, -1e30)


def attend_forward(packed, scale):
    queries, key_rows, value_rows, seg_row, valid_row = packed
    scores = masked_scores(queries, key_rows, seg_row, valid_row, scale)
    peak = jnp.max(scores, axis=-1, keepdims=True)
    shifted = jnp.exp(scores - peak)
    totals = jnp.sum(shifted, axis=-1, keepdims=True)
    weights = (shifted / totals).astype(bf16)
    context = jnp.einsum("hqk,khd->qhd", weights, value_rows, preferred_element_type=f32)
    return (context.astype(bf16), peak + jnp.log(totals))


def attend_backward(packed, scale):
    queries, key_rows, value_rows, seg_row, valid_row, log_totals, grad_context = packed
    probs = jnp.exp(masked_scores(queries, key_rows, seg_row, valid_row, scale) - log_totals)
    grad_probs = jnp.einsum(
        "qhd,khd->hqk", grad_context, value_rows, preferred_element_type=f32
    )
    centred = grad_probs - jnp.sum(grad_probs * probs, axis=-1, keepdims=True)
    grad_scores = (probs * centred).astype(bf16)
    grad_queries = (
        jnp.einsum("hqk,khd->qhd", grad_scores, key_rows, preferred_element_type=f32) * scale
    )
    grad_keys = (
        jnp.einsum("hqk,qhd->khd", grad_scores, queries, preferred_element_type=f32) * scale
    )
    grad_values = jnp.einsum(
        "hqk,qhd->khd", probs.astype(bf16), grad_context, preferred_element_type=f32
    )
    return (grad_queries.astype(bf16), grad_keys.astype(bf16), grad_values.astype(bf16))


def swap_narrow(values):
    return lax.ppermute(values, "narrow", [(0, 1), (1, 0)])


def swap_wide(values, bit, size):
    return lax.ppermute(values, "wide", [(i, i ^ (1 << bit)) for i in range(size)])


def halve(values, orders, size):
    me = lax.axis_index("wide")
    states = list(values)
    for step in range(len(orders[0])):
        fresh = []
        for state, order in zip(states, orders):
            bit = order[step]
            half = state.shape[0] // 2
            mine = (me >> bit) & 1
            kept = lax.dynamic_slice_in_dim(state, mine * half, half, 0)
            sent = lax.dynamic_slice_in_dim(state, (1 - mine) * half, half, 0)
            got = swap_wide(sent, bit, size)
            fresh.append((kept.astype(f32) + got.astype(f32)).astype(bf16))
        states = fresh
    return states


def double(states, orders, size):
    me = lax.axis_index("wide")
    for step in reversed(range(len(orders[0]))):
        fresh = []
        for state, order in zip(states, orders):
            bit = order[step]
            mine = (me >> bit) & 1
            got = swap_wide(state, bit, size)
            fresh.append(
                jnp.where(
                    mine == 1,
                    jnp.concatenate([got, state], 0),
                    jnp.concatenate([state, got], 0),
                )
            )
        states = fresh
    return states


def sum_wide(values, size):
    bits = size.bit_length() - 1
    if size != 1 << bits or values.shape[0] % (6 * size):
        return lax.psum(values, "wide").astype(f32)
    first = list(range(bits))
    orders = [first]
    if bits >= 3:
        rest = list(range(3, bits))
        orders = [[0, 1, 2] + rest, [1, 2, 0] + rest, [2, 0, 1] + rest]
        sixth = values.shape[0] // 6
        parts = [values[: 3 * sixth], values[3 * sixth : 5 * sixth], values[5 * sixth :]]
    else:
        parts = [values]
    parts = double(halve(parts, orders, size), orders, size)
    return jnp.concatenate(parts, 0).astype(f32)


def sum_small(values, size):
    values = values + swap_narrow(values)
    bits = size.bit_length() - 1
    if size != 1 << bits:
        return lax.psum(values, "wide")
    for bit in range(bits):
        values = values + swap_wide(values, bit, size)
    return values


def body(size, *arrays):
    (
        inputs, segments, valid, w_query, w_key, w_value, b_query, b_value, w_attn_out, b_attn_out,
        gain_one, shift_one, w_ffn_in, b_ffn_in, w_ffn_out, b_ffn_out, gain_two, shift_two, out_grad,
    ) = arrays
    side = lax.axis_index("narrow")
    rows = inputs.shape[0] // 2
    head_width = w_query.shape[1]

    def mine(array):
        return lax.dynamic_slice_in_dim(array, side * rows, rows, 0)

    def both(array, axis):
        return jnp.concatenate([array, swap_narrow(array)], axis)

    def join_rows(array):
        other = swap_narrow(array)
        return jnp.where(
            side == 0,
            jnp.concatenate([array, other], 0),
            jnp.concatenate([other, array], 0),
        )

    hidden_in, seg_rows, valid_rows, cotangent = (mine(a) for a in (inputs, segments, valid, out_grad))
    w_query, w_key, w_value = (both(w, 1) for w in (w_query, w_key, w_value))
    b_query, b_value = both(b_query, 0), both(b_value, 0)
    w_attn_out = both(w_attn_out, 0)
    w_ffn_in, b_ffn_in, w_ffn_out = both(w_ffn_in, 1), both(b_ffn_in, 0), both(w_ffn_out, 0)

    seq_count = rows // SEQ_LEN
    heads = 2 * head_width // HEAD_DIM
    scale = HEAD_DIM ** (-0.5)

    def split_heads(array):
        return array.reshape(seq_count, SEQ_LEN, heads, HEAD_DIM)

    queries = (jnp.dot(hidden_in, w_query, preferred_element_type=f32) + b_query.astype(f32)).astype(bf16)
    key_rows = jnp.dot(hidden_in, w_key, preferred_element_type=f32).astype(bf16)
    value_rows = (jnp.dot(hidden_in, w_value, preferred_element_type=f32) + b_value.astype(f32)).astype(bf16)
    head_inputs = (
        split_heads(queries),
        split_heads(key_rows),
        split_heads(value_rows),
        seg_rows.reshape(seq_count, SEQ_LEN),
        valid_rows.reshape(seq_count, SEQ_LEN),
    )
    context, log_totals = lax.map(partial(attend_forward, scale=scale), head_inputs)
    context = context.reshape(rows, 2 * head_width)
    attn = jnp.dot(context, w_attn_out, preferred_element_type=f32) + b_attn_out.astype(f32)
    mixed = hidden_in.astype(f32) + attn
    first, normed_one, inverse_one = layer_norm(mixed, gain_one.astype(f32), shift_one.astype(f32))
    first_low = first.astype(bf16)
    pre_act = jnp.dot(first_low, w_ffn_in, preferred_element_type=f32) + b_ffn_in.astype(f32)
    activated = jax.nn.gelu(pre_act, approximate=False).astype(bf16)
    ffn_out = jnp.dot(activated, w_ffn_out, preferred_element_type=f32) + b_ffn_out.astype(f32)
    second = first + ffn_out
    final, normed_two, inverse_two = layer_norm(second, gain_two.astype(f32), shift_two.astype(f32))
    output = join_rows(final.astype(bf16))
    valid_float = valid_rows.astype(f32)
    grad_out = cotangent.astype(f32) * valid_float[:, None]
    d_gain_two = jnp.sum(grad_out * normed_two, axis=0)
    d_shift_two = jnp.sum(grad_out, axis=0)
    grad_second = norm_back(grad_out, normed_two, inverse_two, gain_two.astype(f32))
    d_b_ffn_out = jnp.sum(grad_second, axis=0)
    low_second = grad_second.astype(bf16)

    def reduce_rows(left, right):
        half = left.shape[1] // 2
        sent = left_contract(left[:, half:], right).astype(bf16)
        kept = left_contract(left[:, :half], right)
        return sum_wide((kept + swap_narrow(sent).astype(f32)).astype(bf16), size)

    def reduce_columns(left, kept_right, sent_right):
        sent = left_contract(left, sent_right).astype(bf16)
        kept = left_contract(left, kept_right)
        return sum_wide((kept + swap_narrow(sent).astype(f32)).astype(bf16), size)

    d_w_ffn_out = reduce_rows(activated, low_second)
    grad_act = right_contract(low_second, w_ffn_out)
    unused_value, gelu_back = jax.vjp(partial(jax.nn.gelu, approximate=False), pre_act)
    grad_pre = gelu_back(grad_act)[0].astype(bf16)
    d_b_ffn_in = jnp.sum(grad_pre.astype(f32), axis=0)
    half = grad_pre.shape[1] // 2
    d_w_ffn_in = reduce_columns(first_low, grad_pre[:, :half], grad_pre[:, half:])
    grad_first = grad_second + right_contract(grad_pre, w_ffn_in)
    d_gain_one = jnp.sum(grad_first * normed_one, axis=0)
    d_shift_one = jnp.sum(grad_first, axis=0)
    grad_mixed = norm_back(grad_first, normed_one, inverse_one, gain_one.astype(f32))
    d_b_attn_out = jnp.sum(grad_mixed, axis=0)
    low_mixed = grad_mixed.astype(bf16)
    d_w_attn_out = reduce_rows(context, low_mixed)
    grad_context = right_contract(low_mixed, w_attn_out).astype(bf16)
    back_inputs = head_inputs + (log_totals, split_heads(grad_context))
    grads = lax.map(partial(attend_backward, scale=scale), back_inputs)
    grad_queries, grad_keys, grad_values = (g.reshape(rows, 2 * head_width) for g in grads)
    d_b_query = jnp.sum(grad_queries.astype(f32), axis=0)
    d_b_value = jnp.sum(grad_values.astype(f32), axis=0)
    three = (grad_queries, grad_keys, grad_values)
    d_w_three = reduce_columns(
        hidden_in,
        jnp.concatenate([g[:, :head_width] for g in three], 1),
        jnp.concatenate([g[:, head_width:] for g in three], 1),
    )
    grad_in = (
        grad_mixed
        + right_contract(grad_queries, w_query)
        + right_contract(grad_keys, w_key)
        + right_contract(grad_values, w_value)
    )
    input_grad = join_rows(grad_in.astype(bf16))
    stats = jnp.stack(
        [
            jnp.sum(valid_float * jnp.sum(g * g, axis=-1))
            for g in (grad_in, grad_second, grad_first, grad_mixed)
        ]
        + [jnp.sum(valid_float)]
    )

    def by_side(array):
        half = array.shape[0] // 2
        return jnp.where(side == 0, array, jnp.roll(array, half))

    small = sum_small(
        jnp.concatenate(
            [by_side(d_b_query), by_side(d_b_value), by_side(d_b_ffn_in)]
            + [d_b_attn_out, d_gain_one, d_shift_one, d_b_ffn_out, d_gain_two, d_shift_two]
            + [jnp.pad(stats, (0, 128 - 5))]
        ),
        size,
    )
    ends = []
    at = 0
    for length in (2 * head_width, 2 * head_width, b_ffn_in.shape[0]) + (D,) * 6 + (128,):
        ends.append(small[at : at + length])
        at += length

    def own(array):
        half = array.shape[0] // 2
        return lax.dynamic_slice_in_dim(array, side * half, half, 0)

    rms = jnp.sqrt(ends[9][:4] / (ends[9][4] * D))
    return (
        output,
        input_grad,
        d_w_three[:, :head_width],
        d_w_three[:, head_width : 2 * head_width],
        d_w_three[:, 2 * head_width :],
        own(ends[0]),
        own(ends[1]),
        d_w_attn_out,
        ends[3],
        ends[4],
        ends[5],
        d_w_ffn_in,
        own(ends[2]),
        d_w_ffn_out,
        ends[6],
        ends[7],
        ends[8],
        rms,
    )


def solution(mesh):
    row, col = P("narrow", None), P(None, "narrow")
    one, rows = P("narrow"), P("wide", None)
    in_specs = (
        rows, P("wide"), P("wide"), col, col, col, one, one, row, P(), P(), P(), col, one, row, P(), P(), P(), rows,
    )
    out_specs = (
        rows, rows, col, col, col, one, one, row, P(), P(), P(), col, one, row, P(), P(), P(), P(),
    )
    return jax.shard_map(
        partial(body, mesh.shape["wide"]), mesh=mesh, in_specs=in_specs, out_specs=out_specs, check_vma=False
    )
```

```python
from functools import partial

import jax
import jax.numpy as jnp
from jax import lax
from jax.experimental import pallas as pl
from jax.experimental.pallas import tpu as pltpu
from jax.sharding import PartitionSpec as P

D = 768
HEAD_DIM = 64
SEQ_LEN = 512
PAIR = 2 * HEAD_DIM
norm_eps = 1e-06
f32 = jnp.float32
bf16 = jnp.bfloat16
VMEM_BYTES = 58 << 20


def dot(left, right, left_dim=1, right_dim=0):
    return lax.dot_general(
        left, right, (((left_dim,), (right_dim,)), ((), ())), preferred_element_type=f32
    )


def normalise(values):
    centred = values - jnp.mean(values, axis=-1, keepdims=True)
    inverse = lax.rsqrt(jnp.mean(centred * centred, axis=-1, keepdims=True) + norm_eps)
    return centred * inverse, inverse


def norm_back(grad_rows, normed, inverse, gain):
    inner = grad_rows * gain
    centre_part = jnp.mean(inner, axis=-1, keepdims=True)
    slope_part = jnp.mean(inner * normed, axis=-1, keepdims=True)
    return inverse * (inner - centre_part - normed * slope_part)


def as_column(row):
    return jnp.broadcast_to(row, (8, row.shape[1])).T[:, :1]


def add_rows(ref, rows):
    @pl.when(pl.program_id(0) == 0)
    def _():
        ref[...] = jnp.zeros_like(ref)

    for at, values in enumerate(rows):
        ref[at : at + 1, :] += jnp.sum(values, axis=0, keepdims=True)


def gelu_both(pre):
    size = jnp.abs(pre)
    t = 1.0 / (1.0 + size * (0.3275911 * 0.7071067811865476))
    bell = jnp.exp(pre * pre * -0.5)
    tail = t * (
        0.5 * 0.254829592
        + t * (0.5 * -0.284496736 + t * (0.5 * 1.421413741 + t * (0.5 * -1.453152027 + t * (0.5 * 1.061405429))))
    )
    tail = tail * bell
    below = jnp.where(pre >= 0, 1.0 - tail, tail)
    return pre * below, below + pre * bell * 0.3989422804014327


def attend_kernel(
    side, x_ref, seg_ref, valid_ref, wq_a, wq_b, wk_a, wk_b, wv_a, wv_b, bq_ref, bv_ref, wo_a, wo_b, bo_ref,
    q_ref, k_ref, v_ref, p_ref, ctx_ref, mixed_ref, bias_ref,
):
    x = x_ref[...]
    seg = seg_ref[0].astype(f32)
    allowed = (as_column(seg) == seg) & (valid_ref[0] == 1)
    bias_ref[...] = jnp.where(allowed, 0.0, -1e30)
    width = wq_a.shape[1]
    for at, (wq, wk, wv) in enumerate(((wq_a, wk_a, wv_a), (wq_b, wk_b, wv_b))):
        here = slice(at * width, (at + 1) * width)
        q_ref[:, here] = (dot(x, wq[...]) + bq_ref[:, here].astype(f32)).astype(bf16) * jnp.asarray(HEAD_DIM ** -0.5, bf16)
        k_ref[:, here] = dot(x, wk[...]).astype(bf16)
        v_ref[:, here] = (dot(x, wv[...]) + bv_ref[:, here].astype(f32)).astype(bf16)

    lane = lax.broadcasted_iota(jnp.int32, (1, PAIR), 1)

    def pair_step(pair, carry):
        here = pl.ds(pl.multiple_of(pair * PAIR, PAIR), PAIR)
        q, k, v = q_ref[:, here], k_ref[:, here], v_ref[:, here]
        parts = []
        for head in range(2):
            scores = dot(jnp.where(lane // HEAD_DIM == head, q, 0), k, 1, 1) + bias_ref[...]
            shifted = jnp.exp(scores - jnp.max(scores, axis=-1, keepdims=True))
            probs = (shifted * (1.0 / jnp.sum(shifted, axis=-1, keepdims=True))).astype(bf16)
            p_ref[0, 2 * pair + head] = probs
            parts.append(dot(probs, v))
        ctx_ref[:, here] = jnp.where(lane < HEAD_DIM, parts[0], parts[1]).astype(bf16)
        return carry

    lax.fori_loop(0, 2 * width // PAIR, pair_step, 0)
    attn = dot(ctx_ref[:, :width], wo_a[...]) + dot(ctx_ref[:, width:], wo_b[...])
    mixed_ref[...] = x.astype(f32) + attn + bo_ref[...].astype(f32)


def ffn_kernel(
    side, mixed_ref, valid_ref, cot_ref, w1_a, w1_b, b1_ref, w2_a, w2_b, b2_ref, g1_ref, s1_ref, g2_ref, s2_ref,
    low_first_ref, act_ref, slope_ref, out_ref, grad_ref, low_ref, vec_ref,
):
    normed_one, _ = normalise(mixed_ref[...])
    first = normed_one * g1_ref[...].astype(f32) + s1_ref[...].astype(f32)
    low_first = first.astype(bf16)
    low_first_ref[...] = low_first
    second = first + b2_ref[...].astype(f32)
    width = w1_a.shape[1]
    step = 512
    for half, (w1, w2) in enumerate(((w1_a, w2_a), (w1_b, w2_b))):
        for at in range(0, width, step):
            here = slice(half * width + at, half * width + at + step)
            pre = dot(low_first, w1[:, at : at + step]) + b1_ref[:, here].astype(f32)
            act, slope = gelu_both(pre)
            act = act.astype(bf16)
            act_ref[:, here] = act
            slope_ref[:, here] = slope.astype(bf16)
            second += dot(act, w2[at : at + step, :])
    normed_two, inverse_two = normalise(second)
    gain = g2_ref[...].astype(f32)
    out_ref[...] = (normed_two * gain + s2_ref[...].astype(f32)).astype(bf16)
    valid = as_column(valid_ref[0].astype(f32))
    grad_out = cot_ref[...].astype(f32) * valid
    grad = norm_back(grad_out, normed_two, inverse_two, gain)
    grad_ref[...] = grad
    low_ref[...] = grad.astype(bf16)
    add_rows(vec_ref, (grad_out * normed_two, grad_out, grad, grad * grad * valid))


def ffn_back_kernel(
    side, low_ref, grad_ref, slope_ref, mixed_ref, valid_ref, w1_a, w1_b, w2_a, w2_b, wo_a, wo_b, g1_ref,
    pre_ref, mixed_grad_ref, low_mixed_ref, ctx_grad_ref, vec_ref, hidden_ref,
):
    low = low_ref[...]
    grad_first = grad_ref[...]
    width = w1_a.shape[1]
    step = 512

    @pl.when(pl.program_id(0) == 0)
    def _():
        hidden_ref[...] = jnp.zeros_like(hidden_ref)

    for half, (w1, w2) in enumerate(((w1_a, w2_a), (w1_b, w2_b))):
        for at in range(0, width, step):
            here = slice(half * width + at, half * width + at + step)
            grad_pre = (dot(low, w2[at : at + step, :], 1, 1) * slope_ref[:, here].astype(f32)).astype(bf16)
            pre_ref[:, here] = grad_pre
            hidden_ref[:, here] += jnp.sum(grad_pre.astype(f32), axis=0, keepdims=True)
            grad_first += dot(grad_pre, w1[:, at : at + step], 1, 1)
    normed_one, inverse_one = normalise(mixed_ref[...])
    grad_mixed = norm_back(grad_first, normed_one, inverse_one, g1_ref[...].astype(f32))
    mixed_grad_ref[...] = grad_mixed
    low_mixed = grad_mixed.astype(bf16)
    low_mixed_ref[...] = low_mixed
    head_width = wo_a.shape[0]
    ctx_grad_ref[:, :head_width] = dot(low_mixed, wo_a[...], 1, 1).astype(bf16)
    ctx_grad_ref[:, head_width:] = dot(low_mixed, wo_b[...], 1, 1).astype(bf16)
    valid = as_column(valid_ref[0].astype(f32))
    add_rows(
        vec_ref,
        (grad_first * normed_one, grad_first, grad_mixed, grad_first * grad_first * valid, grad_mixed * grad_mixed * valid),
    )


def attend_back_kernel(
    side, q_ref, k_ref, v_ref, p_ref, ctx_ref, ctx_grad_ref, mixed_grad_ref, valid_ref, wq_a, wq_b, wk_a, wk_b, wv_a, wv_b,
    dq_ref, dk_ref, dv_ref, in_grad_ref, vec_ref,
):
    lane = lax.broadcasted_iota(jnp.int32, (1, PAIR), 1)
    width = wq_a.shape[1]

    def pair_step(pair, carry):
        here = pl.ds(pl.multiple_of(pair * PAIR, PAIR), PAIR)
        q, k, v = q_ref[:, here], k_ref[:, here], v_ref[:, here]
        ctx, ctx_grad = ctx_ref[:, here].astype(f32), ctx_grad_ref[:, here]
        dq, dk, dv = [], 0.0, 0.0
        for head in range(2):
            ours = lane // HEAD_DIM == head
            masked = jnp.where(ours, ctx_grad, 0)
            inner = jnp.sum(masked.astype(f32) * ctx, axis=-1, keepdims=True)
            probs = p_ref[0, 2 * pair + head]
            grad_scores = (probs.astype(f32) * (dot(masked, v, 1, 1) - inner)).astype(bf16)
            dq.append(dot(grad_scores, k))
            dk += dot(jnp.where(ours, q, 0), grad_scores, 0, 0)
            dv += dot(masked, probs, 0, 0)
        dq_ref[:, here] = (jnp.where(lane < HEAD_DIM, dq[0], dq[1]) * HEAD_DIM ** -0.5).astype(bf16)
        dk_ref[:, here] = dk.T.astype(bf16)
        dv_ref[:, here] = dv.T.astype(bf16)
        return carry

    lax.fori_loop(0, 2 * width // PAIR, pair_step, 0)
    grad_in = mixed_grad_ref[...]
    for at, weights in enumerate(((wq_a, wk_a, wv_a), (wq_b, wk_b, wv_b))):
        here = slice(at * width, (at + 1) * width)
        for rows, weight in zip((dq_ref, dk_ref, dv_ref), weights):
            grad_in += dot(rows[:, here], weight[...], 1, 1)
    in_grad_ref[...] = grad_in.astype(bf16)
    valid = as_column(valid_ref[0].astype(f32))
    add_rows(vec_ref, (dq_ref[...].astype(f32), dv_ref[...].astype(f32), grad_in * grad_in * valid))


def run_kernel(kernel, grid, side, operands, outs, scratch=(), cost=(0, 0)):
    def spec(block, kind):
        rest = (0,) * (len(block) - 1)
        if kind == "all":
            return pl.BlockSpec(block, lambda i, s: (0,) + rest, pipeline_mode=pl.Buffered(1))
        if kind == "sum":
            return pl.BlockSpec(block, lambda i, s: (0,) + rest)
        if kind == "shared":
            return pl.BlockSpec(block, lambda i, s: (s[0] * grid + i,) + rest)
        return pl.BlockSpec(block, lambda i, s: (i,) + rest)

    return pl.pallas_call(
        kernel,
        grid_spec=pltpu.PrefetchScalarGridSpec(
            num_scalar_prefetch=1,
            grid=(grid,),
            in_specs=[spec(block, kind) for _, block, kind in operands],
            out_specs=[spec(block, kind) for _, block, kind in outs],
            scratch_shapes=list(scratch),
        ),
        out_shape=[shape for shape, _, _ in outs],
        compiler_params=pltpu.CompilerParams(vmem_limit_bytes=VMEM_BYTES),
        cost_estimate=pl.CostEstimate(flops=int(cost[0]), bytes_accessed=int(cost[1]), transcendentals=0),
    )(side, *[array for array, _, _ in operands])


def like(shape, dtype):
    return jax.ShapeDtypeStruct(shape, dtype)


def whole(array):
    return (array, array.shape, "all")


def swap_narrow(values):
    return lax.ppermute(values, "narrow", [(0, 1), (1, 0)])


def swap_wide(values, bit, size):
    return lax.ppermute(values, "wide", [(i, i ^ (1 << bit)) for i in range(size)])


def halve(values, orders, size):
    me = lax.axis_index("wide")
    states = list(values)
    for step in range(len(orders[0])):
        fresh = []
        for state, order in zip(states, orders):
            bit = order[step]
            half = state.shape[0] // 2
            mine = (me >> bit) & 1
            kept = lax.dynamic_slice_in_dim(state, mine * half, half, 0)
            sent = lax.dynamic_slice_in_dim(state, (1 - mine) * half, half, 0)
            got = swap_wide(sent, bit, size)
            fresh.append((kept.astype(f32) + got.astype(f32)).astype(bf16))
        states = fresh
    return states


def double(states, orders, size):
    me = lax.axis_index("wide")
    for step in reversed(range(len(orders[0]))):
        fresh = []
        for state, order in zip(states, orders):
            bit = order[step]
            mine = (me >> bit) & 1
            got = swap_wide(state, bit, size)
            fresh.append(
                jnp.where(
                    mine == 1,
                    jnp.concatenate([got, state], 0),
                    jnp.concatenate([state, got], 0),
                )
            )
        states = fresh
    return states


def sum_wide(values, size):
    bits = size.bit_length() - 1
    if size != 1 << bits or values.shape[0] % (6 * size):
        return lax.psum(values, "wide").astype(f32)
    first = list(range(bits))
    orders = [first]
    if bits >= 3:
        rest = list(range(3, bits))
        orders = [[0, 1, 2] + rest, [1, 2, 0] + rest, [2, 0, 1] + rest]
        sixth = values.shape[0] // 6
        parts = [values[: 3 * sixth], values[3 * sixth : 5 * sixth], values[5 * sixth :]]
    else:
        parts = [values]
    parts = double(halve(parts, orders, size), orders, size)
    return jnp.concatenate(parts, 0).astype(f32)


def sum_small(values, size):
    bits = size.bit_length() - 1
    if size != 1 << bits:
        return lax.psum(values, "wide")
    for bit in range(bits):
        values = values + swap_wide(values, bit, size)
    return values


def body(size, *arrays):
    (
        inputs, segments, valid, w_query, w_key, w_value, b_query, b_value, w_attn_out, b_attn_out,
        gain_one, shift_one, w_ffn_in, b_ffn_in, w_ffn_out, b_ffn_out, gain_two, shift_two, out_grad,
    ) = arrays
    side = lax.axis_index("narrow")
    rows = inputs.shape[0] // 2
    seqs = rows // SEQ_LEN
    head_width = w_query.shape[1]
    hidden = w_ffn_in.shape[1]
    heads = 2 * head_width // HEAD_DIM
    side_ref = side.astype(jnp.int32).reshape(1)
    row_block = 256
    blocks = rows // row_block

    def pair_of(array):
        return (array, swap_narrow(array))

    def join_rows(array):
        other = swap_narrow(array)
        return jnp.where(
            side == 0,
            jnp.concatenate([array, other], 0),
            jnp.concatenate([other, array], 0),
        )

    def line(array):
        return array.reshape(1, -1)

    wq, wk, wv = pair_of(w_query), pair_of(w_key), pair_of(w_value)
    small_own = jnp.concatenate([b_query, b_value, b_ffn_in])
    small_other = swap_narrow(small_own)
    bq = jnp.concatenate([b_query, small_other[:head_width]])
    bv = jnp.concatenate([b_value, small_other[head_width : 2 * head_width]])
    b1 = jnp.concatenate([b_ffn_in, small_other[2 * head_width :]])
    wo, w1, w2 = pair_of(w_attn_out), pair_of(w_ffn_in), pair_of(w_ffn_out)
    seg_rows = segments.reshape(-1, 1, SEQ_LEN)
    valid_seq = valid.reshape(-1, 1, SEQ_LEN)
    valid_block = valid.reshape(-1, 1, row_block)
    seq = (SEQ_LEN, D)
    blk = (row_block, D)
    wide_blk = (row_block, 2 * hidden)
    low_rows = like((rows, D), bf16)
    full_rows = like((rows, D), f32)

    queries, keys, values, probs, context, mixed = run_kernel(
        attend_kernel,
        seqs,
        side_ref,
        [(inputs, seq, "shared"), (seg_rows, (1, 1, SEQ_LEN), "shared"), (valid_seq, (1, 1, SEQ_LEN), "shared")]
        + [whole(w) for w in wq + wk + wv]
        + [whole(line(bq)), whole(line(bv))]
        + [whole(w) for w in wo]
        + [whole(line(b_attn_out))],
        [(low_rows, seq, "own")] * 3
        + [(like((seqs, heads, SEQ_LEN, SEQ_LEN), bf16), (1, heads, SEQ_LEN, SEQ_LEN), "own")]
        + [(low_rows, seq, "own"), (full_rows, seq, "own")],
        [pltpu.VMEM((SEQ_LEN, SEQ_LEN), f32)],
        (rows * D * D * 8 + rows * SEQ_LEN * D * 4, rows * D * 16),
    )
    low_first, activated, slope, final, grad_second, low_second, vec_two = run_kernel(
        ffn_kernel,
        blocks,
        side_ref,
        [(mixed, blk, "own"), (valid_block, (1, 1, row_block), "shared"), (out_grad, blk, "shared")]
        + [whole(w) for w in w1]
        + [whole(line(b1))]
        + [whole(w) for w in w2]
        + [whole(line(v)) for v in (b_ffn_out, gain_one, shift_one, gain_two, shift_two)],
        [
            (low_rows, blk, "own"),
            (like((rows, 2 * hidden), bf16), wide_blk, "own"),
            (like((rows, 2 * hidden), bf16), wide_blk, "own"),
            (low_rows, blk, "own"),
            (full_rows, blk, "own"),
            (low_rows, blk, "own"),
            (like((8, D), f32), (8, D), "sum"),
        ],
        (),
        (rows * D * hidden * 8, rows * D * 30),
    )
    output = join_rows(final)

    def shared_sum(sent, kept):
        return sum_wide((kept + swap_narrow(sent.astype(bf16)).astype(f32)).astype(bf16), size)

    d_w_ffn_out = shared_sum(
        dot(activated[:, hidden:], low_second, 0, 0), dot(activated[:, :hidden], low_second, 0, 0)
    )
    grad_pre, grad_mixed, low_mixed, grad_context, vec_one, vec_hidden = run_kernel(
        ffn_back_kernel,
        blocks,
        side_ref,
        [
            (low_second, blk, "own"),
            (grad_second, blk, "own"),
            (slope, wide_blk, "own"),
            (mixed, blk, "own"),
            (valid_block, (1, 1, row_block), "shared"),
        ]
        + [whole(w) for w in w1 + w2 + wo]
        + [whole(line(gain_one))],
        [
            (like((rows, 2 * hidden), bf16), wide_blk, "own"),
            (full_rows, blk, "own"),
            (low_rows, blk, "own"),
            (low_rows, blk, "own"),
            (like((8, D), f32), (8, D), "sum"),
            (like((1, 2 * hidden), f32), (1, 2 * hidden), "sum"),
        ],
        (),
        (rows * D * hidden * 8, rows * D * 30),
    )
    d_w_ffn_in = shared_sum(
        dot(low_first, grad_pre[:, hidden:], 0, 0), dot(low_first, grad_pre[:, :hidden], 0, 0)
    )
    d_w_attn_out = shared_sum(
        dot(context[:, head_width:], low_mixed, 0, 0), dot(context[:, :head_width], low_mixed, 0, 0)
    )
    grad_queries, grad_keys, grad_values, grad_in, vec_in = run_kernel(
        attend_back_kernel,
        seqs,
        side_ref,
        [(a, seq, "own") for a in (queries, keys, values)]
        + [(probs, (1, heads, SEQ_LEN, SEQ_LEN), "own")]
        + [(a, seq, "own") for a in (context, grad_context, grad_mixed)]
        + [(valid_seq, (1, 1, SEQ_LEN), "shared")]
        + [whole(w) for w in wq + wk + wv],
        [(low_rows, seq, "own")] * 4 + [(like((8, D), f32), (8, D), "sum")],
        (),
        (rows * D * D * 6 + rows * SEQ_LEN * D * 8, rows * D * 30),
    )
    input_grad = join_rows(grad_in)
    own_rows = lax.dynamic_slice_in_dim(inputs, side * rows, rows, 0)
    three = (grad_queries, grad_keys, grad_values)
    d_w_three = shared_sum(
        dot(own_rows, jnp.concatenate([g[:, head_width:] for g in three], 1), 0, 0),
        dot(own_rows, jnp.concatenate([g[:, :head_width] for g in three], 1), 0, 0),
    )

    count = jnp.sum(lax.dynamic_slice_in_dim(valid, side * rows, rows, 0).astype(f32))
    halves = jnp.concatenate(
        [vec_in[0, :head_width], vec_in[1, :head_width], vec_hidden[0, :hidden]]
        + [vec_in[0, head_width:], vec_in[1, head_width:], vec_hidden[0, hidden:]]
    )
    stats = jnp.stack([jnp.sum(v) for v in (vec_in[2], vec_two[3], vec_one[3], vec_one[4])] + [count])
    rest = jnp.concatenate(
        [vec_one[2], vec_one[0], vec_one[1], vec_two[2], vec_two[0], vec_two[1], jnp.pad(stats, (0, 128 - 5))]
    )
    split = halves.shape[0] // 2
    moved = swap_narrow(jnp.concatenate([halves[split:], rest]))
    small = jnp.concatenate([halves[:split], rest]) + moved
    small = sum_small(small, size)
    ends = []
    at = 0
    for length in (head_width, head_width, hidden) + (D,) * 6 + (128,):
        ends.append(small[at : at + length])
        at += length
    rms = jnp.sqrt(ends[9][:4] / (ends[9][4] * D))
    return (
        output,
        input_grad,
        d_w_three[:, :head_width],
        d_w_three[:, head_width : 2 * head_width],
        d_w_three[:, 2 * head_width :],
        ends[0],
        ends[1],
        d_w_attn_out,
        ends[3],
        ends[4],
        ends[5],
        d_w_ffn_in,
        ends[2],
        d_w_ffn_out,
        ends[6],
        ends[7],
        ends[8],
        rms,
    )


def solution(mesh):
    row, col = P("narrow", None), P(None, "narrow")
    one, rows = P("narrow"), P("wide", None)
    in_specs = (
        rows, P("wide"), P("wide"), col, col, col, one, one, row, P(), P(), P(), col, one, row, P(), P(), P(), rows,
    )
    out_specs = (
        rows, rows, col, col, col, one, one, row, P(), P(), P(), col, one, row, P(), P(), P(), P(),
    )
    return jax.shard_map(
        partial(body, mesh.shape["wide"]), mesh=mesh, in_specs=in_specs, out_specs=out_specs, check_vma=False
    )
```

```python
from functools import partial

import jax
import jax.numpy as jnp
from jax import lax
from jax.experimental import pallas as pl
from jax.experimental.pallas import tpu as pltpu
from jax.sharding import PartitionSpec as P

D = 768
HEAD_DIM = 64
SEQ_LEN = 512
PAIR = 2 * HEAD_DIM
norm_eps = 1e-06
f32 = jnp.float32
bf16 = jnp.bfloat16
VMEM_BYTES = 58 << 20
B_OUT, B_FFN, GAIN_ONE, SHIFT_ONE, GAIN_TWO, SHIFT_TWO = (slice(row, row + 1) for row in range(6, 12))


def dot(left, right, left_dim=1, right_dim=0):
    return lax.dot_general(
        left, right, (((left_dim,), (right_dim,)), ((), ())), preferred_element_type=f32
    )


def normalise(values):
    centred = values - jnp.mean(values, axis=-1, keepdims=True)
    inverse = lax.rsqrt(jnp.mean(centred * centred, axis=-1, keepdims=True) + norm_eps)
    return centred * inverse, inverse


def norm_back(grad_rows, normed, inverse, gain):
    inner = grad_rows * gain
    centre_part = jnp.mean(inner, axis=-1, keepdims=True)
    slope_part = jnp.mean(inner * normed, axis=-1, keepdims=True)
    return inverse * (inner - centre_part - normed * slope_part)


def as_column(row):
    return jnp.broadcast_to(row, (8, row.shape[1])).T[:, :1]


def add_rows(ref, rows):
    @pl.when(pl.program_id(0) == 0)
    def _():
        ref[...] = jnp.zeros_like(ref)

    for at, values in enumerate(rows):
        ref[at : at + 1, :] += jnp.sum(values, axis=0, keepdims=True)


def hidden_bias(weights_ref, half, at, step):
    pieces = []
    while step:
        row, lane = divmod(at, D)
        take = min(step, D - lane)
        pieces.append(weights_ref[3 * half + 1 + row : 3 * half + 2 + row, lane : lane + take])
        at, step = at + take, step - take
    return pieces[0] if len(pieces) == 1 else jnp.concatenate(pieces, 1)


def gelu_both(pre):
    size = jnp.abs(pre)
    t = 1.0 / (1.0 + size * (0.3275911 * 0.7071067811865476))
    bell = jnp.exp(pre * pre * -0.5)
    tail = t * (
        0.5 * 0.254829592
        + t * (0.5 * -0.284496736 + t * (0.5 * 1.421413741 + t * (0.5 * -1.453152027 + t * (0.5 * 1.061405429))))
    )
    tail = tail * bell
    below = jnp.where(pre >= 0, 1.0 - tail, tail)
    return pre * below, below + pre * bell * 0.3989422804014327


def attend_kernel(
    side, x_ref, seg_ref, valid_ref, wq_a, wq_b, wk_a, wk_b, wv_a, wv_b, wo_a, wo_b, vec_ref,
    q_ref, k_ref, v_ref, p_ref, ctx_ref, mixed_ref, bias_ref,
):
    x = x_ref[...]
    seg = seg_ref[0].astype(f32)
    allowed = (as_column(seg) == seg) & (valid_ref[0] == 1)
    bias_ref[...] = jnp.where(allowed, 0.0, -1e30)
    width = wq_a.shape[1]
    for at, (wq, wk, wv) in enumerate(((wq_a, wk_a, wv_a), (wq_b, wk_b, wv_b))):
        here = slice(at * width, (at + 1) * width)
        q_ref[:, here] = (dot(x, wq[...]) + vec_ref[3 * at : 3 * at + 1, :width]).astype(bf16) * jnp.asarray(HEAD_DIM ** -0.5, bf16)
        k_ref[:, here] = dot(x, wk[...]).astype(bf16)
        v_ref[:, here] = (dot(x, wv[...]) + vec_ref[3 * at : 3 * at + 1, width:]).astype(bf16)

    lane = lax.broadcasted_iota(jnp.int32, (1, PAIR), 1)

    def pair_step(pair, carry):
        here = pl.ds(pl.multiple_of(pair * PAIR, PAIR), PAIR)
        q, k, v = q_ref[:, here], k_ref[:, here], v_ref[:, here]
        parts = []
        for head in range(2):
            scores = dot(jnp.where(lane // HEAD_DIM == head, q, 0), k, 1, 1) + bias_ref[...]
            shifted = jnp.exp(scores - jnp.max(scores, axis=-1, keepdims=True))
            probs = (shifted * (1.0 / jnp.sum(shifted, axis=-1, keepdims=True))).astype(bf16)
            p_ref[0, 2 * pair + head] = probs
            parts.append(dot(probs, v))
        ctx_ref[:, here] = jnp.where(lane < HEAD_DIM, parts[0], parts[1]).astype(bf16)
        return carry

    lax.fori_loop(0, 2 * width // PAIR, pair_step, 0)
    attn = dot(ctx_ref[:, :width], wo_a[...]) + dot(ctx_ref[:, width:], wo_b[...])
    mixed_ref[...] = x.astype(f32) + attn + vec_ref[B_OUT]


def ffn_kernel(
    side, mixed_ref, valid_ref, cot_ref, w1_a, w1_b, w2_a, w2_b, weights_ref,
    low_first_ref, act_ref, slope_ref, out_ref, grad_ref, low_ref, vec_ref,
):
    normed_one, _ = normalise(mixed_ref[...])
    first = normed_one * weights_ref[GAIN_ONE] + weights_ref[SHIFT_ONE]
    low_first = first.astype(bf16)
    low_first_ref[...] = low_first
    second = first + weights_ref[B_FFN]
    width = w1_a.shape[1]
    step = 512
    for half, (w1, w2) in enumerate(((w1_a, w2_a), (w1_b, w2_b))):
        for at in range(0, width, step):
            here = slice(half * width + at, half * width + at + step)
            pre = dot(low_first, w1[:, at : at + step]) + hidden_bias(weights_ref, half, at, step)
            act, slope = gelu_both(pre)
            act = act.astype(bf16)
            act_ref[:, here] = act
            slope_ref[:, here] = slope.astype(bf16)
            second += dot(act, w2[at : at + step, :])
    normed_two, inverse_two = normalise(second)
    gain = weights_ref[GAIN_TWO]
    out_ref[...] = (normed_two * gain + weights_ref[SHIFT_TWO]).astype(bf16)
    valid = as_column(valid_ref[0].astype(f32))
    grad_out = cot_ref[...].astype(f32) * valid
    grad = norm_back(grad_out, normed_two, inverse_two, gain)
    grad_ref[...] = grad
    low_ref[...] = grad.astype(bf16)
    add_rows(vec_ref, (grad_out * normed_two, grad_out, grad, grad * grad * valid, valid))


def ffn_back_kernel(
    side, low_ref, grad_ref, slope_ref, mixed_ref, valid_ref, w1_a, w1_b, w2_a, w2_b, wo_a, wo_b, weights_ref,
    pre_ref, mixed_grad_ref, low_mixed_ref, ctx_grad_ref, vec_ref, hidden_ref,
):
    low = low_ref[...]
    grad_first = grad_ref[...]
    width = w1_a.shape[1]
    step = 512

    @pl.when(pl.program_id(0) == 0)
    def _():
        hidden_ref[...] = jnp.zeros_like(hidden_ref)

    for half, (w1, w2) in enumerate(((w1_a, w2_a), (w1_b, w2_b))):
        for at in range(0, width, step):
            here = slice(half * width + at, half * width + at + step)
            grad_pre = (dot(low, w2[at : at + step, :], 1, 1) * slope_ref[:, here].astype(f32)).astype(bf16)
            pre_ref[:, here] = grad_pre
            total = jnp.sum(grad_pre.astype(f32), axis=0, keepdims=True)
            for piece in range(0, step, 256):
                row, lane = divmod(at + piece, D)
                hidden_ref[4 * half + row : 4 * half + row + 1, lane : lane + 256] += total[:, piece : piece + 256]
            grad_first += dot(grad_pre, w1[:, at : at + step], 1, 1)
    normed_one, inverse_one = normalise(mixed_ref[...])
    grad_mixed = norm_back(grad_first, normed_one, inverse_one, weights_ref[GAIN_ONE])
    mixed_grad_ref[...] = grad_mixed
    low_mixed = grad_mixed.astype(bf16)
    low_mixed_ref[...] = low_mixed
    head_width = wo_a.shape[0]
    ctx_grad_ref[:, :head_width] = dot(low_mixed, wo_a[...], 1, 1).astype(bf16)
    ctx_grad_ref[:, head_width:] = dot(low_mixed, wo_b[...], 1, 1).astype(bf16)
    valid = as_column(valid_ref[0].astype(f32))
    add_rows(
        vec_ref,
        (grad_first * normed_one, grad_first, grad_mixed, grad_first * grad_first * valid, grad_mixed * grad_mixed * valid),
    )


def attend_back_kernel(side, q_ref, k_ref, v_ref, p_ref, ctx_ref, ctx_grad_ref, out_ref, vec_ref):
    lane = lax.broadcasted_iota(jnp.int32, (1, PAIR), 1)
    q, k, v = q_ref[...], k_ref[...], v_ref[...]
    ctx, ctx_grad = ctx_ref[...].astype(f32), ctx_grad_ref[...]
    dq, dk, dv = [], 0.0, 0.0
    for head in range(2):
        ours = lane // HEAD_DIM == head
        masked = jnp.where(ours, ctx_grad, 0)
        inner = jnp.sum(masked.astype(f32) * ctx, axis=-1, keepdims=True)
        probs = p_ref[0, head]
        grad_scores = (probs.astype(f32) * (dot(masked, v, 1, 1) - inner)).astype(bf16)
        dq.append(dot(grad_scores, k))
        dk += dot(jnp.where(ours, q, 0), grad_scores, 0, 0)
        dv += dot(masked, probs, 0, 0)
    out_ref[0, :, :PAIR] = (jnp.where(lane < HEAD_DIM, dq[0], dq[1]) * HEAD_DIM ** -0.5).astype(bf16)
    out_ref[0, :, PAIR : 2 * PAIR] = dk.T.astype(bf16)
    out_ref[0, :, 2 * PAIR :] = dv.T.astype(bf16)

    @pl.when(pl.program_id(1) == 0)
    def _():
        vec_ref[...] = jnp.zeros_like(vec_ref)

    vec_ref[0, 0:1, :] += jnp.sum(out_ref[0].astype(f32), axis=0, keepdims=True)


def input_grad_kernel(side, mixed_grad_ref, valid_ref, *refs):
    *three, wq_a, wq_b, wk_a, wk_b, wv_a, wv_b, out_ref, vec_ref = refs
    grad_in = mixed_grad_ref[...]
    for pair, rows in enumerate(three):
        here = slice(pair * PAIR, (pair + 1) * PAIR)
        for half, weights in enumerate(((wq_a, wk_a, wv_a), (wq_b, wk_b, wv_b))):
            weight = jnp.concatenate([w[:, here] for w in weights], 1)
            grad_in += dot(rows[half], weight, 1, 1)
    out_ref[...] = grad_in.astype(bf16)
    add_rows(vec_ref, (grad_in * grad_in * as_column(valid_ref[0].astype(f32)),))


def run_kernel(kernel, grid, token, operands, outs, scratch=(), micros=1):
    steps = grid if isinstance(grid, tuple) else (grid,)

    def spec(block, kind):
        rest = (0,) * (len(block) - 1)
        if callable(kind):
            return pl.BlockSpec(block, kind)
        if kind == "all":
            return pl.BlockSpec(block, lambda *i: (0,) + rest, pipeline_mode=pl.Buffered(1))
        if kind == "sum":
            return pl.BlockSpec(block, lambda *i: (0,) + rest)
        if kind == "shared":
            return pl.BlockSpec(block, lambda i, s: (s[0] * grid + i,) + rest)
        return pl.BlockSpec(block, lambda i, s: (i,) + rest)

    return pl.pallas_call(
        kernel,
        grid_spec=pltpu.PrefetchScalarGridSpec(
            num_scalar_prefetch=1,
            grid=steps,
            in_specs=[spec(block, kind) for _, block, kind in operands],
            out_specs=[spec(block, kind) for _, block, kind in outs],
            scratch_shapes=list(scratch),
        ),
        out_shape=[shape for shape, _, _ in outs],
        compiler_params=pltpu.CompilerParams(vmem_limit_bytes=VMEM_BYTES),
        cost_estimate=pl.CostEstimate(flops=int(micros * 1.1e9), bytes_accessed=0, transcendentals=0),
    )(token, *[array for array, _, _ in operands])


def like(shape, dtype):
    return jax.ShapeDtypeStruct(shape, dtype)


def whole(array):
    return (array, array.shape, "all")


def swap_narrow(values):
    return lax.ppermute(values, "narrow", [(0, 1), (1, 0)])


class WideSum:
    def __init__(self, values, size):
        bits = size.bit_length() - 1
        late = list(range(3, bits))
        first = [0, 1, 2][:bits]
        turned = [first[i:] + first[:i] + late for i in range(3)]
        self.size, self.bits = size, bits
        self.orders = [(turned[0], turned[1]), (turned[2], turned[2])]
        cut = values.shape[0] * 2 // 3
        self.parts = [values[:cut], values[cut:]]
        self.step = 0

    def move(self, values, masks):
        return lax.ppermute(
            values,
            ("wide", "narrow"),
            [(w * 2 + c, (w ^ masks[c]) * 2 + c) for w in range(self.size) for c in range(2)],
        )

    def start(self):
        halving = self.step < self.bits
        at = self.step if halving else 2 * self.bits - 1 - self.step
        moving = []
        self.kept, self.mine = [], []
        for part, orders in zip(self.parts, self.orders):
            masks = [1 << order[at] for order in orders]
            bit = jnp.where(lax.axis_index("narrow") == 0, orders[0][at], orders[1][at])
            mine = (lax.axis_index("wide") >> bit) & 1
            if halving:
                half = part.shape[0] // 2
                sent = lax.dynamic_slice_in_dim(part, (1 - mine) * half, half, 0)
                self.kept.append(lax.dynamic_slice_in_dim(part, mine * half, half, 0))
            else:
                sent = part
                self.kept.append(part)
            self.mine.append(mine)
            moving.append(self.move(sent, masks))
        return moving

    def finish(self, moved):
        if self.step < self.bits:
            self.parts = [(k.astype(f32) + m.astype(f32)).astype(bf16) for k, m in zip(self.kept, moved)]
        else:
            self.parts = [
                jnp.where(mine == 1, jnp.concatenate([m, k], 0), jnp.concatenate([k, m], 0))
                for mine, k, m in zip(self.mine, self.kept, moved)
            ]
        self.step += 1

    @property
    def done(self):
        return self.step == 2 * self.bits

    def result(self):
        return jnp.concatenate(self.parts, 0).astype(f32)


class SmallSum:
    def __init__(self, values, size):
        self.parts, self.size, self.step = [values], size, 0
        self.bits = size.bit_length() - 1

    def start(self):
        return [lax.ppermute(self.parts[0], "wide", [(i, i ^ (1 << self.step)) for i in range(self.size)])]

    def finish(self, moved):
        self.parts = [self.parts[0] + moved[0]]
        self.step += 1

    @property
    def done(self):
        return self.step == self.bits


def slot(sums, compute, token):
    live = [s for s in sums if not s.done]
    moving = [s.start() for s in live]
    outs = compute(token) if compute else ()
    moving, outs, token = lax.optimization_barrier((moving, outs, token))
    for one, moved in zip(live, moving):
        one.finish(moved)
    return outs, token


def body(size, *arrays):
    (
        inputs, segments, valid, w_query, w_key, w_value, b_query, b_value, w_attn_out, b_attn_out,
        gain_one, shift_one, w_ffn_in, b_ffn_in, w_ffn_out, b_ffn_out, gain_two, shift_two, out_grad,
    ) = arrays
    side = lax.axis_index("narrow")
    rows = inputs.shape[0] // 2
    seqs = rows // SEQ_LEN
    head_width = w_query.shape[1]
    hidden = w_ffn_in.shape[1]
    pairs = head_width // PAIR
    token = side.astype(jnp.int32).reshape(1)
    row_block = 256
    blocks = rows // row_block

    def pair_of(array):
        return (array, swap_narrow(array))

    def join_rows(array, other):
        return jnp.where(
            side == 0,
            jnp.concatenate([array, other], 0),
            jnp.concatenate([other, array], 0),
        )

    own_vectors = jnp.concatenate([b_query, b_value, b_ffn_in])
    vectors = jnp.concatenate(
        [own_vectors, swap_narrow(own_vectors), b_attn_out, b_ffn_out, gain_one, shift_one, gain_two, shift_two]
    )
    vectors = jnp.pad(vectors.astype(f32).reshape(-1, D), ((0, 4), (0, 0)))
    wq, wk, wv = pair_of(w_query), pair_of(w_key), pair_of(w_value)
    wo, w1, w2 = pair_of(w_attn_out), pair_of(w_ffn_in), pair_of(w_ffn_out)
    seg_rows = segments.reshape(-1, 1, SEQ_LEN)
    valid_seq = valid.reshape(-1, 1, SEQ_LEN)
    valid_block = valid.reshape(-1, 1, row_block)
    seq = (SEQ_LEN, D)
    blk = (row_block, D)
    wide_blk = (row_block, 2 * hidden)
    low_rows = like((rows, D), bf16)
    full_rows = like((rows, D), f32)
    sums_shape = (like((8, D), f32), (8, D), "sum")

    queries, keys, values, probs, context, mixed = run_kernel(
        attend_kernel,
        seqs,
        token,
        [(inputs, seq, "shared"), (seg_rows, (1, 1, SEQ_LEN), "shared"), (valid_seq, (1, 1, SEQ_LEN), "shared")]
        + [whole(w) for w in wq + wk + wv + wo]
        + [whole(vectors)],
        [(low_rows, seq, "own")] * 3
        + [(like((seqs, 4 * pairs, SEQ_LEN, SEQ_LEN), bf16), (1, 4 * pairs, SEQ_LEN, SEQ_LEN), "own")]
        + [(low_rows, seq, "own"), (full_rows, seq, "own")],
        [pltpu.VMEM((SEQ_LEN, SEQ_LEN), f32)],
        30,
    )
    low_first, activated, slope, final, grad_second, low_second, vec_two = run_kernel(
        ffn_kernel,
        blocks,
        token,
        [(mixed, blk, "own"), (valid_block, (1, 1, row_block), "shared"), (out_grad, blk, "shared")]
        + [whole(w) for w in w1 + w2]
        + [whole(vectors)],
        [
            (low_rows, blk, "own"),
            (like((rows, 2 * hidden), bf16), wide_blk, "own"),
            (like((rows, 2 * hidden), bf16), wide_blk, "own"),
            (low_rows, blk, "own"),
            (full_rows, blk, "own"),
            (low_rows, blk, "own"),
            sums_shape,
        ],
        (),
        30,
    )

    def product(left, right):
        return dot(left, right, 0, 0).astype(bf16)

    def meet(own, moved):
        return (own.astype(f32) + moved.astype(f32)).astype(bf16)

    sent = product(activated[:, hidden:], low_second)
    moved = swap_narrow(sent)
    output = join_rows(final, swap_narrow(final))
    sum_out = WideSum(meet(product(activated[:, :hidden], low_second), moved), size)

    def ffn_back(first_block):
        half = rows // 2
        many = blocks // 2

        def at(i, s):
            return (first_block + i, 0)

        def run(token):
            return tuple(
                run_kernel(
                    ffn_back_kernel,
                    many,
                    token,
                    [
                        (low_second, blk, at),
                        (grad_second, blk, at),
                        (slope, wide_blk, at),
                        (mixed, blk, at),
                        (valid_block, (1, 1, row_block), lambda i, s: (s[0] * blocks + first_block + i, 0, 0)),
                    ]
                    + [whole(w) for w in w1 + w2 + wo]
                    + [whole(vectors)],
                    [
                        (like((half, 2 * hidden), bf16), wide_blk, "own"),
                        (like((half, D), f32), blk, "own"),
                        (like((half, D), bf16), blk, "own"),
                        (like((half, D), bf16), blk, "own"),
                        sums_shape,
                        sums_shape,
                    ],
                    (),
                    13,
                )
            )

        return run

    back_a, token = slot([sum_out], ffn_back(0), token)
    back_b, token = slot([sum_out], ffn_back(blocks // 2), token)
    grad_pre, grad_mixed, low_mixed, grad_context = (
        jnp.concatenate([x, y], 0) for x, y in zip(back_a[:4], back_b[:4])
    )
    vec_one, vec_hidden = back_a[4] + back_b[4], back_a[5] + back_b[5]

    def grad_ffn_in(token):
        moved = swap_narrow(product(low_first, grad_pre[:, hidden:]))
        return (meet(product(low_first, grad_pre[:, :hidden]), moved),)

    (d_w_ffn_in,), token = slot([sum_out], grad_ffn_in, token)
    sum_in = WideSum(d_w_ffn_in, size)

    def attend_back(pair):
        def column(h, i, s):
            return (i, pair + h * pairs)

        def run(token):
            return tuple(
                run_kernel(
                    attend_back_kernel,
                    (2, seqs),
                    token,
                    [(a, (SEQ_LEN, PAIR), column) for a in (queries, keys, values)]
                    + [(probs, (1, 2, SEQ_LEN, SEQ_LEN), lambda h, i, s: (i, pair + h * pairs, 0, 0))]
                    + [(a, (SEQ_LEN, PAIR), column) for a in (context, grad_context)],
                    [
                        (like((2, rows, 3 * PAIR), bf16), (1, SEQ_LEN, 3 * PAIR), lambda h, i, s: (h, i, 0)),
                        (like((2, 8, 3 * PAIR), f32), (1, 8, 3 * PAIR), lambda h, i, s: (h, 0, 0)),
                    ],
                    (),
                    9,
                )
            )

        return run

    own_rows = lax.dynamic_slice_in_dim(inputs, side * rows, rows, 0)
    three, vec_pairs = [], []
    pieces_own, pieces_sent = [], []
    for pair in range(pairs):
        (grads, vec_pair), token = slot([sum_out, sum_in], attend_back(pair), token)
        three.append(grads)
        vec_pairs.append(vec_pair)
    sent = jnp.concatenate([product(low_mixed, context[:, head_width:])] + [product(own_rows, g[1]) for g in three], 1)
    own = jnp.concatenate([product(low_mixed, context[:, :head_width])] + [product(own_rows, g[0]) for g in three], 1)
    sum_attn = WideSum(meet(own, swap_narrow(sent)), size)

    def last(token):
        return tuple(
            run_kernel(
                input_grad_kernel,
                blocks,
                token,
                [(grad_mixed, blk, "own"), (valid_block, (1, 1, row_block), "shared")]
                + [(g, (2, row_block, 3 * PAIR), lambda i, s: (0, i, 0)) for g in three]
                + [whole(w) for w in wq + wk + wv],
                [(low_rows, blk, "own"), sums_shape],
                (),
                8,
            )
        )

    (grad_in, vec_in), token = slot([sum_out, sum_in, sum_attn], last, token)
    input_grad = join_rows(grad_in, swap_narrow(grad_in))

    def arrange(own, other):
        flat = [vec_pairs[p][h, :, k * PAIR : (k + 1) * PAIR] for h in (own, other) for k in (0, 2) for p in range(pairs)]
        width = 2 * head_width
        return [
            jnp.concatenate(flat[: len(flat) // 2], 1)[:, :width],
            vec_hidden[4 * own : 4 * own + 4],
        ]

    common = [vec_two, vec_one, vec_in]
    moved = swap_narrow(jnp.concatenate(common + arrange(1, 0), 0))
    small = SmallSum(jnp.concatenate(common + arrange(0, 1), 0) + moved, size)
    sums = [sum_out, sum_in, sum_attn, small]
    while not all(s.done for s in sums):
        _, token = slot(sums, None, token)
    small = small.parts[0]
    total = jnp.sum(jnp.stack([small[16], small[3], small[11], small[12]]), axis=1)
    rms = jnp.sqrt(total / (small[4, 0] * D))
    d_attn = sum_attn.result()
    three_way = [
        jnp.concatenate(
            [d_attn[:, head_width + (3 * p + k) * PAIR : head_width + (3 * p + k + 1) * PAIR] for p in range(pairs)], 1
        )
        for k in range(3)
    ]
    return (
        output,
        input_grad,
        *three_way,
        small[24, :head_width],
        small[24, head_width:],
        d_attn[:, :head_width].T,
        small[10],
        small[8],
        small[9],
        sum_in.result(),
        small[32 : 32 + hidden // D].reshape(-1),
        sum_out.result(),
        small[2],
        small[0],
        small[1],
        rms,
    )


def solution(mesh):
    row, col = P("narrow", None), P(None, "narrow")
    one, rows = P("narrow"), P("wide", None)
    in_specs = (
        rows, P("wide"), P("wide"), col, col, col, one, one, row, P(), P(), P(), col, one, row, P(), P(), P(), rows,
    )
    out_specs = (
        rows, rows, col, col, col, one, one, row, P(), P(), P(), col, one, row, P(), P(), P(), P(),
    )
    return jax.shard_map(
        partial(body, mesh.shape["wide"]), mesh=mesh, in_specs=in_specs, out_specs=out_specs, check_vma=False
    )
```

```python
from functools import partial

import jax
import jax.numpy as jnp
from jax import lax
from jax.experimental import pallas as pl
from jax.experimental.pallas import tpu as pltpu
from jax.sharding import PartitionSpec as P

D = 768
HEAD_DIM = 64
SEQ_LEN = 512
PAIR = 2 * HEAD_DIM
norm_eps = 1e-06
f32 = jnp.float32
bf16 = jnp.bfloat16
VMEM_BYTES = 58 << 20
LIGHT = pl.CostEstimate(flops=1 << 20, bytes_accessed=0, transcendentals=0)
B_OUT, B_FFN, GAIN_ONE, SHIFT_ONE, GAIN_TWO, SHIFT_TWO = (slice(row, row + 1) for row in range(6, 12))


def dot(left, right, left_dim=1, right_dim=0):
    return lax.dot_general(
        left, right, (((left_dim,), (right_dim,)), ((), ())), preferred_element_type=f32
    )


def normalise(values):
    centred = values - jnp.mean(values, axis=-1, keepdims=True)
    inverse = lax.rsqrt(jnp.mean(centred * centred, axis=-1, keepdims=True) + norm_eps)
    return centred * inverse, inverse


def norm_back(grad_rows, normed, inverse, gain):
    inner = grad_rows * gain
    centre_part = jnp.mean(inner, axis=-1, keepdims=True)
    slope_part = jnp.mean(inner * normed, axis=-1, keepdims=True)
    return inverse * (inner - centre_part - normed * slope_part)


def as_column(row):
    return jnp.broadcast_to(row, (8, row.shape[1])).T[:, :1]


def add_rows(ref, rows):
    for at, values in enumerate(rows):
        ref[at : at + 1, :] += jnp.sum(values, axis=0, keepdims=True)


def clear_first(ref):
    @pl.when(pl.program_id(0) == 0)
    def _():
        ref[...] = jnp.zeros_like(ref)


def by_head(rows, lane):
    return jnp.concatenate([jnp.where(lane < HEAD_DIM, rows, 0), jnp.where(lane < HEAD_DIM, 0, rows)], 0)


def gelu_both(pre):
    below = 0.5 * lax.erf(pre * 0.7071067811865476) + 0.5
    return pre * below, below + pre * (0.3989422804014327 * jnp.exp(pre * pre * -0.5))


def attend_kernel(
    side, x_ref, seg_ref, valid_ref, wq_a, wq_b, wk_a, wk_b, wv_a, wv_b, wo_a, wo_b, vec_ref,
    q_ref, k_ref, v_ref, p_ref, ctx_ref, mixed_ref, bias_ref,
):
    x = x_ref[...]
    seg = seg_ref[0].astype(f32)
    allowed = (as_column(seg) == seg) & (valid_ref[0] == 1)
    bias_ref[...] = jnp.where(allowed, 0.0, -1e30)
    width = wq_a.shape[1]
    for at, (wq, wk, wv) in enumerate(((wq_a, wk_a, wv_a), (wq_b, wk_b, wv_b))):
        here = slice(at * width, (at + 1) * width)
        q_ref[:, here] = (dot(x, wq[...]) + vec_ref[3 * at : 3 * at + 1, :width]).astype(bf16) * jnp.asarray(HEAD_DIM ** -0.5, bf16)
        k_ref[:, here] = dot(x, wk[...]).astype(bf16)
        v_ref[:, here] = (dot(x, wv[...]) + vec_ref[3 * at : 3 * at + 1, width:]).astype(bf16)

    lane = lax.broadcasted_iota(jnp.int32, (1, PAIR), 1)
    for pair in range(2 * width // PAIR):
        here = slice(pair * PAIR, (pair + 1) * PAIR)
        scores = dot(by_head(q_ref[:, here], lane), k_ref[:, here], 1, 1)
        parts = []
        for head in range(2):
            ours = scores[head * SEQ_LEN : (head + 1) * SEQ_LEN] + bias_ref[...]
            shifted = jnp.exp(ours - jnp.max(ours, axis=-1, keepdims=True))
            p_ref[0, 2 * pair + head] = (shifted * (1.0 / jnp.sum(shifted, axis=-1, keepdims=True))).astype(bf16)
        both = dot(p_ref[0, 2 * pair : 2 * pair + 2].reshape(2 * SEQ_LEN, SEQ_LEN), v_ref[:, here])
        ctx_ref[:, here] = jnp.where(lane < HEAD_DIM, both[:SEQ_LEN], both[SEQ_LEN:]).astype(bf16)
    attn = dot(ctx_ref[:, :width], wo_a[...]) + dot(ctx_ref[:, width:], wo_b[...])
    mixed_ref[...] = x.astype(f32) + attn + vec_ref[B_OUT]


SUB = 256


def ffn_kernel(
    side, mixed_ref, valid_ref, cot_ref, w1_a, w1_b, w2_a, w2_b, weights_ref,
    low_first_ref, act_ref, slope_ref, out_ref, grad_ref, low_ref, vec_ref,
):
    normed_one, _ = normalise(mixed_ref[...])
    first = normed_one * weights_ref[GAIN_ONE] + weights_ref[SHIFT_ONE]
    low_first = first.astype(bf16)
    low_first_ref[...] = low_first
    second = first + weights_ref[B_FFN]
    width = w1_a.shape[1]
    step = 256
    for half, (w1, w2) in enumerate(((w1_a, w2_a), (w1_b, w2_b))):
        for at in range(0, width, step):
            here = slice(half * width + at, half * width + at + step)
            pre = dot(low_first, w1[:, at : at + step]) + weights_ref[3 * half + 1 + at // D : 3 * half + 2 + at // D, at % D : at % D + step]
            act, slope = gelu_both(pre)
            act = act.astype(bf16)
            act_ref[:, here] = act
            slope_ref[:, here] = slope.astype(bf16)
            second += dot(act, w2[at : at + step, :])
    normed_two, inverse_two = normalise(second)
    gain = weights_ref[GAIN_TWO]
    out_ref[...] = (normed_two * gain + weights_ref[SHIFT_TWO]).astype(bf16)
    valid = as_column(valid_ref[0].astype(f32))
    grad_out = cot_ref[...].astype(f32) * valid
    grad = norm_back(grad_out, normed_two, inverse_two, gain)
    grad_ref[...] = grad
    low_ref[...] = grad.astype(bf16)
    clear_first(vec_ref)
    add_rows(vec_ref, (grad_out * normed_two, grad_out, grad, grad * grad * valid, valid))


def ffn_back_chunk(low_ref, low_first_ref, act_ref, slope_ref, w1, w2, both_ref, total_ref, hidden_ref, pre_ref):
    step = pl.program_id(0)
    both_ref[0, 0] = dot(act_ref[...], low_ref[...], 0, 0).astype(bf16)
    grad_pre = dot(low_ref[...], w2[...], 1, 1) * slope_ref[...].astype(f32)
    pre_ref[...] = grad_pre.astype(bf16)
    hidden_ref[pl.ds(step, 1), :] = jnp.sum(grad_pre, axis=0, keepdims=True)
    both_ref[1, 0] = dot(low_first_ref[...], pre_ref[...], 0, 0).astype(bf16)
    total_ref[...] += dot(pre_ref[...], w1[...], 1, 1)


def ffn_back_other_kernel(
    side, low_ref, low_first_ref, grad_ref, act_ref, slope_ref, w1, w2,
    both_ref, total_ref, hidden_ref, pre_ref,
):
    @pl.when(pl.program_id(0) == 0)
    def _():
        total_ref[...] = grad_ref[...]

    ffn_back_chunk(
        low_ref, low_first_ref, act_ref, slope_ref, w1, w2, both_ref, total_ref, hidden_ref, pre_ref
    )


def ffn_back_own_kernel(
    side, low_ref, low_first_ref, grad_ref, act_ref, slope_ref, w1, w2, mixed_ref, valid_ref, wo_a, wo_b,
    weights_ref,
    both_ref, mixed_grad_ref, low_mixed_ref, ctx_grad_ref, hidden_ref, vec_ref, total_ref, pre_ref,
):
    @pl.when(pl.program_id(0) == 0)
    def _():
        total_ref[...] = grad_ref[...]

    ffn_back_chunk(
        low_ref, low_first_ref, act_ref, slope_ref, w1, w2, both_ref, total_ref, hidden_ref, pre_ref
    )

    @pl.when(pl.program_id(0) == pl.num_programs(0) - 1)
    def _():
        vec_ref[...] = jnp.zeros_like(vec_ref)
        head_width = wo_a.shape[0]
        for at in range(0, mixed_ref.shape[0], SUB):
            here = slice(at, at + SUB)
            normed_one, inverse_one = normalise(mixed_ref[here])
            grad_first = total_ref[here]
            grad_mixed = norm_back(grad_first, normed_one, inverse_one, weights_ref[GAIN_ONE])
            mixed_grad_ref[here] = grad_mixed
            low_mixed_ref[here] = grad_mixed.astype(bf16)
            valid = as_column(valid_ref[at // SUB].astype(f32))
            add_rows(
                vec_ref,
                (
                    grad_first * normed_one,
                    grad_first,
                    grad_mixed,
                    grad_first * grad_first * valid,
                    grad_mixed * grad_mixed * valid,
                ),
            )
        ctx_grad_ref[:, :head_width] = dot(low_mixed_ref[...], wo_a[...], 1, 1).astype(bf16)
        ctx_grad_ref[:, head_width:] = dot(low_mixed_ref[...], wo_b[...], 1, 1).astype(bf16)


def attend_back_kernel(side, q_ref, k_ref, v_ref, p_ref, ctx_ref, ctx_grad_ref, out_ref, vec_ref):
    lane = lax.broadcasted_iota(jnp.int32, (1, PAIR), 1)
    q, k, v = q_ref[...], k_ref[...], v_ref[...]
    masked = by_head(ctx_grad_ref[...], lane)
    ctx = ctx_ref[...].astype(f32)
    inner = jnp.sum(masked.astype(f32) * jnp.concatenate([ctx, ctx], 0), axis=-1, keepdims=True)
    probs = p_ref[0].reshape(2 * SEQ_LEN, SEQ_LEN)
    grad_scores = (probs.astype(f32) * (dot(masked, v, 1, 1) - inner)).astype(bf16)
    dq = dot(grad_scores, k)
    dk = dot(by_head(q, lane), grad_scores, 0, 0)
    dv = dot(masked, probs, 0, 0)
    out_ref[0, :, :PAIR] = (jnp.where(lane < HEAD_DIM, dq[:SEQ_LEN], dq[SEQ_LEN:]) * HEAD_DIM ** -0.5).astype(bf16)
    out_ref[0, :, PAIR : 2 * PAIR] = dk.T.astype(bf16)
    out_ref[0, :, 2 * PAIR :] = dv.T.astype(bf16)

    @pl.when((pl.program_id(1) == 0) & (pl.program_id(2) == 0))
    def _():
        vec_ref[...] = jnp.zeros_like(vec_ref)

    here = pl.ds(pl.multiple_of(pl.program_id(2) * 3 * PAIR, PAIR), 3 * PAIR)
    vec_ref[0, 0:1, here] += jnp.sum(out_ref[0].astype(f32), axis=0, keepdims=True)


def attend_weights_kernel(side, three_ref, x_ref, ctx_ref, low_mixed_ref, out_ref):
    width = ctx_ref.shape[1]
    out_ref[:width] = dot(ctx_ref[...], low_mixed_ref[...], 0, 0).astype(bf16)
    out_ref[width:] = dot(three_ref[0], x_ref[...], 0, 0).astype(bf16)


def input_grad_kernel(side, mixed_grad_ref, valid_ref, *refs):
    three_ref, wq_a, wq_b, wk_a, wk_b, wv_a, wv_b, out_ref, vec_ref = refs
    grad_in = mixed_grad_ref[...]
    for half, weights in enumerate(((wq_a, wk_a, wv_a), (wq_b, wk_b, wv_b))):
        for pair in range(wq_a.shape[1] // PAIR):
            here = slice(pair * PAIR, (pair + 1) * PAIR)
            weight = jnp.concatenate([w[:, here] for w in weights], 1)
            grad_in += dot(three_ref[half, :, 3 * pair * PAIR : 3 * (pair + 1) * PAIR], weight, 1, 1)
    out_ref[...] = grad_in.astype(bf16)

    @pl.when(pl.program_id(0) == 0)
    def _():
        vec_ref[...] = jnp.zeros_like(vec_ref)

    add_rows(vec_ref, (grad_in * grad_in * as_column(valid_ref[0].astype(f32)),))


def meet_kernel(sources, own, moved, *outs):
    count = sources.shape[0] // 2
    start = 0
    for part in range(2):
        kept, sent = outs[2 * part : 2 * part + 2]
        size = 2 * kept.shape[0] // count
        for block in range(count):
            at = pl.multiple_of(start + sources[part * count + block] * size, size)
            total = (own[pl.ds(at, size)].astype(f32) + moved[pl.ds(at, size)].astype(f32)).astype(bf16)
            ref, row = (kept, block) if block < count // 2 else (sent, block - count // 2)
            ref[row * size : (row + 1) * size] = total
        start += count * size


def ordered_blocks(places, pieces):
    count = places.shape[0] // 2
    start = 0
    for part in range(2):
        low, high = pieces[2 * part], pieces[2 * part + 1]
        size = 2 * low.shape[0] // count
        for block in range(count):
            place = places[part * count + block]
            below = place < count // 2
            at = pl.multiple_of(jnp.where(below, place, 0) * size, size)
            after = pl.multiple_of(jnp.where(below, 0, place - count // 2) * size, size)
            rows = jnp.where(below, low[pl.ds(at, size)], high[pl.ds(after, size)])
            yield start + block * size, rows.astype(f32)
        start += count * size


def place_ffn_kernel(places, *refs):
    *pieces, w2_ref, w1_ref = refs
    for row, rows in ordered_blocks(places, pieces):
        size = rows.shape[0]
        if row < w2_ref.shape[0]:
            w2_ref[row : row + size] = rows
        else:
            chunk, row = divmod(row - w2_ref.shape[0], D)
            w1_ref[row : row + size, chunk * D : (chunk + 1) * D] = rows


def place_attend_kernel(places, *refs):
    *pieces, wo_ref, wq_ref, wk_ref, wv_ref, sorted_ref = refs
    for row, rows in ordered_blocks(places, pieces):
        sorted_ref[row : row + rows.shape[0]] = rows
    width = wo_ref.shape[0]
    wo_ref[...] = sorted_ref[:width]
    for pair in range(width // PAIR):
        for at, ref in enumerate((wq_ref, wk_ref, wv_ref)):
            start = width + (3 * pair + at) * PAIR
            ref[:, pair * PAIR : (pair + 1) * PAIR] = sorted_ref[start : start + PAIR].T


def run_kernel(kernel, grid, token, operands, outs, scratch=(), micros=1):
    steps = grid if isinstance(grid, tuple) else (grid,)

    def spec(block, kind):
        rest = (0,) * (len(block) - 1)
        if callable(kind):
            return pl.BlockSpec(block, kind)
        if kind == "all":
            return pl.BlockSpec(block, lambda *i: (0,) + rest, pipeline_mode=pl.Buffered(1))
        if kind == "side":
            return pl.BlockSpec(block, lambda *i: (i[-1][0],) + rest, pipeline_mode=pl.Buffered(1))
        if kind == "sum":
            return pl.BlockSpec(block, lambda *i: (0,) + rest)
        if kind == "shared":
            return pl.BlockSpec(block, lambda i, s: (s[0] * grid + i,) + rest)
        return pl.BlockSpec(block, lambda i, s: (i,) + rest)

    return pl.pallas_call(
        kernel,
        grid_spec=pltpu.PrefetchScalarGridSpec(
            num_scalar_prefetch=1,
            grid=steps,
            in_specs=[spec(block, kind) for _, block, kind in operands],
            out_specs=[spec(block, kind) for _, block, kind in outs],
            scratch_shapes=list(scratch),
        ),
        out_shape=[shape for shape, _, _ in outs],
        compiler_params=pltpu.CompilerParams(vmem_limit_bytes=VMEM_BYTES),
        cost_estimate=LIGHT,
    )(token, *[array for array, _, _ in operands])


def like(shape, dtype):
    return jax.ShapeDtypeStruct(shape, dtype)


def whole(array):
    return (array, array.shape, "all")


def swap_narrow(values):
    return lax.ppermute(values, "narrow", [(0, 1), (1, 0)])


class WideSum:
    def __init__(self, own, moved, size):
        bits = size.bit_length() - 1
        late = list(range(3, bits))
        first = [0, 1, 2][:bits]
        turned = [first[i:] + first[:i] + late for i in range(3)]
        self.size, self.bits = size, bits
        self.orders = [(turned[0], turned[1]), (turned[2], turned[2])]
        self.step = 0
        me, core = lax.axis_index("wide"), lax.axis_index("narrow")
        place = jnp.arange(size, dtype=jnp.int32)

        def spread(value, order):
            return sum(((value >> (bits - 1 - at)) & 1) << bit for at, bit in enumerate(order))

        def gather(value, order):
            return sum(((value >> bit) & 1) << (bits - 1 - at) for at, bit in enumerate(order))

        def both(change, value):
            return jnp.concatenate([jnp.where(core == 0, *(change(value, o) for o in pair)) for pair in self.orders])

        sources = both(spread, place) ^ me
        self.places = both(gather, place ^ me)
        rows = own.shape[0]
        halves = (rows // 3, rows // 6)
        self.parts = pl.pallas_call(
            meet_kernel,
            in_specs=[pl.BlockSpec(memory_space=pltpu.SMEM)] + [pl.BlockSpec(memory_space=pltpu.VMEM)] * 2,
            out_specs=[pl.BlockSpec(memory_space=pltpu.VMEM)] * 4,
            out_shape=[like((half, D), bf16) for half in halves for _ in range(2)],
            compiler_params=pltpu.CompilerParams(vmem_limit_bytes=VMEM_BYTES),
            cost_estimate=LIGHT,
        )(sources, own, moved)

    def start(self):
        halving = self.step < self.bits
        at = self.step if halving else 2 * self.bits - 1 - self.step
        moving = []
        for part, orders in enumerate(self.orders):
            masks = [1 << order[at] for order in orders]
            pairs = [(w * 2 + c, (w ^ masks[c]) * 2 + c) for w in range(self.size) for c in range(2)]
            moving.append(lax.ppermute(self.parts[2 * part + 1] if halving else self.parts[part], ("wide", "narrow"), pairs))
        return moving

    def finish(self, moved):
        parts = []
        for part, got in enumerate(moved):
            if self.step < self.bits:
                kept = self.parts[2 * part]
                half = kept.shape[0] // 2
                cuts = ((0, half), (half, 2 * half)) if self.step < self.bits - 1 else ((0, 2 * half),)
                parts += [(kept[a:b].astype(f32) + got[a:b].astype(f32)).astype(bf16) for a, b in cuts]
            elif self.step < 2 * self.bits - 1:
                parts.append(jnp.concatenate([self.parts[part], got], 0))
            else:
                parts += [self.parts[part], got]
        self.parts = parts
        self.step += 1

    @property
    def done(self):
        return self.step == 2 * self.bits

    def result(self, kernel, outs, scratch=()):
        return pl.pallas_call(
            kernel,
            in_specs=[pl.BlockSpec(memory_space=pltpu.SMEM)] + [pl.BlockSpec(memory_space=pltpu.VMEM)] * 4,
            out_specs=[pl.BlockSpec(memory_space=pltpu.VMEM)] * len(outs),
            out_shape=[like(shape, f32) for shape in outs],
            scratch_shapes=list(scratch),
            compiler_params=pltpu.CompilerParams(vmem_limit_bytes=VMEM_BYTES),
            cost_estimate=LIGHT,
        )(self.places, *self.parts)


class SmallSum:
    def __init__(self, values, size):
        self.parts, self.size, self.step = [values], size, 0
        self.bits = size.bit_length() - 1

    def start(self):
        return [lax.ppermute(self.parts[0], "wide", [(i, i ^ (1 << self.step)) for i in range(self.size)])]

    def finish(self, moved):
        self.parts = [self.parts[0] + moved[0]]
        self.step += 1

    @property
    def done(self):
        return self.step == self.bits


def slot(sums, compute, token):
    live = [s for s in sums if not s.done]
    parts, token = lax.optimization_barrier(([s.parts for s in live], token))
    for one, held in zip(live, parts):
        one.parts = held
    moving = [s.start() for s in live]
    outs = compute(token) if compute else ()
    moving, outs, token = lax.optimization_barrier((moving, outs, token))
    for one, moved in zip(live, moving):
        one.finish(moved)
    return outs, token


def body(size, *arrays):
    (
        inputs, segments, valid, w_query, w_key, w_value, b_query, b_value, w_attn_out, b_attn_out,
        gain_one, shift_one, w_ffn_in, b_ffn_in, w_ffn_out, b_ffn_out, gain_two, shift_two, out_grad,
    ) = arrays
    side = lax.axis_index("narrow")
    rows = inputs.shape[0] // 2
    seqs = rows // SEQ_LEN
    head_width = w_query.shape[1]
    hidden = w_ffn_in.shape[1]
    pairs = head_width // PAIR
    token = side.astype(jnp.int32).reshape(1)
    row_block = 256
    blocks = rows // row_block

    def pair_of(array):
        return (array, swap_narrow(array))

    def join_rows(array, other):
        return jnp.where(
            side == 0,
            jnp.concatenate([array, other], 0),
            jnp.concatenate([other, array], 0),
        )

    own_vectors = jnp.concatenate([b_query, b_value, b_ffn_in])
    flat = [own_vectors, swap_narrow(own_vectors), b_attn_out, b_ffn_out, gain_one, shift_one, gain_two, shift_two]
    vectors, at = 0.0, 0
    for vector in flat:
        vectors += jnp.pad(vector.astype(f32), (at, 16 * D - at - vector.shape[0]))
        at += vector.shape[0]
    vectors = vectors.reshape(16, D)
    wq, wk, wv = pair_of(w_query), pair_of(w_key), pair_of(w_value)
    wo, w1, w2 = pair_of(w_attn_out), pair_of(w_ffn_in), pair_of(w_ffn_out)
    seg_rows = segments.reshape(-1, 1, SEQ_LEN)
    valid_seq = valid.reshape(-1, 1, SEQ_LEN)
    valid_block = valid.reshape(-1, 1, row_block)
    seq = (SEQ_LEN, D)
    blk = (row_block, D)
    low_rows = like((rows, D), bf16)
    full_rows = like((rows, D), f32)
    sums_shape = (like((8, D), f32), (8, D), "sum")

    queries, keys, values, probs, context, mixed = run_kernel(
        attend_kernel,
        seqs,
        token,
        [(inputs, seq, "shared"), (seg_rows, (1, 1, SEQ_LEN), "shared"), (valid_seq, (1, 1, SEQ_LEN), "shared")]
        + [whole(w) for w in wq + wk + wv + wo]
        + [whole(vectors)],
        [(low_rows, seq, "own")] * 3
        + [(like((seqs, 4 * pairs, SEQ_LEN, SEQ_LEN), bf16), (1, 4 * pairs, SEQ_LEN, SEQ_LEN), "own")]
        + [(low_rows, seq, "own"), (full_rows, seq, "own")],
        [pltpu.VMEM((SEQ_LEN, SEQ_LEN), f32)],
        30,
    )
    chunks = hidden // D
    row_shape = (rows, D)
    hidden_rows = like((rows, 2 * hidden), bf16)
    low_first, activated, slope, final, grad_second, low_second, vec_two = run_kernel(
        ffn_kernel,
        blocks,
        token,
        [(mixed, blk, "own"), (valid_block, (1, 1, row_block), "shared"), (out_grad, blk, "shared")]
        + [whole(w) for w in w1 + w2]
        + [whole(vectors)],
        [
            (low_rows, blk, "own"),
            (hidden_rows, (row_block, 2 * hidden), "own"),
            (hidden_rows, (row_block, 2 * hidden), "own"),
            (low_rows, blk, "own"),
            (full_rows, blk, "own"),
            (low_rows, blk, "own"),
            sums_shape,
        ],
        (),
        25,
    )

    def ffn_back(kernel, half, total, extra, outs, scratch):
        return run_kernel(
            kernel,
            chunks,
            token,
            [whole(a) for a in (low_second, low_first, total)]
            + [(a, (rows, D), lambda i, s: (0, half * chunks + i)) for a in (activated, slope)]
            + [(w1[half], (D, D), lambda i, s: (0, i)), (w2[half], (D, D), lambda i, s: (i, 0))]
            + extra,
            [(like((2, chunks, D, D), bf16), (2, 1, D, D), lambda i, s: (0, i, 0, 0))] + outs,
            scratch + [pltpu.VMEM((rows, D), bf16)],
            18,
        )

    valid_part = (valid_block, (blocks, 1, row_block), "side")
    sent, total, hidden_other = ffn_back(
        ffn_back_other_kernel, 1, grad_second, [], [(full_rows, row_shape, "sum"), sums_shape], []
    )
    moved = swap_narrow(sent)
    own, grad_mixed, low_mixed, grad_context, hidden_own, vec_one = ffn_back(
        ffn_back_own_kernel,
        0,
        total,
        [whole(mixed), valid_part] + [whole(w) for w in wo] + [whole(vectors)],
        [(full_rows, row_shape, "sum"), (low_rows, row_shape, "sum"), (low_rows, row_shape, "sum"), sums_shape, sums_shape],
        [pltpu.VMEM(row_shape, f32)],
    )
    sum_ffn = WideSum(own.reshape(-1, D), moved.reshape(-1, D), size)

    def attend_back(token):
        def column(h, i, p, s):
            return (i, h * pairs + p)

        three, vec_three = run_kernel(
            attend_back_kernel,
            (2, seqs, pairs),
            token,
            [(a, (SEQ_LEN, PAIR), column) for a in (queries, keys, values)]
            + [(probs, (1, 2, SEQ_LEN, SEQ_LEN), lambda h, i, p, s: (i, h * pairs + p, 0, 0))]
            + [(a, (SEQ_LEN, PAIR), column) for a in (context, grad_context)],
            [
                (like((2, rows, 3 * head_width), bf16), (1, SEQ_LEN, 3 * PAIR), lambda h, i, p, s: (h, i, p)),
                (like((2, 8, 3 * head_width), f32), (1, 8, 3 * head_width), lambda h, i, p, s: (h, 0, 0)),
            ],
            (),
            22,
        )

        return three, vec_three, weights(1, three, token)

    def weights(half, three, token):
        return run_kernel(
            attend_weights_kernel,
            1,
            token,
            [
                (three, (1, rows, 3 * head_width), lambda i, s: (half, 0, 0)),
                (inputs, row_shape, "side"),
                (context, (rows, head_width), lambda i, s: (0, half)),
                whole(low_mixed),
            ],
            [(like((4 * head_width, D), bf16), (4 * head_width, D), "sum")],
            (),
            5,
        )[0]

    (three, vec_three, sent), token = slot([sum_ffn], attend_back, token)
    (moved, own), token = slot([sum_ffn], lambda token: (swap_narrow(sent), weights(0, three, token)), token)
    sum_attn = WideSum(own, moved, size)

    def last(token):
        return tuple(
            run_kernel(
                input_grad_kernel,
                blocks,
                token,
                [(grad_mixed, blk, "own"), (valid_block, (1, 1, row_block), "shared")]
                + [(three, (2, row_block, 3 * head_width), lambda i, s: (0, i, 0))]
                + [whole(w) for w in wq + wk + wv],
                [(low_rows, blk, "own"), sums_shape],
                (),
                10,
            )
        )

    (grad_in, vec_in), token = slot([sum_ffn, sum_attn], last, token)
    output = join_rows(final, swap_narrow(final))
    input_grad = join_rows(grad_in, swap_narrow(grad_in))

    def arrange(own, other):
        flat = [vec_three[h, :, (3 * p + k) * PAIR : (3 * p + k + 1) * PAIR] for h in (own, other) for k in (0, 2) for p in range(pairs)]
        width = 2 * head_width
        return [
            jnp.concatenate(flat[: len(flat) // 2], 1)[:, :width],
            (hidden_own, hidden_other)[own],
        ]

    common = [vec_two, vec_one, vec_in]
    moved = swap_narrow(jnp.concatenate(common + arrange(1, 0), 0))
    small = SmallSum(jnp.concatenate(common + arrange(0, 1), 0) + moved, size)
    sums = [sum_ffn, sum_attn, small]
    while not all(s.done for s in sums):
        _, token = slot(sums, None, token)
    small = small.parts[0]
    total = jnp.sum(jnp.stack([small[16], small[3], small[11], small[12]]), axis=1)
    rms = jnp.sqrt(total / (small[4, 0] * D))
    d_w_out, d_w_in = sum_ffn.result(place_ffn_kernel, [(hidden, D), (D, hidden)])
    d_w_attn, *d_w_three = sum_attn.result(
        place_attend_kernel, [(head_width, D)] + [(D, head_width)] * 3, [pltpu.VMEM((4 * head_width, D), f32)]
    )
    return (
        output,
        input_grad,
        *d_w_three,
        small[24, :head_width],
        small[24, head_width:],
        d_w_attn,
        small[10],
        small[8],
        small[9],
        d_w_in,
        small[32 : 32 + chunks].reshape(-1),
        d_w_out,
        small[2],
        small[0],
        small[1],
        rms,
    )


def solution(mesh):
    row, col = P("narrow", None), P(None, "narrow")
    one, rows = P("narrow"), P("wide", None)
    in_specs = (
        rows, P("wide"), P("wide"), col, col, col, one, one, row, P(), P(), P(), col, one, row, P(), P(), P(), rows,
    )
    out_specs = (
        rows, rows, col, col, col, one, one, row, P(), P(), P(), col, one, row, P(), P(), P(), P(),
    )
    return jax.shard_map(
        partial(body, mesh.shape["wide"]), mesh=mesh, in_specs=in_specs, out_specs=out_specs, check_vma=False
    )
```

```python
from functools import partial

import jax
import jax.numpy as jnp
from jax import lax
from jax.experimental import pallas as pl
from jax.experimental.pallas import tpu as pltpu
from jax.sharding import PartitionSpec as P

D = 768
HEAD_DIM = 64
SEQ_LEN = 512
PAIR = 2 * HEAD_DIM
norm_eps = 1e-06
f32 = jnp.float32
bf16 = jnp.bfloat16
VMEM_BYTES = 58 << 20
LIGHT = pl.CostEstimate(flops=1 << 20, bytes_accessed=0, transcendentals=0)
B_OUT, B_FFN, GAIN_ONE, SHIFT_ONE, GAIN_TWO, SHIFT_TWO = (slice(row, row + 1) for row in range(6, 12))


def dot(left, right, left_dim=1, right_dim=0):
    return lax.dot_general(
        left, right, (((left_dim,), (right_dim,)), ((), ())), preferred_element_type=f32
    )


def normalise(values):
    centred = values - jnp.mean(values, axis=-1, keepdims=True)
    inverse = lax.rsqrt(jnp.mean(centred * centred, axis=-1, keepdims=True) + norm_eps)
    return centred * inverse, inverse


def norm_back(grad_rows, normed, inverse, gain):
    inner = grad_rows * gain
    centre_part = jnp.mean(inner, axis=-1, keepdims=True)
    slope_part = jnp.mean(inner * normed, axis=-1, keepdims=True)
    return inverse * (inner - centre_part - normed * slope_part)


def as_column(row):
    return jnp.broadcast_to(row, (8, row.shape[1])).T[:, :1]


def add_rows(ref, rows):
    for at, values in enumerate(rows):
        ref[at : at + 1, :] += jnp.sum(values, axis=0, keepdims=True)


def clear_first(ref):
    @pl.when(pl.program_id(0) == 0)
    def _():
        ref[...] = jnp.zeros_like(ref)


def by_head(rows, lane):
    return jnp.concatenate([jnp.where(lane < HEAD_DIM, rows, 0), jnp.where(lane < HEAD_DIM, 0, rows)], 0)


def gelu_both(pre):
    below = 0.5 * lax.erf(pre * 0.7071067811865476) + 0.5
    return pre * below, below + pre * (0.3989422804014327 * jnp.exp(pre * pre * -0.5))


def attend_kernel(
    side, x_ref, seg_ref, valid_ref, wq_a, wq_b, wk_a, wk_b, wv_a, wv_b, wo_a, wo_b, vec_ref,
    q_ref, k_ref, v_ref, p_ref, ctx_ref, mixed_ref, bias_ref,
):
    x = x_ref[...]
    seg = seg_ref[0].astype(f32)
    allowed = (as_column(seg) == seg) & (valid_ref[0] == 1)
    bias_ref[...] = jnp.where(allowed, 0.0, -1e30)
    width = wq_a.shape[1]
    for at, (wq, wk, wv) in enumerate(((wq_a, wk_a, wv_a), (wq_b, wk_b, wv_b))):
        here = slice(at * width, (at + 1) * width)
        q_ref[:, here] = (dot(x, wq[...]) + vec_ref[3 * at : 3 * at + 1, :width]).astype(bf16) * jnp.asarray(HEAD_DIM ** -0.5, bf16)
        k_ref[:, here] = dot(x, wk[...]).astype(bf16)
        v_ref[:, here] = (dot(x, wv[...]) + vec_ref[3 * at : 3 * at + 1, width:]).astype(bf16)

    lane = lax.broadcasted_iota(jnp.int32, (1, PAIR), 1)
    for pair in range(2 * width // PAIR):
        here = slice(pair * PAIR, (pair + 1) * PAIR)
        scores = dot(by_head(q_ref[:, here], lane), k_ref[:, here], 1, 1)
        parts = []
        for head in range(2):
            ours = scores[head * SEQ_LEN : (head + 1) * SEQ_LEN] + bias_ref[...]
            shifted = jnp.exp(ours - jnp.max(ours, axis=-1, keepdims=True))
            p_ref[0, 2 * pair + head] = (shifted * (1.0 / jnp.sum(shifted, axis=-1, keepdims=True))).astype(bf16)
        both = dot(p_ref[0, 2 * pair : 2 * pair + 2].reshape(2 * SEQ_LEN, SEQ_LEN), v_ref[:, here])
        ctx_ref[:, here] = jnp.where(lane < HEAD_DIM, both[:SEQ_LEN], both[SEQ_LEN:]).astype(bf16)
    attn = dot(ctx_ref[:, :width], wo_a[...]) + dot(ctx_ref[:, width:], wo_b[...])
    mixed_ref[...] = x.astype(f32) + attn + vec_ref[B_OUT]


SUB = 256


def ffn_kernel(
    side, mixed_ref, valid_ref, cot_ref, w1_a, w1_b, w2_a, w2_b, weights_ref,
    low_first_ref, act_ref, slope_ref, out_ref, grad_ref, low_ref, vec_ref,
):
    normed_one, _ = normalise(mixed_ref[...])
    first = normed_one * weights_ref[GAIN_ONE] + weights_ref[SHIFT_ONE]
    low_first = first.astype(bf16)
    low_first_ref[...] = low_first
    second = first + weights_ref[B_FFN]
    width = w1_a.shape[1]
    step = 256
    for half, (w1, w2) in enumerate(((w1_a, w2_a), (w1_b, w2_b))):
        for at in range(0, width, step):
            here = slice(half * width + at, half * width + at + step)
            pre = dot(low_first, w1[:, at : at + step]) + weights_ref[3 * half + 1 + at // D : 3 * half + 2 + at // D, at % D : at % D + step]
            act, slope = gelu_both(pre)
            act = act.astype(bf16)
            act_ref[:, here] = act
            slope_ref[:, here] = slope.astype(bf16)
            second += dot(act, w2[at : at + step, :])
    normed_two, inverse_two = normalise(second)
    gain = weights_ref[GAIN_TWO]
    out_ref[...] = (normed_two * gain + weights_ref[SHIFT_TWO]).astype(bf16)
    valid = as_column(valid_ref[0].astype(f32))
    grad_out = cot_ref[...].astype(f32) * valid
    grad = norm_back(grad_out, normed_two, inverse_two, gain)
    grad_ref[...] = grad
    low_ref[...] = grad.astype(bf16)
    clear_first(vec_ref)
    add_rows(vec_ref, (grad_out * normed_two, grad_out, grad, grad * grad * valid, valid))


def ffn_back_chunk(low_ref, low_first_ref, act_ref, slope_ref, w1, w2, both_ref, total_ref, hidden_ref, pre_ref):
    step = pl.program_id(0)
    both_ref[0, 0] = dot(act_ref[...], low_ref[...], 0, 0).astype(bf16)
    grad_pre = dot(low_ref[...], w2[...], 1, 1) * slope_ref[...].astype(f32)
    pre_ref[...] = grad_pre.astype(bf16)
    hidden_ref[pl.ds(step, 1), :] = jnp.sum(grad_pre, axis=0, keepdims=True)
    both_ref[1, 0] = dot(low_first_ref[...], pre_ref[...], 0, 0).astype(bf16)
    total_ref[...] += dot(pre_ref[...], w1[...], 1, 1)


def ffn_back_other_kernel(
    side, low_ref, low_first_ref, grad_ref, act_ref, slope_ref, w1, w2,
    both_ref, total_ref, hidden_ref, pre_ref,
):
    @pl.when(pl.program_id(0) == 0)
    def _():
        total_ref[...] = grad_ref[...]

    ffn_back_chunk(
        low_ref, low_first_ref, act_ref, slope_ref, w1, w2, both_ref, total_ref, hidden_ref, pre_ref
    )


def ffn_back_own_kernel(
    side, low_ref, low_first_ref, grad_ref, act_ref, slope_ref, w1, w2, mixed_ref, valid_ref, wo_a, wo_b,
    weights_ref,
    both_ref, mixed_grad_ref, low_mixed_ref, ctx_grad_ref, hidden_ref, vec_ref, total_ref, pre_ref,
):
    @pl.when(pl.program_id(0) == 0)
    def _():
        total_ref[...] = grad_ref[...]

    ffn_back_chunk(
        low_ref, low_first_ref, act_ref, slope_ref, w1, w2, both_ref, total_ref, hidden_ref, pre_ref
    )

    @pl.when(pl.program_id(0) == pl.num_programs(0) - 1)
    def _():
        vec_ref[...] = jnp.zeros_like(vec_ref)
        head_width = wo_a.shape[0]
        for at in range(0, mixed_ref.shape[0], SUB):
            here = slice(at, at + SUB)
            normed_one, inverse_one = normalise(mixed_ref[here])
            grad_first = total_ref[here]
            grad_mixed = norm_back(grad_first, normed_one, inverse_one, weights_ref[GAIN_ONE])
            mixed_grad_ref[here] = grad_mixed
            low_mixed_ref[here] = grad_mixed.astype(bf16)
            valid = as_column(valid_ref[at // SUB].astype(f32))
            add_rows(
                vec_ref,
                (
                    grad_first * normed_one,
                    grad_first,
                    grad_mixed,
                    grad_first * grad_first * valid,
                    grad_mixed * grad_mixed * valid,
                ),
            )
        ctx_grad_ref[:, :head_width] = dot(low_mixed_ref[...], wo_a[...], 1, 1).astype(bf16)
        ctx_grad_ref[:, head_width:] = dot(low_mixed_ref[...], wo_b[...], 1, 1).astype(bf16)


def attend_back_kernel(side, q_ref, k_ref, v_ref, p_ref, ctx_ref, ctx_grad_ref, out_ref, vec_ref):
    lane = lax.broadcasted_iota(jnp.int32, (1, PAIR), 1)
    for pair in range(q_ref.shape[1] // PAIR):
        here = slice(pair * PAIR, (pair + 1) * PAIR)
        masked = by_head(ctx_grad_ref[:, here], lane)
        ctx = ctx_ref[:, here].astype(f32)
        inner = jnp.sum(masked.astype(f32) * jnp.concatenate([ctx, ctx], 0), axis=-1, keepdims=True)
        probs = p_ref[0, 2 * pair : 2 * pair + 2].reshape(2 * SEQ_LEN, SEQ_LEN)
        grad_scores = (probs.astype(f32) * (dot(masked, v_ref[:, here], 1, 1) - inner)).astype(bf16)
        dq = dot(grad_scores, k_ref[:, here])
        dk = dot(by_head(q_ref[:, here], lane), grad_scores, 0, 0)
        dv = dot(masked, probs, 0, 0)
        dq = jnp.where(lane < HEAD_DIM, dq[:SEQ_LEN], dq[SEQ_LEN:]) * HEAD_DIM ** -0.5
        for at, rows in enumerate((dq, dk.T, dv.T)):
            out_ref[0, :, (3 * pair + at) * PAIR : (3 * pair + at + 1) * PAIR] = rows.astype(bf16)

    @pl.when(pl.program_id(1) == 0)
    def _():
        vec_ref[...] = jnp.zeros_like(vec_ref)

    vec_ref[0, 0:1, :] += jnp.sum(out_ref[0].astype(f32), axis=0, keepdims=True)


def attend_weights_kernel(side, three_ref, x_ref, ctx_ref, low_mixed_ref, out_ref):
    width = ctx_ref.shape[1]
    out_ref[:width] = dot(ctx_ref[...], low_mixed_ref[...], 0, 0).astype(bf16)
    out_ref[width:] = dot(three_ref[0], x_ref[...], 0, 0).astype(bf16)


def input_grad_kernel(side, mixed_grad_ref, valid_ref, *refs):
    three_ref, wq_a, wq_b, wk_a, wk_b, wv_a, wv_b, out_ref, vec_ref = refs
    grad_in = mixed_grad_ref[...]
    for half, weights in enumerate(((wq_a, wk_a, wv_a), (wq_b, wk_b, wv_b))):
        for pair in range(wq_a.shape[1] // PAIR):
            here = slice(pair * PAIR, (pair + 1) * PAIR)
            weight = jnp.concatenate([w[:, here] for w in weights], 1)
            grad_in += dot(three_ref[half, :, 3 * pair * PAIR : 3 * (pair + 1) * PAIR], weight, 1, 1)
    out_ref[...] = grad_in.astype(bf16)

    @pl.when(pl.program_id(0) == 0)
    def _():
        vec_ref[...] = jnp.zeros_like(vec_ref)

    add_rows(vec_ref, (grad_in * grad_in * as_column(valid_ref[0].astype(f32)),))


def meet_kernel(places, own, moved, *refs):
    *outs, own_rows, moved_rows, total_rows, in_sems, out_sems = refs
    count = places.shape[0] // 2
    rows = own_rows.shape[0]
    pieces = in_sems.shape[0]
    arriving = []
    for piece in range(pieces):
        here = pl.ds(piece * rows // pieces, rows // pieces)
        copies = [
            pltpu.make_async_copy(ref.at[here], held.at[here], in_sems.at[piece, which])
            for which, (ref, held) in enumerate(((own, own_rows), (moved, moved_rows)))
        ]
        for copy in copies:
            copy.start()
        arriving.append(copies)
    start, leaving = 0, []
    for part in range(2):
        half = outs[2 * part].shape[0]
        size = 2 * half // count
        for block in range(count):
            at = start + block * size
            while pieces - len(arriving) <= (at + size - 1) * pieces // rows:
                for copy in arriving.pop(0):
                    copy.wait()
            here = slice(at, at + size)
            place = pl.multiple_of(start + places[part * count + block] * size, size)
            total_rows[pl.ds(place, size)] = (own_rows[here].astype(f32) + moved_rows[here].astype(f32)).astype(bf16)
        for which in range(2):
            here = pl.ds(start + which * half, half)
            leaving.append(pltpu.make_async_copy(total_rows.at[here], outs[2 * part + which], out_sems.at[len(leaving)]))
            leaving[-1].start()
        start += count * size
    for copy in leaving:
        copy.wait()


def ordered_blocks(places, pieces):
    count = places.shape[0] // 2
    start = 0
    for part in range(2):
        low, high = pieces[2 * part], pieces[2 * part + 1]
        size = 2 * low.shape[0] // count
        for block in range(count):
            place = places[part * count + block]
            below = place < count // 2
            at = pl.multiple_of(jnp.where(below, place, 0) * size, size)
            after = pl.multiple_of(jnp.where(below, 0, place - count // 2) * size, size)
            rows = jnp.where(below, low[pl.ds(at, size)], high[pl.ds(after, size)])
            yield start + block * size, rows.astype(f32)
        start += count * size


def place_ffn_kernel(places, *refs):
    *pieces, w2_ref, w1_ref = refs
    for row, rows in ordered_blocks(places, pieces):
        size = rows.shape[0]
        if row < w2_ref.shape[0]:
            w2_ref[row : row + size] = rows
        else:
            chunk, row = divmod(row - w2_ref.shape[0], D)
            w1_ref[row : row + size, chunk * D : (chunk + 1) * D] = rows


def place_attend_kernel(places, *refs):
    *pieces, wo_ref, wq_ref, wk_ref, wv_ref, sorted_ref = refs
    for row, rows in ordered_blocks(places, pieces):
        sorted_ref[row : row + rows.shape[0]] = rows
    width = wo_ref.shape[0]
    wo_ref[...] = sorted_ref[:width]
    for pair in range(width // PAIR):
        for at, ref in enumerate((wq_ref, wk_ref, wv_ref)):
            start = width + (3 * pair + at) * PAIR
            ref[:, pair * PAIR : (pair + 1) * PAIR] = sorted_ref[start : start + PAIR].T


def run_kernel(kernel, grid, token, operands, outs, scratch=(), micros=1):
    steps = grid if isinstance(grid, tuple) else (grid,)

    def spec(block, kind):
        rest = (0,) * (len(block) - 1)
        if callable(kind):
            return pl.BlockSpec(block, kind)
        if kind == "all":
            return pl.BlockSpec(block, lambda *i: (0,) + rest, pipeline_mode=pl.Buffered(1))
        if kind == "side":
            return pl.BlockSpec(block, lambda *i: (i[-1][0],) + rest, pipeline_mode=pl.Buffered(1))
        if kind == "sum":
            return pl.BlockSpec(block, lambda *i: (0,) + rest)
        if kind == "shared":
            return pl.BlockSpec(block, lambda i, s: (s[0] * grid + i,) + rest)
        return pl.BlockSpec(block, lambda i, s: (i,) + rest)

    return pl.pallas_call(
        kernel,
        grid_spec=pltpu.PrefetchScalarGridSpec(
            num_scalar_prefetch=1,
            grid=steps,
            in_specs=[spec(block, kind) for _, block, kind in operands],
            out_specs=[spec(block, kind) for _, block, kind in outs],
            scratch_shapes=list(scratch),
        ),
        out_shape=[shape for shape, _, _ in outs],
        compiler_params=pltpu.CompilerParams(vmem_limit_bytes=VMEM_BYTES),
        cost_estimate=LIGHT,
    )(token, *[array for array, _, _ in operands])


def like(shape, dtype):
    return jax.ShapeDtypeStruct(shape, dtype)


def whole(array):
    return (array, array.shape, "all")


def swap_narrow(values):
    return lax.ppermute(values, "narrow", [(0, 1), (1, 0)])


class WideSum:
    def __init__(self, own, moved, size):
        bits = size.bit_length() - 1
        late = list(range(3, bits))
        first = [0, 1, 2][:bits]
        turned = [first[i:] + first[:i] + late for i in range(3)]
        self.size, self.bits = size, bits
        self.orders = [(turned[0], turned[1]), (turned[2], turned[2])]
        self.step = 0
        me, core = lax.axis_index("wide"), lax.axis_index("narrow")
        place = jnp.arange(size, dtype=jnp.int32)

        def gather(value, order):
            return sum(((value >> bit) & 1) << (bits - 1 - at) for at, bit in enumerate(order))

        def both(change, value):
            return jnp.concatenate([jnp.where(core == 0, *(change(value, o) for o in pair)) for pair in self.orders])

        self.places = both(gather, place ^ me)
        rows = own.shape[0]
        halves = (rows // 3, rows // 6)
        self.parts = pl.pallas_call(
            meet_kernel,
            in_specs=[pl.BlockSpec(memory_space=pltpu.SMEM)] + [pl.BlockSpec(memory_space=pl.ANY)] * 2,
            out_specs=[pl.BlockSpec(memory_space=pl.ANY)] * 4,
            out_shape=[like((half, D), bf16) for half in halves for _ in range(2)],
            scratch_shapes=[pltpu.VMEM((rows, D), bf16)] * 3
            + [pltpu.SemaphoreType.DMA((6, 2)), pltpu.SemaphoreType.DMA((4,))],
            compiler_params=pltpu.CompilerParams(vmem_limit_bytes=VMEM_BYTES),
            cost_estimate=LIGHT,
        )(self.places, own, moved)

    def start(self):
        halving = self.step < self.bits
        at = self.step if halving else 2 * self.bits - 1 - self.step
        moving = []
        for part, orders in enumerate(self.orders):
            masks = [1 << order[at] for order in orders]
            pairs = [(w * 2 + c, (w ^ masks[c]) * 2 + c) for w in range(self.size) for c in range(2)]
            moving.append(lax.ppermute(self.parts[2 * part + 1] if halving else self.parts[part], ("wide", "narrow"), pairs))
        return moving

    def finish(self, moved):
        parts = []
        for part, got in enumerate(moved):
            if self.step < self.bits:
                kept = self.parts[2 * part]
                half = kept.shape[0] // 2
                cuts = ((0, half), (half, 2 * half)) if self.step < self.bits - 1 else ((0, 2 * half),)
                parts += [(kept[a:b].astype(f32) + got[a:b].astype(f32)).astype(bf16) for a, b in cuts]
            elif self.step < 2 * self.bits - 1:
                parts.append(jnp.concatenate([self.parts[part], got], 0))
            else:
                parts += [self.parts[part], got]
        self.parts = parts
        self.step += 1

    @property
    def done(self):
        return self.step == 2 * self.bits

    def result(self, kernel, outs, scratch=()):
        return pl.pallas_call(
            kernel,
            in_specs=[pl.BlockSpec(memory_space=pltpu.SMEM)] + [pl.BlockSpec(memory_space=pltpu.VMEM)] * 4,
            out_specs=[pl.BlockSpec(memory_space=pltpu.VMEM)] * len(outs),
            out_shape=[like(shape, f32) for shape in outs],
            scratch_shapes=list(scratch),
            compiler_params=pltpu.CompilerParams(vmem_limit_bytes=VMEM_BYTES),
            cost_estimate=LIGHT,
        )(self.places, *self.parts)


class SmallSum:
    def __init__(self, values, size):
        self.parts, self.size, self.step = [values], size, 0
        self.bits = size.bit_length() - 1

    def start(self):
        return [lax.ppermute(self.parts[0], "wide", [(i, i ^ (1 << self.step)) for i in range(self.size)])]

    def finish(self, moved):
        self.parts = [self.parts[0] + moved[0]]
        self.step += 1

    @property
    def done(self):
        return self.step == self.bits


def slot(sums, compute, token):
    live = [s for s in sums if not s.done]
    parts, token = lax.optimization_barrier(([s.parts for s in live], token))
    for one, held in zip(live, parts):
        one.parts = held
    moving = [s.start() for s in live]
    outs = compute(token) if compute else ()
    moving, outs, token = lax.optimization_barrier((moving, outs, token))
    for one, moved in zip(live, moving):
        one.finish(moved)
    return outs, token


def body(size, *arrays):
    (
        inputs, segments, valid, w_query, w_key, w_value, b_query, b_value, w_attn_out, b_attn_out,
        gain_one, shift_one, w_ffn_in, b_ffn_in, w_ffn_out, b_ffn_out, gain_two, shift_two, out_grad,
    ) = arrays
    side = lax.axis_index("narrow")
    rows = inputs.shape[0] // 2
    seqs = rows // SEQ_LEN
    head_width = w_query.shape[1]
    hidden = w_ffn_in.shape[1]
    pairs = head_width // PAIR
    token = side.astype(jnp.int32).reshape(1)
    row_block = 256
    blocks = rows // row_block

    def pair_of(array):
        return (array, swap_narrow(array))

    def join_rows(array, other):
        return jnp.where(
            side == 0,
            jnp.concatenate([array, other], 0),
            jnp.concatenate([other, array], 0),
        )

    wq, wk, wv = pair_of(w_query), pair_of(w_key), pair_of(w_value)
    wo = pair_of(w_attn_out)
    def packed(pieces, length):
        total = 0.0
        for at, vector in pieces:
            total += jnp.pad(vector.astype(f32), (at, length - at - vector.shape[0]))
        return total

    own_vectors = packed([(0, b_query), (head_width, b_value), (2 * head_width, b_ffn_in)], 3 * D)
    rest = [b_attn_out, b_ffn_out, gain_one, shift_one, gain_two, shift_two]
    vectors = packed(
        [(0, own_vectors), (3 * D, swap_narrow(own_vectors))] + [((6 + at) * D, v) for at, v in enumerate(rest)], 16 * D
    ).reshape(16, D)
    _, ffn_in, ffn_out = lax.optimization_barrier(((wq, wk, wv, wo, vectors), w_ffn_in, w_ffn_out))
    w1, w2 = (w_ffn_in, swap_narrow(ffn_in)), (w_ffn_out, swap_narrow(ffn_out))
    seg_rows = segments.reshape(-1, 1, SEQ_LEN)
    valid_seq = valid.reshape(-1, 1, SEQ_LEN)
    valid_block = valid.reshape(-1, 1, row_block)
    seq = (SEQ_LEN, D)
    blk = (row_block, D)
    low_rows = like((rows, D), bf16)
    full_rows = like((rows, D), f32)
    sums_shape = (like((8, D), f32), (8, D), "sum")

    queries, keys, values, probs, context, mixed = run_kernel(
        attend_kernel,
        seqs,
        token,
        [(inputs, seq, "shared"), (seg_rows, (1, 1, SEQ_LEN), "shared"), (valid_seq, (1, 1, SEQ_LEN), "shared")]
        + [whole(w) for w in wq + wk + wv + wo]
        + [whole(vectors)],
        [(low_rows, seq, "own")] * 3
        + [(like((seqs, 4 * pairs, SEQ_LEN, SEQ_LEN), bf16), (1, 4 * pairs, SEQ_LEN, SEQ_LEN), "own")]
        + [(low_rows, seq, "own"), (full_rows, seq, "own")],
        [pltpu.VMEM((SEQ_LEN, SEQ_LEN), f32)],
        30,
    )
    chunks = hidden // D
    row_shape = (rows, D)
    hidden_rows = like((rows, 2 * hidden), bf16)
    low_first, activated, slope, final, grad_second, low_second, vec_two = run_kernel(
        ffn_kernel,
        blocks,
        token,
        [(mixed, blk, "own"), (valid_block, (1, 1, row_block), "shared"), (out_grad, blk, "shared")]
        + [whole(w) for w in w1 + w2]
        + [whole(vectors)],
        [
            (low_rows, blk, "own"),
            (hidden_rows, (row_block, 2 * hidden), "own"),
            (hidden_rows, (row_block, 2 * hidden), "own"),
            (low_rows, blk, "own"),
            (full_rows, blk, "own"),
            (low_rows, blk, "own"),
            sums_shape,
        ],
        (),
        25,
    )

    def ffn_back(kernel, half, total, extra, outs, scratch):
        return run_kernel(
            kernel,
            chunks,
            token,
            [whole(a) for a in (low_second, low_first, total)]
            + [(a, (rows, D), lambda i, s: (0, half * chunks + i)) for a in (activated, slope)]
            + [(w1[half], (D, D), lambda i, s: (0, i)), (w2[half], (D, D), lambda i, s: (i, 0))]
            + extra,
            [(like((2, chunks, D, D), bf16), (2, 1, D, D), lambda i, s: (0, i, 0, 0))] + outs,
            scratch + [pltpu.VMEM((rows, D), bf16)],
            18,
        )

    valid_part = (valid_block, (blocks, 1, row_block), "side")
    sent, total, hidden_other = ffn_back(
        ffn_back_other_kernel, 1, grad_second, [], [(full_rows, row_shape, "sum"), sums_shape], []
    )
    moved = swap_narrow(sent)
    own, grad_mixed, low_mixed, grad_context, hidden_own, vec_one = ffn_back(
        ffn_back_own_kernel,
        0,
        total,
        [whole(mixed), valid_part] + [whole(w) for w in wo] + [whole(vectors)],
        [(full_rows, row_shape, "sum"), (low_rows, row_shape, "sum"), (low_rows, row_shape, "sum"), sums_shape, sums_shape],
        [pltpu.VMEM(row_shape, f32)],
    )
    sum_ffn = WideSum(own.reshape(-1, D), moved.reshape(-1, D), size)

    def attend_back(token):
        def column(h, i, s):
            return (i, h)

        three, vec_three = run_kernel(
            attend_back_kernel,
            (2, seqs),
            token,
            [(a, (SEQ_LEN, head_width), column) for a in (queries, keys, values)]
            + [(probs, (1, 2 * pairs, SEQ_LEN, SEQ_LEN), lambda h, i, s: (i, h, 0, 0))]
            + [(a, (SEQ_LEN, head_width), column) for a in (context, grad_context)],
            [
                (like((2, rows, 3 * head_width), bf16), (1, SEQ_LEN, 3 * head_width), lambda h, i, s: (h, i, 0)),
                (like((2, 8, 3 * head_width), f32), (1, 8, 3 * head_width), lambda h, i, s: (h, 0, 0)),
            ],
            (),
            22,
        )

        return three, vec_three, weights(1, three, token)

    def weights(half, three, token):
        return run_kernel(
            attend_weights_kernel,
            1,
            token,
            [
                (three, (1, rows, 3 * head_width), lambda i, s: (half, 0, 0)),
                (inputs, row_shape, "side"),
                (context, (rows, head_width), lambda i, s: (0, half)),
                whole(low_mixed),
            ],
            [(like((4 * head_width, D), bf16), (4 * head_width, D), "sum")],
            (),
            5,
        )[0]

    (three, vec_three, sent), token = slot([sum_ffn], attend_back, token)
    (moved, own), token = slot([sum_ffn], lambda token: (swap_narrow(sent), weights(0, three, token)), token)
    sum_attn = WideSum(own, moved, size)

    def last(token):
        return tuple(
            run_kernel(
                input_grad_kernel,
                seqs,
                token,
                [(grad_mixed, seq, "own"), (valid_seq, (1, 1, SEQ_LEN), "shared")]
                + [(three, (2, SEQ_LEN, 3 * head_width), lambda i, s: (0, i, 0))]
                + [whole(w) for w in wq + wk + wv],
                [(low_rows, seq, "own"), sums_shape],
                (),
                10,
            )
        )

    (grad_in, vec_in, final_other), token = slot(
        [sum_ffn, sum_attn], lambda token: last(token) + (swap_narrow(final),), token
    )
    def arrange(own, other):
        flat = [vec_three[h, :, (3 * p + k) * PAIR : (3 * p + k + 1) * PAIR] for h in (own, other) for k in (0, 2) for p in range(pairs)]
        width = 2 * head_width
        return [
            jnp.concatenate(flat[: len(flat) // 2], 1)[:, :width],
            (hidden_own, hidden_other)[own],
        ]

    common = [vec_two, vec_one, vec_in]
    moved = swap_narrow(jnp.concatenate(common + arrange(1, 0), 0))
    small = SmallSum(jnp.concatenate(common + arrange(0, 1), 0) + moved, size)
    sums = [sum_ffn, sum_attn, small]

    def place_ffn(token):
        return tuple(sum_ffn.result(place_ffn_kernel, [(hidden, D), (D, hidden)]))

    (output, grad_other), token = slot(
        sums, lambda token: (join_rows(final, final_other), swap_narrow(grad_in)), token
    )
    (input_grad,), token = slot(sums, lambda token: (join_rows(grad_in, grad_other),), token)
    placed = None
    while not all(s.done for s in sums):
        late = sum_ffn.done and placed is None
        outs, token = slot(sums, place_ffn if late else None, token)
        placed = outs if late else placed
    d_w_out, d_w_in = placed
    small = small.parts[0]
    total = jnp.sum(jnp.stack([small[16], small[3], small[11], small[12]]), axis=1)
    rms = jnp.sqrt(total / (small[4, 0] * D))
    d_w_attn, *d_w_three = sum_attn.result(
        place_attend_kernel, [(head_width, D)] + [(D, head_width)] * 3, [pltpu.VMEM((4 * head_width, D), f32)]
    )
    return (
        output,
        input_grad,
        *d_w_three,
        small[24, :head_width],
        small[24, head_width:],
        d_w_attn,
        small[10],
        small[8],
        small[9],
        d_w_in,
        small[32 : 32 + chunks].reshape(-1),
        d_w_out,
        small[2],
        small[0],
        small[1],
        rms,
    )


def solution(mesh):
    row, col = P("narrow", None), P(None, "narrow")
    one, rows = P("narrow"), P("wide", None)
    in_specs = (
        rows, P("wide"), P("wide"), col, col, col, one, one, row, P(), P(), P(), col, one, row, P(), P(), P(), rows,
    )
    out_specs = (
        rows, rows, col, col, col, one, one, row, P(), P(), P(), col, one, row, P(), P(), P(), P(),
    )
    return jax.shard_map(
        partial(body, mesh.shape["wide"]), mesh=mesh, in_specs=in_specs, out_specs=out_specs, check_vma=False
    )
```

```python
from functools import partial

import jax
import jax.numpy as jnp
from jax import lax
from jax.experimental import pallas as pl
from jax.experimental.pallas import tpu as pltpu
from jax.sharding import PartitionSpec as P

D = 768
HEAD_DIM = 64
SEQ_LEN = 512
PAIR = 2 * HEAD_DIM
norm_eps = 1e-06
f32 = jnp.float32
bf16 = jnp.bfloat16
VMEM_BYTES = 58 << 20
LIGHT = pl.CostEstimate(flops=1 << 20, bytes_accessed=0, transcendentals=0)
B_OUT, B_FFN, GAIN_ONE, SHIFT_ONE, GAIN_TWO, SHIFT_TWO = (slice(row, row + 1) for row in range(6, 12))


def dot(left, right, left_dim=1, right_dim=0):
    return lax.dot_general(
        left, right, (((left_dim,), (right_dim,)), ((), ())), preferred_element_type=f32
    )


def normalise(values):
    centred = values - jnp.mean(values, axis=-1, keepdims=True)
    inverse = lax.rsqrt(jnp.mean(centred * centred, axis=-1, keepdims=True) + norm_eps)
    return centred * inverse, inverse


def norm_back(grad_rows, normed, inverse, gain):
    inner = grad_rows * gain
    centre_part = jnp.mean(inner, axis=-1, keepdims=True)
    slope_part = jnp.mean(inner * normed, axis=-1, keepdims=True)
    return inverse * (inner - centre_part - normed * slope_part)


def as_column(row):
    return jnp.broadcast_to(row, (8, row.shape[1])).T[:, :1]


def add_rows(ref, rows):
    for at, values in enumerate(rows):
        ref[at : at + 1, :] += jnp.sum(values, axis=0, keepdims=True)


def clear_first(ref):
    @pl.when(pl.program_id(0) == 0)
    def _():
        ref[...] = jnp.zeros_like(ref)


def by_head(rows, lane):
    return jnp.concatenate([jnp.where(lane < HEAD_DIM, rows, 0), jnp.where(lane < HEAD_DIM, 0, rows)], 0)


def gelu_both(pre):
    below = 0.5 * lax.erf(pre * 0.7071067811865476) + 0.5
    return pre * below, below + pre * (0.3989422804014327 * jnp.exp(pre * pre * -0.5))


def attend_kernel(
    side, x_ref, seg_ref, valid_ref, wq_a, wq_b, wk_a, wk_b, wv_a, wv_b, wo_a, wo_b, vec_ref,
    q_ref, k_ref, v_ref, p_ref, ctx_ref, mixed_ref, bias_ref,
):
    x = x_ref[...]
    seg = seg_ref[0].astype(f32)
    allowed = (as_column(seg) == seg) & (valid_ref[0] == 1)
    bias_ref[...] = jnp.where(allowed, 0.0, -1e30)
    width = wq_a.shape[1]
    for at, (wq, wk, wv) in enumerate(((wq_a, wk_a, wv_a), (wq_b, wk_b, wv_b))):
        here = slice(at * width, (at + 1) * width)
        q_ref[:, here] = (dot(x, wq[...]) + vec_ref[3 * at : 3 * at + 1, :width]).astype(bf16) * jnp.asarray(HEAD_DIM ** -0.5, bf16)
        k_ref[:, here] = dot(x, wk[...]).astype(bf16)
        v_ref[:, here] = (dot(x, wv[...]) + vec_ref[3 * at : 3 * at + 1, width:]).astype(bf16)

    lane = lax.broadcasted_iota(jnp.int32, (1, PAIR), 1)
    for pair in range(2 * width // PAIR):
        here = slice(pair * PAIR, (pair + 1) * PAIR)
        scores = dot(by_head(q_ref[:, here], lane), k_ref[:, here], 1, 1)
        parts = []
        for head in range(2):
            ours = scores[head * SEQ_LEN : (head + 1) * SEQ_LEN] + bias_ref[...]
            shifted = jnp.exp(ours - jnp.max(ours, axis=-1, keepdims=True))
            p_ref[0, 2 * pair + head] = (shifted * (1.0 / jnp.sum(shifted, axis=-1, keepdims=True))).astype(bf16)
        both = dot(p_ref[0, 2 * pair : 2 * pair + 2].reshape(2 * SEQ_LEN, SEQ_LEN), v_ref[:, here])
        ctx_ref[:, here] = jnp.where(lane < HEAD_DIM, both[:SEQ_LEN], both[SEQ_LEN:]).astype(bf16)
    attn = dot(ctx_ref[:, :width], wo_a[...]) + dot(ctx_ref[:, width:], wo_b[...])
    mixed_ref[...] = x.astype(f32) + attn + vec_ref[B_OUT]


SUB = 256


def ffn_kernel(
    side, mixed_ref, valid_ref, cot_ref, w1_a, w1_b, w2_a, w2_b, weights_ref,
    low_first_ref, act_ref, slope_ref, out_ref, grad_ref, low_ref, vec_ref,
):
    normed_one, _ = normalise(mixed_ref[...])
    first = normed_one * weights_ref[GAIN_ONE] + weights_ref[SHIFT_ONE]
    low_first = first.astype(bf16)
    low_first_ref[...] = low_first
    second = first + weights_ref[B_FFN]
    width = w1_a.shape[1]
    step = 256
    for half, (w1, w2) in enumerate(((w1_a, w2_a), (w1_b, w2_b))):
        for at in range(0, width, step):
            here = slice(half * width + at, half * width + at + step)
            pre = dot(low_first, w1[:, at : at + step]) + weights_ref[3 * half + 1 + at // D : 3 * half + 2 + at // D, at % D : at % D + step]
            act, slope = gelu_both(pre)
            act = act.astype(bf16)
            act_ref[:, here] = act
            slope_ref[:, here] = slope.astype(bf16)
            second += dot(act, w2[at : at + step, :])
    normed_two, inverse_two = normalise(second)
    gain = weights_ref[GAIN_TWO]
    out_ref[...] = (normed_two * gain + weights_ref[SHIFT_TWO]).astype(bf16)
    valid = as_column(valid_ref[0].astype(f32))
    grad_out = cot_ref[...].astype(f32) * valid
    grad = norm_back(grad_out, normed_two, inverse_two, gain)
    grad_ref[...] = grad
    low_ref[...] = grad.astype(bf16)
    clear_first(vec_ref)
    add_rows(vec_ref, (grad_out * normed_two, grad_out, grad, grad * grad * valid, valid))


def ffn_back_chunk(low_ref, low_first_ref, act_ref, slope_ref, w1, w2, both_ref, total_ref, hidden_ref, pre_ref):
    step = pl.program_id(0)
    both_ref[0, 0] = dot(act_ref[...], low_ref[...], 0, 0).astype(bf16)
    grad_pre = dot(low_ref[...], w2[...], 1, 1) * slope_ref[...].astype(f32)
    pre_ref[...] = grad_pre.astype(bf16)
    hidden_ref[pl.ds(step, 1), :] = jnp.sum(grad_pre, axis=0, keepdims=True)
    both_ref[1, 0] = dot(low_first_ref[...], pre_ref[...], 0, 0).astype(bf16)

    @pl.when(step == 0)
    def _():
        total_ref[...] = dot(pre_ref[...], w1[...], 1, 1)

    @pl.when(step > 0)
    def _():
        total_ref[...] += dot(pre_ref[...], w1[...], 1, 1)


def ffn_back_other_kernel(
    side, low_ref, low_first_ref, act_ref, slope_ref, w1, w2, both_ref, total_ref, hidden_ref, pre_ref
):
    ffn_back_chunk(low_ref, low_first_ref, act_ref, slope_ref, w1, w2, both_ref, total_ref, hidden_ref, pre_ref)


def ffn_back_own_kernel(
    side, low_ref, low_first_ref, act_ref, slope_ref, w1, w2, valid_ref, weights_ref, *refs
):
    late, refs = refs[:5], refs[5:]
    both_ref, mixed_grad_ref, low_mixed_ref, ctx_grad_ref, hidden_ref, vec_ref, total_ref, pre_ref = refs[:8]
    here_refs, sems = refs[8:13], refs[13]
    copies = [pltpu.make_async_copy(ref, here, sems.at[at]) for at, (ref, here) in enumerate(zip(late, here_refs))]

    @pl.when(pl.program_id(0) == 0)
    def _():
        for copy in copies:
            copy.start()

    ffn_back_chunk(low_ref, low_first_ref, act_ref, slope_ref, w1, w2, both_ref, total_ref, hidden_ref, pre_ref)

    @pl.when(pl.program_id(0) == pl.num_programs(0) - 1)
    def _():
        for copy in copies:
            copy.wait()
        grad_second_ref, other_ref, mixed_ref, wo_a, wo_b = here_refs
        vec_ref[...] = jnp.zeros_like(vec_ref)
        head_width = wo_a.shape[0]
        for at in range(0, mixed_ref.shape[0], SUB):
            here = slice(at, at + SUB)
            normed_one, inverse_one = normalise(mixed_ref[here])
            grad_first = total_ref[here] + other_ref[here] + grad_second_ref[here]
            grad_mixed = norm_back(grad_first, normed_one, inverse_one, weights_ref[GAIN_ONE])
            mixed_grad_ref[here] = grad_mixed
            low_mixed_ref[here] = grad_mixed.astype(bf16)
            valid = as_column(valid_ref[at // SUB].astype(f32))
            add_rows(
                vec_ref,
                (
                    grad_first * normed_one,
                    grad_first,
                    grad_mixed,
                    grad_first * grad_first * valid,
                    grad_mixed * grad_mixed * valid,
                ),
            )
        ctx_grad_ref[:, :head_width] = dot(low_mixed_ref[...], wo_a[...], 1, 1).astype(bf16)
        ctx_grad_ref[:, head_width:] = dot(low_mixed_ref[...], wo_b[...], 1, 1).astype(bf16)


def attend_back_kernel(
    side, q_ref, k_ref, v_ref, p_ref, ctx_ref, ctx_grad_ref, x_ref, low_mixed_ref, out_ref, vec_ref, other_ref, sum_ref
):
    lane = lax.broadcasted_iota(jnp.int32, (1, PAIR), 1)
    for pair in range(q_ref.shape[1] // PAIR):
        here = slice(pair * PAIR, (pair + 1) * PAIR)
        masked = by_head(ctx_grad_ref[:, here], lane)
        ctx = ctx_ref[:, here].astype(f32)
        inner = jnp.sum(masked.astype(f32) * jnp.concatenate([ctx, ctx], 0), axis=-1, keepdims=True)
        probs = p_ref[0, 2 * pair : 2 * pair + 2].reshape(2 * SEQ_LEN, SEQ_LEN)
        grad_scores = (probs.astype(f32) * (dot(masked, v_ref[:, here], 1, 1) - inner)).astype(bf16)
        dq = dot(grad_scores, k_ref[:, here])
        dk = dot(by_head(q_ref[:, here], lane), grad_scores, 0, 0)
        dv = dot(masked, probs, 0, 0)
        dq = jnp.where(lane < HEAD_DIM, dq[:SEQ_LEN], dq[SEQ_LEN:]) * HEAD_DIM ** -0.5
        for at, rows in enumerate((dq, dk.T, dv.T)):
            out_ref[0, :, (3 * pair + at) * PAIR : (3 * pair + at + 1) * PAIR] = rows.astype(bf16)

    @pl.when(pl.program_id(1) == 0)
    def _():
        vec_ref[...] = jnp.zeros_like(vec_ref)

    width = ctx_ref.shape[1]
    other = pl.program_id(0) == 0
    last = pl.program_id(1) == pl.num_programs(1) - 1

    @pl.when(other & (pl.program_id(1) == 0))
    def _():
        sum_ref[:width] = dot(ctx_ref[...], low_mixed_ref[...], 0, 0)
        sum_ref[width:] = dot(out_ref[0], x_ref[...], 0, 0)

    @pl.when(other & (pl.program_id(1) > 0))
    def _():
        sum_ref[:width] += dot(ctx_ref[...], low_mixed_ref[...], 0, 0)
        sum_ref[width:] += dot(out_ref[0], x_ref[...], 0, 0)

    @pl.when(other & last)
    def _():
        other_ref[...] = sum_ref[...].astype(bf16)

    vec_ref[0, 0:1, :] += jnp.sum(out_ref[0].astype(f32), axis=0, keepdims=True)


def attend_weights_kernel(side, three_ref, x_ref, ctx_ref, low_mixed_ref, out_ref):
    width = ctx_ref.shape[1]
    out_ref[:width] = dot(ctx_ref[...], low_mixed_ref[...], 0, 0).astype(bf16)
    out_ref[width:] = dot(three_ref[0], x_ref[...], 0, 0).astype(bf16)


def input_grad_kernel(side, mixed_grad_ref, valid_ref, *refs):
    three_ref, wq_a, wq_b, wk_a, wk_b, wv_a, wv_b, out_ref, vec_ref = refs
    grad_in = mixed_grad_ref[...]
    for half, weights in enumerate(((wq_a, wk_a, wv_a), (wq_b, wk_b, wv_b))):
        for pair in range(wq_a.shape[1] // PAIR):
            here = slice(pair * PAIR, (pair + 1) * PAIR)
            weight = jnp.concatenate([w[:, here] for w in weights], 1)
            grad_in += dot(three_ref[half, :, 3 * pair * PAIR : 3 * (pair + 1) * PAIR], weight, 1, 1)
    out_ref[...] = grad_in.astype(bf16)

    @pl.when(pl.program_id(0) == 0)
    def _():
        vec_ref[...] = jnp.zeros_like(vec_ref)

    add_rows(vec_ref, (grad_in * grad_in * as_column(valid_ref[0].astype(f32)),))


def meet_kernel(places, own, moved, *refs):
    *outs, own_rows, moved_rows, total_rows, in_sems, out_sems = refs
    count = places.shape[0] // 2
    rows = own_rows.shape[0]
    pieces = in_sems.shape[0]
    arriving = []
    for piece in range(pieces):
        here = pl.ds(piece * rows // pieces, rows // pieces)
        copies = [
            pltpu.make_async_copy(ref.at[here], held.at[here], in_sems.at[piece, which])
            for which, (ref, held) in enumerate(((own, own_rows), (moved, moved_rows)))
        ]
        for copy in copies:
            copy.start()
        arriving.append(copies)
    start, leaving = 0, []
    for part in range(2):
        half = outs[2 * part].shape[0]
        size = 2 * half // count
        for block in range(count):
            at = start + block * size
            while pieces - len(arriving) <= (at + size - 1) * pieces // rows:
                for copy in arriving.pop(0):
                    copy.wait()
            here = slice(at, at + size)
            place = pl.multiple_of(start + places[part * count + block] * size, size)
            total_rows[pl.ds(place, size)] = (own_rows[here].astype(f32) + moved_rows[here].astype(f32)).astype(bf16)
        for which in range(2):
            here = pl.ds(start + which * half, half)
            leaving.append(pltpu.make_async_copy(total_rows.at[here], outs[2 * part + which], out_sems.at[len(leaving)]))
            leaving[-1].start()
        start += count * size
    for copy in leaving:
        copy.wait()


def ordered_blocks(places, pieces):
    count = places.shape[0] // 2
    start = 0
    for part in range(2):
        low, high = pieces[2 * part], pieces[2 * part + 1]
        size = 2 * low.shape[0] // count
        for block in range(count):
            place = places[part * count + block]
            below = place < count // 2
            at = pl.multiple_of(jnp.where(below, place, 0) * size, size)
            after = pl.multiple_of(jnp.where(below, 0, place - count // 2) * size, size)
            rows = jnp.where(below, low[pl.ds(at, size)], high[pl.ds(after, size)])
            yield start + block * size, rows.astype(f32)
        start += count * size


def place_ffn_kernel(places, *refs):
    *pieces, w2_ref, w1_ref = refs
    for row, rows in ordered_blocks(places, pieces):
        size = rows.shape[0]
        if row < w2_ref.shape[0]:
            w2_ref[row : row + size] = rows
        else:
            chunk, row = divmod(row - w2_ref.shape[0], D)
            w1_ref[row : row + size, chunk * D : (chunk + 1) * D] = rows


def place_attend_kernel(places, *refs):
    *pieces, wo_ref, wq_ref, wk_ref, wv_ref, sorted_ref = refs
    for row, rows in ordered_blocks(places, pieces):
        sorted_ref[row : row + rows.shape[0]] = rows
    width = wo_ref.shape[0]
    wo_ref[...] = sorted_ref[:width]
    for pair in range(width // PAIR):
        for at, ref in enumerate((wq_ref, wk_ref, wv_ref)):
            start = width + (3 * pair + at) * PAIR
            ref[:, pair * PAIR : (pair + 1) * PAIR] = sorted_ref[start : start + PAIR].T


def run_kernel(kernel, grid, token, operands, outs, scratch=()):
    steps = grid if isinstance(grid, tuple) else (grid,)

    def spec(block, kind):
        rest = (0,) * (len(block) - 1)
        if kind == "late":
            return pl.BlockSpec(memory_space=pl.ANY)
        if callable(kind):
            return pl.BlockSpec(block, kind)
        if kind == "all":
            return pl.BlockSpec(block, lambda *i: (0,) + rest, pipeline_mode=pl.Buffered(1))
        if kind == "side":
            return pl.BlockSpec(block, lambda *i: (i[-1][0],) + rest, pipeline_mode=pl.Buffered(1))
        if kind == "sum":
            return pl.BlockSpec(block, lambda *i: (0,) + rest)
        if kind == "shared":
            return pl.BlockSpec(block, lambda i, s: (s[0] * grid + i,) + rest)
        return pl.BlockSpec(block, lambda i, s: (i,) + rest)

    return pl.pallas_call(
        kernel,
        grid_spec=pltpu.PrefetchScalarGridSpec(
            num_scalar_prefetch=1,
            grid=steps,
            in_specs=[spec(block, kind) for _, block, kind in operands],
            out_specs=[spec(block, kind) for _, block, kind in outs],
            scratch_shapes=list(scratch),
        ),
        out_shape=[shape for shape, _, _ in outs],
        compiler_params=pltpu.CompilerParams(vmem_limit_bytes=VMEM_BYTES),
        cost_estimate=LIGHT,
    )(token, *[array for array, _, _ in operands])


def like(shape, dtype):
    return jax.ShapeDtypeStruct(shape, dtype)


def whole(array):
    return (array, array.shape, "all")


def swap_narrow(values):
    return lax.ppermute(values, "narrow", [(0, 1), (1, 0)])


class WideSum:
    def __init__(self, own, moved, size):
        bits = size.bit_length() - 1
        late = list(range(3, bits))
        first = [0, 1, 2][:bits]
        turned = [first[i:] + first[:i] + late for i in range(3)]
        self.size, self.bits = size, bits
        self.orders = [(turned[0], turned[1]), (turned[2], turned[2])]
        self.step = 0
        me, core = lax.axis_index("wide"), lax.axis_index("narrow")
        place = jnp.arange(size, dtype=jnp.int32)

        def gather(value, order):
            return sum(((value >> bit) & 1) << (bits - 1 - at) for at, bit in enumerate(order))

        def both(change, value):
            return jnp.concatenate([jnp.where(core == 0, *(change(value, o) for o in pair)) for pair in self.orders])

        self.places = both(gather, place ^ me)
        rows = own.shape[0]
        halves = (rows // 3, rows // 6)
        self.parts = pl.pallas_call(
            meet_kernel,
            in_specs=[pl.BlockSpec(memory_space=pltpu.SMEM)] + [pl.BlockSpec(memory_space=pl.ANY)] * 2,
            out_specs=[pl.BlockSpec(memory_space=pl.ANY)] * 4,
            out_shape=[like((half, D), bf16) for half in halves for _ in range(2)],
            scratch_shapes=[pltpu.VMEM((rows, D), bf16)] * 3
            + [pltpu.SemaphoreType.DMA((6, 2)), pltpu.SemaphoreType.DMA((4,))],
            compiler_params=pltpu.CompilerParams(vmem_limit_bytes=VMEM_BYTES),
            cost_estimate=LIGHT,
        )(self.places, own, moved)

    def start(self):
        halving = self.step < self.bits
        at = self.step if halving else 2 * self.bits - 1 - self.step
        moving = []
        for part, orders in enumerate(self.orders):
            masks = [1 << order[at] for order in orders]
            pairs = [(w * 2 + c, (w ^ masks[c]) * 2 + c) for w in range(self.size) for c in range(2)]
            moving.append(lax.ppermute(self.parts[2 * part + 1] if halving else self.parts[part], ("wide", "narrow"), pairs))
        return moving

    def finish(self, moved):
        parts = []
        for part, got in enumerate(moved):
            if self.step < self.bits:
                kept = self.parts[2 * part]
                half = kept.shape[0] // 2
                cuts = ((0, half), (half, 2 * half)) if self.step < self.bits - 1 else ((0, 2 * half),)
                parts += [(kept[a:b].astype(f32) + got[a:b].astype(f32)).astype(bf16) for a, b in cuts]
            elif self.step < 2 * self.bits - 1:
                parts.append(jnp.concatenate([self.parts[part], got], 0))
            else:
                parts += [self.parts[part], got]
        self.parts = parts
        self.step += 1

    @property
    def done(self):
        return self.step == 2 * self.bits

    def result(self, kernel, outs, scratch=()):
        return pl.pallas_call(
            kernel,
            in_specs=[pl.BlockSpec(memory_space=pltpu.SMEM)] + [pl.BlockSpec(memory_space=pltpu.VMEM)] * 4,
            out_specs=[pl.BlockSpec(memory_space=pltpu.VMEM)] * len(outs),
            out_shape=[like(shape, f32) for shape in outs],
            scratch_shapes=list(scratch),
            compiler_params=pltpu.CompilerParams(vmem_limit_bytes=VMEM_BYTES),
            cost_estimate=LIGHT,
        )(self.places, *self.parts)


class SmallSum:
    def __init__(self, values, size):
        self.parts, self.size, self.step = [values], size, 0
        self.bits = size.bit_length() - 1

    def start(self):
        return [lax.ppermute(self.parts[0], "wide", [(i, i ^ (1 << self.step)) for i in range(self.size)])]

    def finish(self, moved):
        self.parts = [self.parts[0] + moved[0]]
        self.step += 1

    @property
    def done(self):
        return self.step == self.bits


def slot(sums, compute, token):
    live = [s for s in sums if not s.done]
    parts, token = lax.optimization_barrier(([s.parts for s in live], token))
    for one, held in zip(live, parts):
        one.parts = held
    moving = [s.start() for s in live]
    outs = compute(token) if compute else ()
    moving, outs, token = lax.optimization_barrier((moving, outs, token))
    for one, moved in zip(live, moving):
        one.finish(moved)
    return outs, token


def body(size, *arrays):
    (
        inputs, segments, valid, w_query, w_key, w_value, b_query, b_value, w_attn_out, b_attn_out,
        gain_one, shift_one, w_ffn_in, b_ffn_in, w_ffn_out, b_ffn_out, gain_two, shift_two, out_grad,
    ) = arrays
    side = lax.axis_index("narrow")
    rows = inputs.shape[0] // 2
    seqs = rows // SEQ_LEN
    head_width = w_query.shape[1]
    hidden = w_ffn_in.shape[1]
    pairs = head_width // PAIR
    token = side.astype(jnp.int32).reshape(1)
    row_block = 256
    blocks = rows // row_block

    def pair_of(array):
        return (array, swap_narrow(array))

    def join_rows(array, other):
        return jnp.where(
            side == 0,
            jnp.concatenate([array, other], 0),
            jnp.concatenate([other, array], 0),
        )

    wq, wk, wv = pair_of(w_query), pair_of(w_key), pair_of(w_value)
    wo = pair_of(w_attn_out)
    def packed(pieces, length):
        total = 0.0
        for at, vector in pieces:
            total += jnp.pad(vector.astype(f32), (at, length - at - vector.shape[0]))
        return total

    own_vectors = packed([(0, b_query), (head_width, b_value), (2 * head_width, b_ffn_in)], 3 * D)
    rest = [b_attn_out, b_ffn_out, gain_one, shift_one, gain_two, shift_two]
    vectors = packed(
        [(0, own_vectors), (3 * D, swap_narrow(own_vectors))] + [((6 + at) * D, v) for at, v in enumerate(rest)], 16 * D
    ).reshape(16, D)
    _, ffn_in, ffn_out = lax.optimization_barrier(((wq, wk, wv, wo, vectors), w_ffn_in, w_ffn_out))
    w1, w2 = (w_ffn_in, swap_narrow(ffn_in)), (w_ffn_out, swap_narrow(ffn_out))
    seg_rows = segments.reshape(-1, 1, SEQ_LEN)
    valid_seq = valid.reshape(-1, 1, SEQ_LEN)
    valid_block = valid.reshape(-1, 1, row_block)
    seq = (SEQ_LEN, D)
    blk = (row_block, D)
    low_rows = like((rows, D), bf16)
    full_rows = like((rows, D), f32)
    sums_shape = (like((8, D), f32), (8, D), "sum")

    queries, keys, values, probs, context, mixed = run_kernel(
        attend_kernel,
        seqs,
        token,
        [(inputs, seq, "shared"), (seg_rows, (1, 1, SEQ_LEN), "shared"), (valid_seq, (1, 1, SEQ_LEN), "shared")]
        + [whole(w) for w in wq + wk + wv + wo]
        + [whole(vectors)],
        [(low_rows, seq, "own")] * 3
        + [(like((seqs, 4 * pairs, SEQ_LEN, SEQ_LEN), bf16), (1, 4 * pairs, SEQ_LEN, SEQ_LEN), "own")]
        + [(low_rows, seq, "own"), (full_rows, seq, "own")],
        [pltpu.VMEM((SEQ_LEN, SEQ_LEN), f32)],
    )
    chunks = hidden // D
    row_shape = (rows, D)
    hidden_rows = like((rows, 2 * hidden), bf16)
    low_first, activated, slope, final, grad_second, low_second, vec_two = run_kernel(
        ffn_kernel,
        blocks,
        token,
        [(mixed, blk, "own"), (valid_block, (1, 1, row_block), "shared"), (out_grad, blk, "shared")]
        + [whole(w) for w in w1 + w2]
        + [whole(vectors)],
        [
            (low_rows, blk, "own"),
            (hidden_rows, (row_block, 2 * hidden), "own"),
            (hidden_rows, (row_block, 2 * hidden), "own"),
            (low_rows, blk, "own"),
            (full_rows, blk, "own"),
            (low_rows, blk, "own"),
            sums_shape,
        ],
        (),
    )

    def ffn_back(kernel, half, extra, outs, scratch, late=()):
        return run_kernel(
            kernel,
            chunks,
            token,
            [whole(a) for a in (low_second, low_first)]
            + [(a, (rows, D), lambda i, s: (0, half * chunks + i)) for a in (activated, slope)]
            + [(w1[half], (D, D), lambda i, s: (0, i)), (w2[half], (D, D), lambda i, s: (i, 0))]
            + extra
            + [(a, a.shape, "late") for a in late],
            [(like((2, chunks, D, D), bf16), (2, 1, D, D), lambda i, s: (0, i, 0, 0))] + outs,
            scratch
            + [pltpu.VMEM(row_shape, bf16)]
            + [pltpu.VMEM(a.shape, a.dtype) for a in late]
            + [pltpu.SemaphoreType.DMA((len(late),)) for _ in late[:1]],
        )

    valid_part = (valid_block, (blocks, 1, row_block), "side")
    sent, total, hidden_other = ffn_back(
        ffn_back_other_kernel, 1, [], [(full_rows, row_shape, "sum"), sums_shape], []
    )
    moved = swap_narrow(sent)
    own, grad_mixed, low_mixed, grad_context, hidden_own, vec_one = ffn_back(
        ffn_back_own_kernel,
        0,
        [valid_part, whole(vectors)],
        [(full_rows, row_shape, "sum"), (low_rows, row_shape, "sum"), (low_rows, row_shape, "sum"), sums_shape, sums_shape],
        [pltpu.VMEM(row_shape, f32)],
        (grad_second, total, mixed) + wo,
    )
    sum_ffn = WideSum(own.reshape(-1, D), moved.reshape(-1, D), size)

    def attend_back(token):
        def column(h, i, s):
            return (i, 1 - h)

        half_weights = like((4 * head_width, D), bf16)
        return tuple(
            run_kernel(
                attend_back_kernel,
                (2, seqs),
                token,
                [(a, (SEQ_LEN, head_width), column) for a in (queries, keys, values)]
                + [(probs, (1, 2 * pairs, SEQ_LEN, SEQ_LEN), lambda h, i, s: (i, 1 - h, 0, 0))]
                + [(a, (SEQ_LEN, head_width), column) for a in (context, grad_context)]
                + [(inputs, seq, lambda h, i, s: (s[0] * seqs + i, 0)), (low_mixed, seq, lambda h, i, s: (i, 0))],
                [
                    (
                        like((2, rows, 3 * head_width), bf16),
                        (1, SEQ_LEN, 3 * head_width),
                        lambda h, i, s: (1 - h, i, 0),
                    ),
                    (like((2, 8, 3 * head_width), f32), (1, 8, 3 * head_width), lambda h, i, s: (1 - h, 0, 0)),
                    (half_weights, half_weights.shape, "sum"),
                ],
                [pltpu.VMEM(half_weights.shape, f32)],
            )
        )

    def own_weights(token):
        return run_kernel(
            attend_weights_kernel,
            1,
            token,
            [
                (three, (1, rows, 3 * head_width), lambda i, s: (0, 0, 0)),
                (inputs, row_shape, "side"),
                (context, (rows, head_width), lambda i, s: (0, 0)),
                whole(low_mixed),
            ],
            [(like((4 * head_width, D), bf16), (4 * head_width, D), "sum")],
        )[0]

    (three, vec_three, sent), token = slot([sum_ffn], attend_back, token)
    (moved, own), token = slot([sum_ffn], lambda token: (swap_narrow(sent), own_weights(token)), token)
    sum_attn = WideSum(own, moved, size)

    def last(token):
        return tuple(
            run_kernel(
                input_grad_kernel,
                seqs,
                token,
                [(grad_mixed, seq, "own"), (valid_seq, (1, 1, SEQ_LEN), "shared")]
                + [(three, (2, SEQ_LEN, 3 * head_width), lambda i, s: (0, i, 0))]
                + [whole(w) for w in wq + wk + wv],
                [(low_rows, seq, "own"), sums_shape],
                (),
            )
        )

    (grad_in, vec_in, final_other), token = slot(
        [sum_ffn, sum_attn], lambda token: last(token) + (swap_narrow(final),), token
    )
    def arrange(own, other):
        flat = [vec_three[h, :, (3 * p + k) * PAIR : (3 * p + k + 1) * PAIR] for h in (own, other) for k in (0, 2) for p in range(pairs)]
        width = 2 * head_width
        return [
            jnp.concatenate(flat[: len(flat) // 2], 1)[:, :width],
            (hidden_own, hidden_other)[own],
        ]

    common = [vec_two, vec_one, vec_in]
    moved = swap_narrow(jnp.concatenate(common + arrange(1, 0), 0))
    small = SmallSum(jnp.concatenate(common + arrange(0, 1), 0) + moved, size)
    sums = [sum_ffn, sum_attn, small]

    def place_ffn(token):
        return tuple(sum_ffn.result(place_ffn_kernel, [(hidden, D), (D, hidden)]))

    (output, grad_other), token = slot(
        sums, lambda token: (join_rows(final, final_other), swap_narrow(grad_in)), token
    )
    (input_grad,), token = slot(sums, lambda token: (join_rows(grad_in, grad_other),), token)
    placed = None
    while not all(s.done for s in sums):
        late = sum_ffn.done and placed is None
        outs, token = slot(sums, place_ffn if late else None, token)
        placed = outs if late else placed
    d_w_out, d_w_in = placed
    small = small.parts[0]
    total = jnp.sum(jnp.stack([small[16], small[3], small[11], small[12]]), axis=1)
    rms = jnp.sqrt(total / (small[4, 0] * D))
    d_w_attn, *d_w_three = sum_attn.result(
        place_attend_kernel, [(head_width, D)] + [(D, head_width)] * 3, [pltpu.VMEM((4 * head_width, D), f32)]
    )
    return (
        output,
        input_grad,
        *d_w_three,
        small[24, :head_width],
        small[24, head_width:],
        d_w_attn,
        small[10],
        small[8],
        small[9],
        d_w_in,
        small[32 : 32 + chunks].reshape(-1),
        d_w_out,
        small[2],
        small[0],
        small[1],
        rms,
    )


def solution(mesh):
    row, col = P("narrow", None), P(None, "narrow")
    one, rows = P("narrow"), P("wide", None)
    in_specs = (
        rows, P("wide"), P("wide"), col, col, col, one, one, row, P(), P(), P(), col, one, row, P(), P(), P(), rows,
    )
    out_specs = (
        rows, rows, col, col, col, one, one, row, P(), P(), P(), col, one, row, P(), P(), P(), P(),
    )
    return jax.shard_map(
        partial(body, mesh.shape["wide"]), mesh=mesh, in_specs=in_specs, out_specs=out_specs, check_vma=False
    )
```

```python
from functools import partial

import jax
import jax.numpy as jnp
from jax import lax
from jax.experimental import pallas as pl
from jax.experimental.pallas import tpu as pltpu
from jax.sharding import PartitionSpec as P

D = 768
HEAD_DIM = 64
SEQ_LEN = 512
PAIR = 2 * HEAD_DIM
norm_eps = 1e-06
f32 = jnp.float32
bf16 = jnp.bfloat16
VMEM_BYTES = 58 << 20
LIGHT = pl.CostEstimate(flops=1 << 20, bytes_accessed=0, transcendentals=0)
B_OUT, B_FFN, GAIN_ONE, SHIFT_ONE, GAIN_TWO, SHIFT_TWO = (slice(row, row + 1) for row in range(6, 12))


def dot(left, right, left_dim=1, right_dim=0):
    return lax.dot_general(
        left, right, (((left_dim,), (right_dim,)), ((), ())), preferred_element_type=f32
    )


def normalise(values):
    centred = values - jnp.mean(values, axis=-1, keepdims=True)
    inverse = lax.rsqrt(jnp.mean(centred * centred, axis=-1, keepdims=True) + norm_eps)
    return centred * inverse, inverse


def norm_back(grad_rows, normed, inverse, gain):
    inner = grad_rows * gain
    centre_part = jnp.mean(inner, axis=-1, keepdims=True)
    slope_part = jnp.mean(inner * normed, axis=-1, keepdims=True)
    return inverse * (inner - centre_part - normed * slope_part)


def as_column(row):
    return jnp.broadcast_to(row, (8, row.shape[1])).T[:, :1]


def add_rows(ref, rows):
    for at, values in enumerate(rows):
        ref[at : at + 1, :] += jnp.sum(values, axis=0, keepdims=True)


def clear_first(ref):
    @pl.when(pl.program_id(0) == 0)
    def _():
        ref[...] = jnp.zeros_like(ref)


def by_head(rows, lane):
    return jnp.concatenate([jnp.where(lane < HEAD_DIM, rows, 0), jnp.where(lane < HEAD_DIM, 0, rows)], 0)


def gelu_both(pre):
    below = 0.5 * lax.erf(pre * 0.7071067811865476) + 0.5
    return pre * below, below + pre * (0.3989422804014327 * jnp.exp(pre * pre * -0.5))


def attend_kernel(
    side, x_ref, seg_ref, valid_ref, wq_a, wq_b, wk_a, wk_b, wv_a, wv_b, wo_a, wo_b, vec_ref,
    q_ref, k_ref, v_ref, p_ref, ctx_ref, mixed_ref, bias_ref,
):
    x = x_ref[...]
    seg = seg_ref[0].astype(f32)
    allowed = (as_column(seg) == seg) & (valid_ref[0] == 1)
    bias_ref[...] = jnp.where(allowed, 0.0, -1e30)
    width = wq_a.shape[1]
    for at, (wq, wk, wv) in enumerate(((wq_a, wk_a, wv_a), (wq_b, wk_b, wv_b))):
        here = slice(at * width, (at + 1) * width)
        q_ref[:, here] = (dot(x, wq[...]) + vec_ref[3 * at : 3 * at + 1, :width]).astype(bf16) * jnp.asarray(HEAD_DIM ** -0.5, bf16)
        k_ref[:, here] = dot(x, wk[...]).astype(bf16)
        v_ref[:, here] = (dot(x, wv[...]) + vec_ref[3 * at : 3 * at + 1, width:]).astype(bf16)

    lane = lax.broadcasted_iota(jnp.int32, (1, PAIR), 1)
    for pair in range(2 * width // PAIR):
        here = slice(pair * PAIR, (pair + 1) * PAIR)
        scores = dot(by_head(q_ref[:, here], lane), k_ref[:, here], 1, 1)
        parts = []
        for head in range(2):
            ours = scores[head * SEQ_LEN : (head + 1) * SEQ_LEN] + bias_ref[...]
            shifted = jnp.exp(ours - jnp.max(ours, axis=-1, keepdims=True))
            p_ref[0, 2 * pair + head] = (shifted * (1.0 / jnp.sum(shifted, axis=-1, keepdims=True))).astype(bf16)
        both = dot(p_ref[0, 2 * pair : 2 * pair + 2].reshape(2 * SEQ_LEN, SEQ_LEN), v_ref[:, here])
        ctx_ref[:, here] = jnp.where(lane < HEAD_DIM, both[:SEQ_LEN], both[SEQ_LEN:]).astype(bf16)
    attn = dot(ctx_ref[:, :width], wo_a[...]) + dot(ctx_ref[:, width:], wo_b[...])
    mixed_ref[...] = x.astype(f32) + attn + vec_ref[B_OUT]


SUB = 256


def ffn_kernel(
    side, mixed_ref, valid_ref, cot_ref, w1_a, w1_b, w2_a, w2_b, weights_ref,
    low_first_ref, act_ref, slope_ref, out_ref, grad_ref, low_ref, vec_ref,
):
    normed_one, _ = normalise(mixed_ref[...])
    first = normed_one * weights_ref[GAIN_ONE] + weights_ref[SHIFT_ONE]
    low_first = first.astype(bf16)
    low_first_ref[...] = low_first
    second = first + weights_ref[B_FFN]
    width = w1_a.shape[1]
    step = 256
    for half, (w1, w2) in enumerate(((w1_a, w2_a), (w1_b, w2_b))):
        for at in range(0, width, step):
            here = slice(half * width + at, half * width + at + step)
            pre = dot(low_first, w1[:, at : at + step]) + weights_ref[3 * half + 1 + at // D : 3 * half + 2 + at // D, at % D : at % D + step]
            act, slope = gelu_both(pre)
            act = act.astype(bf16)
            act_ref[:, here] = act
            slope_ref[:, here] = slope.astype(bf16)
            second += dot(act, w2[at : at + step, :])
    normed_two, inverse_two = normalise(second)
    gain = weights_ref[GAIN_TWO]
    out_ref[...] = (normed_two * gain + weights_ref[SHIFT_TWO]).astype(bf16)
    valid = as_column(valid_ref[0].astype(f32))
    grad_out = cot_ref[...].astype(f32) * valid
    grad = norm_back(grad_out, normed_two, inverse_two, gain)
    grad_ref[...] = grad
    low_ref[...] = grad.astype(bf16)
    clear_first(vec_ref)
    add_rows(vec_ref, (grad_out * normed_two, grad_out, grad, grad * grad * valid, valid))


def ffn_back_chunk(low_ref, low_first_ref, act_ref, slope_ref, w1, w2, both_ref, total_ref, hidden_ref, pre_ref):
    step = pl.program_id(0)
    both_ref[0, 0] = dot(act_ref[...], low_ref[...], 0, 0).astype(bf16)
    grad_pre = dot(low_ref[...], w2[...], 1, 1) * slope_ref[...].astype(f32)
    pre_ref[...] = grad_pre.astype(bf16)
    hidden_ref[pl.ds(step, 1), :] = jnp.sum(grad_pre, axis=0, keepdims=True)
    both_ref[1, 0] = dot(low_first_ref[...], pre_ref[...], 0, 0).astype(bf16)

    @pl.when(step == 0)
    def _():
        total_ref[...] = dot(pre_ref[...], w1[...], 1, 1)

    @pl.when(step > 0)
    def _():
        total_ref[...] += dot(pre_ref[...], w1[...], 1, 1)


def ffn_back_other_kernel(
    side, low_ref, low_first_ref, act_ref, slope_ref, w1, w2, both_ref, total_ref, hidden_ref, pre_ref
):
    ffn_back_chunk(low_ref, low_first_ref, act_ref, slope_ref, w1, w2, both_ref, total_ref, hidden_ref, pre_ref)


def ffn_back_own_kernel(
    side, low_ref, low_first_ref, act_ref, slope_ref, w1, w2, valid_ref, weights_ref, *refs
):
    late, refs = refs[:5], refs[5:]
    both_ref, mixed_grad_ref, low_mixed_ref, ctx_grad_ref, hidden_ref, vec_ref, total_ref, pre_ref = refs[:8]
    here_refs, sems = refs[8:13], refs[13]
    copies = [pltpu.make_async_copy(ref, here, sems.at[at]) for at, (ref, here) in enumerate(zip(late, here_refs))]

    @pl.when(pl.program_id(0) == 0)
    def _():
        for copy in copies:
            copy.start()

    ffn_back_chunk(low_ref, low_first_ref, act_ref, slope_ref, w1, w2, both_ref, total_ref, hidden_ref, pre_ref)

    @pl.when(pl.program_id(0) == pl.num_programs(0) - 1)
    def _():
        for copy in copies:
            copy.wait()
        grad_second_ref, other_ref, mixed_ref, wo_a, wo_b = here_refs
        vec_ref[...] = jnp.zeros_like(vec_ref)
        head_width = wo_a.shape[0]
        for at in range(0, mixed_ref.shape[0], SUB):
            here = slice(at, at + SUB)
            normed_one, inverse_one = normalise(mixed_ref[here])
            grad_first = total_ref[here] + other_ref[here] + grad_second_ref[here]
            grad_mixed = norm_back(grad_first, normed_one, inverse_one, weights_ref[GAIN_ONE])
            mixed_grad_ref[here] = grad_mixed
            low_mixed_ref[here] = grad_mixed.astype(bf16)
            valid = as_column(valid_ref[at // SUB].astype(f32))
            add_rows(
                vec_ref,
                (
                    grad_first * normed_one,
                    grad_first,
                    grad_mixed,
                    grad_first * grad_first * valid,
                    grad_mixed * grad_mixed * valid,
                ),
            )
        ctx_grad_ref[:, :head_width] = dot(low_mixed_ref[...], wo_a[...], 1, 1).astype(bf16)
        ctx_grad_ref[:, head_width:] = dot(low_mixed_ref[...], wo_b[...], 1, 1).astype(bf16)


def attend_back_kernel(
    side, q_ref, k_ref, v_ref, p_ref, ctx_ref, ctx_grad_ref, x_ref, low_mixed_ref, out_ref, vec_ref, other_ref, sum_ref
):
    lane = lax.broadcasted_iota(jnp.int32, (1, PAIR), 1)
    for pair in range(q_ref.shape[1] // PAIR):
        here = slice(pair * PAIR, (pair + 1) * PAIR)
        masked = by_head(ctx_grad_ref[:, here], lane)
        ctx = ctx_ref[:, here].astype(f32)
        inner = jnp.sum(masked.astype(f32) * jnp.concatenate([ctx, ctx], 0), axis=-1, keepdims=True)
        probs = p_ref[0, 2 * pair : 2 * pair + 2].reshape(2 * SEQ_LEN, SEQ_LEN)
        grad_scores = (probs.astype(f32) * (dot(masked, v_ref[:, here], 1, 1) - inner)).astype(bf16)
        dq = dot(grad_scores, k_ref[:, here])
        dk = dot(by_head(q_ref[:, here], lane), grad_scores, 0, 0)
        dv = dot(masked, probs, 0, 0)
        dq = jnp.where(lane < HEAD_DIM, dq[:SEQ_LEN], dq[SEQ_LEN:]) * HEAD_DIM ** -0.5
        for at, rows in enumerate((dq, dk.T, dv.T)):
            out_ref[0, :, (3 * pair + at) * PAIR : (3 * pair + at + 1) * PAIR] = rows.astype(bf16)

    @pl.when(pl.program_id(1) == 0)
    def _():
        vec_ref[...] = jnp.zeros_like(vec_ref)

    width = ctx_ref.shape[1]
    other = pl.program_id(0) == 0
    last = pl.program_id(1) == pl.num_programs(1) - 1

    @pl.when(other & (pl.program_id(1) == 0))
    def _():
        sum_ref[:width] = dot(ctx_ref[...], low_mixed_ref[...], 0, 0)
        sum_ref[width:] = dot(out_ref[0], x_ref[...], 0, 0)

    @pl.when(other & (pl.program_id(1) > 0))
    def _():
        sum_ref[:width] += dot(ctx_ref[...], low_mixed_ref[...], 0, 0)
        sum_ref[width:] += dot(out_ref[0], x_ref[...], 0, 0)

    @pl.when(other & last)
    def _():
        other_ref[...] = sum_ref[...].astype(bf16)

    vec_ref[0, 0:1, :] += jnp.sum(out_ref[0].astype(f32), axis=0, keepdims=True)


def attend_weights_kernel(side, three_ref, x_ref, ctx_ref, low_mixed_ref, out_ref):
    width = ctx_ref.shape[1]
    out_ref[:width] = dot(ctx_ref[...], low_mixed_ref[...], 0, 0).astype(bf16)
    out_ref[width:] = dot(three_ref[0], x_ref[...], 0, 0).astype(bf16)


def input_grad_kernel(side, mixed_grad_ref, valid_ref, *refs):
    three_ref, wq_a, wq_b, wk_a, wk_b, wv_a, wv_b, out_ref, vec_ref = refs
    grad_in = mixed_grad_ref[...]
    for half, weights in enumerate(((wq_a, wk_a, wv_a), (wq_b, wk_b, wv_b))):
        for pair in range(wq_a.shape[1] // PAIR):
            here = slice(pair * PAIR, (pair + 1) * PAIR)
            weight = jnp.concatenate([w[:, here] for w in weights], 1)
            grad_in += dot(three_ref[half, :, 3 * pair * PAIR : 3 * (pair + 1) * PAIR], weight, 1, 1)
    out_ref[...] = grad_in.astype(bf16)

    @pl.when(pl.program_id(0) == 0)
    def _():
        vec_ref[...] = jnp.zeros_like(vec_ref)

    add_rows(vec_ref, (grad_in * grad_in * as_column(valid_ref[0].astype(f32)),))


def meet_kernel(places, own, moved, *refs):
    *outs, own_rows, moved_rows, total_rows, in_sems, out_sems = refs
    count = places.shape[0] // 2
    rows = own_rows.shape[0]
    pieces = in_sems.shape[0]
    arriving = []
    for piece in range(pieces):
        here = pl.ds(piece * rows // pieces, rows // pieces)
        copies = [
            pltpu.make_async_copy(ref.at[here], held.at[here], in_sems.at[piece, which])
            for which, (ref, held) in enumerate(((own, own_rows), (moved, moved_rows)))
        ]
        for copy in copies:
            copy.start()
        arriving.append(copies)
    start, leaving = 0, []
    for part in range(2):
        half = outs[2 * part].shape[0]
        size = 2 * half // count
        for block in range(count):
            at = start + block * size
            while pieces - len(arriving) <= (at + size - 1) * pieces // rows:
                for copy in arriving.pop(0):
                    copy.wait()
            here = slice(at, at + size)
            place = pl.multiple_of(start + places[part * count + block] * size, size)
            total_rows[pl.ds(place, size)] = (own_rows[here].astype(f32) + moved_rows[here].astype(f32)).astype(bf16)
        for which in range(2):
            here = pl.ds(start + which * half, half)
            leaving.append(pltpu.make_async_copy(total_rows.at[here], outs[2 * part + which], out_sems.at[len(leaving)]))
            leaving[-1].start()
        start += count * size
    for copy in leaving:
        copy.wait()


def ordered_blocks(places, pieces):
    count = places.shape[0] // 2
    start = 0
    for part in range(2):
        low, high = pieces[2 * part], pieces[2 * part + 1]
        size = 2 * low.shape[0] // count
        for block in range(count):
            place = places[part * count + block]
            below = place < count // 2
            at = pl.multiple_of(jnp.where(below, place, 0) * size, size)
            after = pl.multiple_of(jnp.where(below, 0, place - count // 2) * size, size)
            rows = jnp.where(below, low[pl.ds(at, size)], high[pl.ds(after, size)])
            yield start + block * size, rows.astype(f32)
        start += count * size


def place_ffn_kernel(places, *refs):
    *pieces, w2_ref, w1_ref = refs
    for row, rows in ordered_blocks(places, pieces):
        size = rows.shape[0]
        if row < w2_ref.shape[0]:
            w2_ref[row : row + size] = rows
        else:
            chunk, row = divmod(row - w2_ref.shape[0], D)
            w1_ref[row : row + size, chunk * D : (chunk + 1) * D] = rows


def place_attend_kernel(places, *refs):
    *pieces, wo_ref, wq_ref, wk_ref, wv_ref, sorted_ref = refs
    for row, rows in ordered_blocks(places, pieces):
        sorted_ref[row : row + rows.shape[0]] = rows
    width = wo_ref.shape[0]
    wo_ref[...] = sorted_ref[:width]
    for pair in range(width // PAIR):
        for at, ref in enumerate((wq_ref, wk_ref, wv_ref)):
            start = width + (3 * pair + at) * PAIR
            ref[:, pair * PAIR : (pair + 1) * PAIR] = sorted_ref[start : start + PAIR].T


def lines_kernel(side, two_ref, one_ref, in_ref, three_ref, hidden_own, hidden_other, own_ref, sent_ref):
    pairs = three_ref.shape[2] // (3 * PAIR)
    for half, (out, hidden) in enumerate(((own_ref, hidden_own), (sent_ref, hidden_other))):
        out[12:16] = jnp.zeros((4, D), f32)
        out[0:5] = two_ref[0:5]
        out[5:10] = one_ref[0:5]
        out[10:11] = in_ref[0:1]
        for at, which in enumerate((0, 2)):
            for pair in range(pairs):
                to, start = (at * pairs + pair) * PAIR, (3 * pair + which) * PAIR
                out[11:12, to : to + PAIR] = three_ref[half, 0:1, start : start + PAIR]
        out[12:14] = hidden[0:2]


def run_kernel(kernel, grid, token, operands, outs, scratch=()):
    steps = grid if isinstance(grid, tuple) else (grid,)

    def spec(block, kind):
        rest = (0,) * (len(block) - 1)
        if kind == "late":
            return pl.BlockSpec(memory_space=pl.ANY)
        if callable(kind):
            return pl.BlockSpec(block, kind)
        if kind == "all":
            return pl.BlockSpec(block, lambda *i: (0,) + rest, pipeline_mode=pl.Buffered(1))
        if kind == "side":
            return pl.BlockSpec(block, lambda *i: (i[-1][0],) + rest, pipeline_mode=pl.Buffered(1))
        if kind == "sum":
            return pl.BlockSpec(block, lambda *i: (0,) + rest)
        if kind == "shared":
            return pl.BlockSpec(block, lambda i, s: (s[0] * grid + i,) + rest)
        return pl.BlockSpec(block, lambda i, s: (i,) + rest)

    return pl.pallas_call(
        kernel,
        grid_spec=pltpu.PrefetchScalarGridSpec(
            num_scalar_prefetch=1,
            grid=steps,
            in_specs=[spec(block, kind) for _, block, kind in operands],
            out_specs=[spec(block, kind) for _, block, kind in outs],
            scratch_shapes=list(scratch),
        ),
        out_shape=[shape for shape, _, _ in outs],
        compiler_params=pltpu.CompilerParams(vmem_limit_bytes=VMEM_BYTES),
        cost_estimate=LIGHT,
    )(token, *[array for array, _, _ in operands])


def like(shape, dtype):
    return jax.ShapeDtypeStruct(shape, dtype)


def whole(array):
    return (array, array.shape, "all")


def swap_narrow(values):
    return lax.ppermute(values, "narrow", [(0, 1), (1, 0)])


class WideSum:
    def __init__(self, own, moved, size):
        bits = size.bit_length() - 1
        late = list(range(3, bits))
        first = [0, 1, 2][:bits]
        turned = [first[i:] + first[:i] + late for i in range(3)]
        self.size, self.bits = size, bits
        self.orders = [(turned[0], turned[1]), (turned[2], turned[2])]
        self.step = 0
        me, core = lax.axis_index("wide"), lax.axis_index("narrow")
        place = jnp.arange(size, dtype=jnp.int32)

        def gather(value, order):
            return sum(((value >> bit) & 1) << (bits - 1 - at) for at, bit in enumerate(order))

        def both(change, value):
            return jnp.concatenate([jnp.where(core == 0, *(change(value, o) for o in pair)) for pair in self.orders])

        self.places = both(gather, place ^ me)
        rows = own.shape[0]
        halves = (rows // 3, rows // 6)
        self.parts = pl.pallas_call(
            meet_kernel,
            in_specs=[pl.BlockSpec(memory_space=pltpu.SMEM)] + [pl.BlockSpec(memory_space=pl.ANY)] * 2,
            out_specs=[pl.BlockSpec(memory_space=pl.ANY)] * 4,
            out_shape=[like((half, D), bf16) for half in halves for _ in range(2)],
            scratch_shapes=[pltpu.VMEM((rows, D), bf16)] * 3
            + [pltpu.SemaphoreType.DMA((6, 2)), pltpu.SemaphoreType.DMA((4,))],
            compiler_params=pltpu.CompilerParams(vmem_limit_bytes=VMEM_BYTES),
            cost_estimate=LIGHT,
        )(self.places, own, moved)

    def start(self):
        halving = self.step < self.bits
        at = self.step if halving else 2 * self.bits - 1 - self.step
        moving = []
        for part, orders in enumerate(self.orders):
            masks = [1 << order[at] for order in orders]
            pairs = [(w * 2 + c, (w ^ masks[c]) * 2 + c) for w in range(self.size) for c in range(2)]
            moving.append(lax.ppermute(self.parts[2 * part + 1] if halving else self.parts[part], ("wide", "narrow"), pairs))
        return moving

    def finish(self, moved):
        parts = []
        for part, got in enumerate(moved):
            if self.step < self.bits:
                kept = self.parts[2 * part]
                half = kept.shape[0] // 2
                cuts = ((0, half), (half, 2 * half)) if self.step < self.bits - 1 else ((0, 2 * half),)
                parts += [(kept[a:b].astype(f32) + got[a:b].astype(f32)).astype(bf16) for a, b in cuts]
            elif self.step < 2 * self.bits - 1:
                parts.append(jnp.concatenate([self.parts[part], got], 0))
            else:
                parts += [self.parts[part], got]
        self.parts = parts
        self.step += 1

    @property
    def done(self):
        return self.step == 2 * self.bits

    def result(self, kernel, outs, scratch=()):
        return pl.pallas_call(
            kernel,
            in_specs=[pl.BlockSpec(memory_space=pltpu.SMEM)] + [pl.BlockSpec(memory_space=pltpu.VMEM)] * 4,
            out_specs=[pl.BlockSpec(memory_space=pltpu.VMEM)] * len(outs),
            out_shape=[like(shape, f32) for shape in outs],
            scratch_shapes=list(scratch),
            compiler_params=pltpu.CompilerParams(vmem_limit_bytes=VMEM_BYTES),
            cost_estimate=LIGHT,
        )(self.places, *self.parts)


class SmallSum:
    def __init__(self, values, size):
        self.parts, self.size, self.step = [values], size, 0
        self.bits = size.bit_length() - 1

    def start(self):
        return [lax.ppermute(self.parts[0], "wide", [(i, i ^ (1 << self.step)) for i in range(self.size)])]

    def finish(self, moved):
        self.parts = [self.parts[0] + moved[0]]
        self.step += 1

    @property
    def done(self):
        return self.step == self.bits


def slot(sums, compute, token):
    live = [s for s in sums if not s.done]
    parts, token = lax.optimization_barrier(([s.parts for s in live], token))
    for one, held in zip(live, parts):
        one.parts = held
    moving = [s.start() for s in live]
    outs = compute(token) if compute else ()
    moving, outs, token = lax.optimization_barrier((moving, outs, token))
    for one, moved in zip(live, moving):
        one.finish(moved)
    return outs, token


def body(size, *arrays):
    (
        inputs, segments, valid, w_query, w_key, w_value, b_query, b_value, w_attn_out, b_attn_out,
        gain_one, shift_one, w_ffn_in, b_ffn_in, w_ffn_out, b_ffn_out, gain_two, shift_two, out_grad,
    ) = arrays
    side = lax.axis_index("narrow")
    rows = inputs.shape[0] // 2
    seqs = rows // SEQ_LEN
    head_width = w_query.shape[1]
    hidden = w_ffn_in.shape[1]
    pairs = head_width // PAIR
    token = side.astype(jnp.int32).reshape(1)
    row_block = 256
    blocks = rows // row_block

    def pair_of(array):
        return (array, swap_narrow(array))

    def join_rows(array, other):
        return jnp.where(
            side == 0,
            jnp.concatenate([array, other], 0),
            jnp.concatenate([other, array], 0),
        )

    wq, wk, wv = pair_of(w_query), pair_of(w_key), pair_of(w_value)
    wo = pair_of(w_attn_out)
    def packed(pieces, length):
        total = 0.0
        for at, vector in pieces:
            total += jnp.pad(vector.astype(f32), (at, length - at - vector.shape[0]))
        return total

    own_vectors = packed([(0, b_query), (head_width, b_value), (2 * head_width, b_ffn_in)], 3 * D)
    rest = [b_attn_out, b_ffn_out, gain_one, shift_one, gain_two, shift_two]
    vectors = packed(
        [(0, own_vectors), (3 * D, swap_narrow(own_vectors))] + [((6 + at) * D, v) for at, v in enumerate(rest)], 16 * D
    ).reshape(16, D)
    _, ffn_in, ffn_out = lax.optimization_barrier(((wq, wk, wv, wo, vectors), w_ffn_in, w_ffn_out))
    w1, w2 = (w_ffn_in, swap_narrow(ffn_in)), (w_ffn_out, swap_narrow(ffn_out))
    seg_rows = segments.reshape(-1, 1, SEQ_LEN)
    valid_seq = valid.reshape(-1, 1, SEQ_LEN)
    valid_block = valid.reshape(-1, 1, row_block)
    seq = (SEQ_LEN, D)
    blk = (row_block, D)
    low_rows = like((rows, D), bf16)
    full_rows = like((rows, D), f32)
    sums_shape = (like((8, D), f32), (8, D), "sum")

    queries, keys, values, probs, context, mixed = run_kernel(
        attend_kernel,
        seqs,
        token,
        [(inputs, seq, "shared"), (seg_rows, (1, 1, SEQ_LEN), "shared"), (valid_seq, (1, 1, SEQ_LEN), "shared")]
        + [whole(w) for w in wq + wk + wv + wo]
        + [whole(vectors)],
        [(low_rows, seq, "own")] * 3
        + [(like((seqs, 4 * pairs, SEQ_LEN, SEQ_LEN), bf16), (1, 4 * pairs, SEQ_LEN, SEQ_LEN), "own")]
        + [(low_rows, seq, "own"), (full_rows, seq, "own")],
        [pltpu.VMEM((SEQ_LEN, SEQ_LEN), f32)],
    )
    chunks = hidden // D
    row_shape = (rows, D)
    hidden_rows = like((rows, 2 * hidden), bf16)
    low_first, activated, slope, final, grad_second, low_second, vec_two = run_kernel(
        ffn_kernel,
        blocks,
        token,
        [(mixed, blk, "own"), (valid_block, (1, 1, row_block), "shared"), (out_grad, blk, "shared")]
        + [whole(w) for w in w1 + w2]
        + [whole(vectors)],
        [
            (low_rows, blk, "own"),
            (hidden_rows, (row_block, 2 * hidden), "own"),
            (hidden_rows, (row_block, 2 * hidden), "own"),
            (low_rows, blk, "own"),
            (full_rows, blk, "own"),
            (low_rows, blk, "own"),
            sums_shape,
        ],
        (),
    )

    def ffn_back(kernel, half, extra, outs, scratch, late=()):
        return run_kernel(
            kernel,
            chunks,
            token,
            [whole(a) for a in (low_second, low_first)]
            + [(a, (rows, D), lambda i, s: (0, half * chunks + i)) for a in (activated, slope)]
            + [(w1[half], (D, D), lambda i, s: (0, i)), (w2[half], (D, D), lambda i, s: (i, 0))]
            + extra
            + [(a, a.shape, "late") for a in late],
            [(like((2, chunks, D, D), bf16), (2, 1, D, D), lambda i, s: (0, i, 0, 0))] + outs,
            scratch
            + [pltpu.VMEM(row_shape, bf16)]
            + [pltpu.VMEM(a.shape, a.dtype) for a in late]
            + [pltpu.SemaphoreType.DMA((len(late),)) for _ in late[:1]],
        )

    valid_part = (valid_block, (blocks, 1, row_block), "side")
    sent, total, hidden_other = ffn_back(
        ffn_back_other_kernel, 1, [], [(full_rows, row_shape, "sum"), sums_shape], []
    )
    moved = swap_narrow(sent)
    own, grad_mixed, low_mixed, grad_context, hidden_own, vec_one = ffn_back(
        ffn_back_own_kernel,
        0,
        [valid_part, whole(vectors)],
        [(full_rows, row_shape, "sum"), (low_rows, row_shape, "sum"), (low_rows, row_shape, "sum"), sums_shape, sums_shape],
        [pltpu.VMEM(row_shape, f32)],
        (grad_second, total, mixed) + wo,
    )
    sum_ffn = WideSum(own.reshape(-1, D), moved.reshape(-1, D), size)

    def attend_back(token):
        def column(h, i, s):
            return (i, 1 - h)

        half_weights = like((4 * head_width, D), bf16)
        return tuple(
            run_kernel(
                attend_back_kernel,
                (2, seqs),
                token,
                [(a, (SEQ_LEN, head_width), column) for a in (queries, keys, values)]
                + [(probs, (1, 2 * pairs, SEQ_LEN, SEQ_LEN), lambda h, i, s: (i, 1 - h, 0, 0))]
                + [(a, (SEQ_LEN, head_width), column) for a in (context, grad_context)]
                + [(inputs, seq, lambda h, i, s: (s[0] * seqs + i, 0)), (low_mixed, seq, lambda h, i, s: (i, 0))],
                [
                    (
                        like((2, rows, 3 * head_width), bf16),
                        (1, SEQ_LEN, 3 * head_width),
                        lambda h, i, s: (1 - h, i, 0),
                    ),
                    (like((2, 8, 3 * head_width), f32), (1, 8, 3 * head_width), lambda h, i, s: (1 - h, 0, 0)),
                    (half_weights, half_weights.shape, "sum"),
                ],
                [pltpu.VMEM(half_weights.shape, f32)],
            )
        )

    def own_weights(token):
        return run_kernel(
            attend_weights_kernel,
            1,
            token,
            [
                (three, (1, rows, 3 * head_width), lambda i, s: (0, 0, 0)),
                (inputs, row_shape, "side"),
                (context, (rows, head_width), lambda i, s: (0, 0)),
                whole(low_mixed),
            ],
            [(like((4 * head_width, D), bf16), (4 * head_width, D), "sum")],
        )[0]

    (three, vec_three, sent), token = slot([sum_ffn], attend_back, token)
    (moved, own), token = slot([sum_ffn], lambda token: (swap_narrow(sent), own_weights(token)), token)
    sum_attn = WideSum(own, moved, size)

    def last(token):
        grad_in, vec_in = run_kernel(
            input_grad_kernel,
            seqs,
            token,
            [(grad_mixed, seq, "own"), (valid_seq, (1, 1, SEQ_LEN), "shared")]
            + [(three, (2, SEQ_LEN, 3 * head_width), lambda i, s: (0, i, 0))]
            + [whole(w) for w in wq + wk + wv],
            [(low_rows, seq, "own"), sums_shape],
        )
        lines = run_kernel(
            lines_kernel,
            1,
            token,
            [whole(v) for v in (vec_two, vec_one, vec_in, vec_three, hidden_own, hidden_other)],
            [(like((16, D), f32), (16, D), "sum")] * 2,
        )
        return (grad_in, *lines)

    (grad_in, lines_own, lines_sent, final_other), token = slot(
        [sum_ffn, sum_attn], lambda token: last(token) + (swap_narrow(final),), token
    )
    small = SmallSum(lines_own + swap_narrow(lines_sent), size)
    sums = [sum_ffn, sum_attn, small]

    def place_ffn(token):
        return tuple(sum_ffn.result(place_ffn_kernel, [(hidden, D), (D, hidden)]))

    (output, grad_other), token = slot(
        sums, lambda token: (join_rows(final, final_other), swap_narrow(grad_in)), token
    )
    (input_grad,), token = slot(sums, lambda token: (join_rows(grad_in, grad_other),), token)
    placed = None
    while not all(s.done for s in sums):
        late = sum_ffn.done and placed is None
        outs, token = slot(sums, place_ffn if late else None, token)
        placed = outs if late else placed
    d_w_out, d_w_in = placed
    small = small.parts[0]
    total = jnp.sum(jnp.stack([small[10], small[3], small[8], small[9]]), axis=1)
    rms = jnp.sqrt(total / (small[4, 0] * D))
    d_w_attn, *d_w_three = sum_attn.result(
        place_attend_kernel, [(head_width, D)] + [(D, head_width)] * 3, [pltpu.VMEM((4 * head_width, D), f32)]
    )
    return (
        output,
        input_grad,
        *d_w_three,
        small[11, :head_width],
        small[11, head_width:],
        d_w_attn,
        small[7],
        small[5],
        small[6],
        d_w_in,
        small[12 : 12 + chunks].reshape(-1),
        d_w_out,
        small[2],
        small[0],
        small[1],
        rms,
    )


def solution(mesh):
    row, col = P("narrow", None), P(None, "narrow")
    one, rows = P("narrow"), P("wide", None)
    in_specs = (
        rows, P("wide"), P("wide"), col, col, col, one, one, row, P(), P(), P(), col, one, row, P(), P(), P(), rows,
    )
    out_specs = (
        rows, rows, col, col, col, one, one, row, P(), P(), P(), col, one, row, P(), P(), P(), P(),
    )
    return jax.shard_map(
        partial(body, mesh.shape["wide"]), mesh=mesh, in_specs=in_specs, out_specs=out_specs, check_vma=False
    )
```

```python
from functools import partial

import jax
import jax.numpy as jnp
from jax import lax
from jax.experimental import pallas as pl
from jax.experimental.pallas import tpu as pltpu
from jax.sharding import PartitionSpec as P

D = 768
HEAD_DIM = 64
SEQ_LEN = 512
PAIR = 2 * HEAD_DIM
norm_eps = 1e-06
f32 = jnp.float32
bf16 = jnp.bfloat16
VMEM_BYTES = 58 << 20
LIGHT = pl.CostEstimate(flops=1 << 20, bytes_accessed=0, transcendentals=0)
B_OUT, B_FFN, GAIN_ONE, SHIFT_ONE, GAIN_TWO, SHIFT_TWO = (slice(row, row + 1) for row in range(6, 12))


def dot(left, right, left_dim=1, right_dim=0):
    return lax.dot_general(
        left, right, (((left_dim,), (right_dim,)), ((), ())), preferred_element_type=f32
    )


def normalise(values):
    centred = values - jnp.mean(values, axis=-1, keepdims=True)
    inverse = lax.rsqrt(jnp.mean(centred * centred, axis=-1, keepdims=True) + norm_eps)
    return centred * inverse, inverse


def norm_back(grad_rows, normed, inverse, gain):
    inner = grad_rows * gain
    centre_part = jnp.mean(inner, axis=-1, keepdims=True)
    slope_part = jnp.mean(inner * normed, axis=-1, keepdims=True)
    return inverse * (inner - centre_part - normed * slope_part)


def as_column(row):
    return jnp.broadcast_to(row, (8, row.shape[1])).T[:, :1]


def add_rows(ref, rows):
    for at, values in enumerate(rows):
        ref[at : at + 1, :] += jnp.sum(values, axis=0, keepdims=True)


def clear_first(ref):
    @pl.when(pl.program_id(0) == 0)
    def _():
        ref[...] = jnp.zeros_like(ref)


def by_head(rows, lane):
    return jnp.concatenate([jnp.where(lane < HEAD_DIM, rows, 0), jnp.where(lane < HEAD_DIM, 0, rows)], 0)


def gelu_both(pre):
    below = 0.5 * lax.erf(pre * 0.7071067811865476) + 0.5
    return pre * below, below + pre * (0.3989422804014327 * jnp.exp(pre * pre * -0.5))


def attend_kernel(
    side, x_ref, seg_ref, valid_ref, wq_a, wq_b, wk_a, wk_b, wv_a, wv_b, wo_a, wo_b, vec_ref,
    q_ref, k_ref, v_ref, p_ref, ctx_ref, mixed_ref, bias_ref,
):
    x = x_ref[...]
    seg = seg_ref[0].astype(f32)
    allowed = (as_column(seg) == seg) & (valid_ref[0] == 1)
    bias_ref[...] = jnp.where(allowed, 0.0, -1e30)
    width = wq_a.shape[1]
    for at, (wq, wk, wv) in enumerate(((wq_a, wk_a, wv_a), (wq_b, wk_b, wv_b))):
        here = slice(at * width, (at + 1) * width)
        q_ref[:, here] = (dot(x, wq[...]) + vec_ref[3 * at : 3 * at + 1, :width]).astype(bf16) * jnp.asarray(HEAD_DIM ** -0.5, bf16)
        k_ref[:, here] = dot(x, wk[...]).astype(bf16)
        v_ref[:, here] = (dot(x, wv[...]) + vec_ref[3 * at : 3 * at + 1, width:]).astype(bf16)

    lane = lax.broadcasted_iota(jnp.int32, (1, PAIR), 1)
    for pair in range(2 * width // PAIR):
        here = slice(pair * PAIR, (pair + 1) * PAIR)
        scores = dot(by_head(q_ref[:, here], lane), k_ref[:, here], 1, 1)
        parts = []
        for head in range(2):
            ours = scores[head * SEQ_LEN : (head + 1) * SEQ_LEN] + bias_ref[...]
            shifted = jnp.exp(ours - jnp.max(ours, axis=-1, keepdims=True))
            p_ref[0, 2 * pair + head] = (shifted * (1.0 / jnp.sum(shifted, axis=-1, keepdims=True))).astype(bf16)
        both = dot(p_ref[0, 2 * pair : 2 * pair + 2].reshape(2 * SEQ_LEN, SEQ_LEN), v_ref[:, here])
        ctx_ref[:, here] = jnp.where(lane < HEAD_DIM, both[:SEQ_LEN], both[SEQ_LEN:]).astype(bf16)
    attn = dot(ctx_ref[:, :width], wo_a[...]) + dot(ctx_ref[:, width:], wo_b[...])
    mixed_ref[...] = x.astype(f32) + attn + vec_ref[B_OUT]


SUB = 256


def ffn_kernel(
    side, mixed_ref, valid_ref, cot_ref, w1_a, w1_b, w2_a, w2_b, weights_ref,
    low_first_ref, act_ref, slope_ref, out_ref, grad_ref, low_ref, vec_ref,
):
    normed_one, _ = normalise(mixed_ref[...])
    first = normed_one * weights_ref[GAIN_ONE] + weights_ref[SHIFT_ONE]
    low_first = first.astype(bf16)
    low_first_ref[...] = low_first
    second = first + weights_ref[B_FFN]
    width = w1_a.shape[1]
    step = 256
    for half, (w1, w2) in enumerate(((w1_a, w2_a), (w1_b, w2_b))):
        for at in range(0, width, step):
            here = slice(half * width + at, half * width + at + step)
            pre = dot(low_first, w1[:, at : at + step]) + weights_ref[3 * half + 1 + at // D : 3 * half + 2 + at // D, at % D : at % D + step]
            act, slope = gelu_both(pre)
            act = act.astype(bf16)
            act_ref[:, here] = act
            slope_ref[:, here] = slope.astype(bf16)
            second += dot(act, w2[at : at + step, :])
    normed_two, inverse_two = normalise(second)
    gain = weights_ref[GAIN_TWO]
    out_ref[...] = (normed_two * gain + weights_ref[SHIFT_TWO]).astype(bf16)
    valid = as_column(valid_ref[0].astype(f32))
    grad_out = cot_ref[...].astype(f32) * valid
    grad = norm_back(grad_out, normed_two, inverse_two, gain)
    grad_ref[...] = grad
    low_ref[...] = grad.astype(bf16)
    clear_first(vec_ref)
    add_rows(vec_ref, (grad_out * normed_two, grad_out, grad, grad * grad * valid, valid))


def ffn_back_chunk(low_ref, low_first_ref, act_ref, slope_ref, w1, w2, both_ref, total_ref, hidden_ref, pre_ref):
    step = pl.program_id(0)
    both_ref[0, 0] = dot(act_ref[...], low_ref[...], 0, 0).astype(bf16)
    grad_pre = dot(low_ref[...], w2[...], 1, 1) * slope_ref[...].astype(f32)
    pre_ref[...] = grad_pre.astype(bf16)
    hidden_ref[pl.ds(step, 1), :] = jnp.sum(grad_pre, axis=0, keepdims=True)
    both_ref[1, 0] = dot(low_first_ref[...], pre_ref[...], 0, 0).astype(bf16)

    @pl.when(step == 0)
    def _():
        total_ref[...] = dot(pre_ref[...], w1[...], 1, 1)

    @pl.when(step > 0)
    def _():
        total_ref[...] += dot(pre_ref[...], w1[...], 1, 1)


def ffn_back_other_kernel(
    side, low_ref, low_first_ref, act_ref, slope_ref, w1, w2, both_ref, total_ref, hidden_ref, pre_ref
):
    ffn_back_chunk(low_ref, low_first_ref, act_ref, slope_ref, w1, w2, both_ref, total_ref, hidden_ref, pre_ref)


def ffn_back_own_kernel(
    side, low_ref, low_first_ref, act_ref, slope_ref, w1, w2, valid_ref, weights_ref, *refs
):
    late, refs = refs[:5], refs[5:]
    both_ref, mixed_grad_ref, low_mixed_ref, ctx_grad_ref, hidden_ref, vec_ref, total_ref, pre_ref = refs[:8]
    here_refs, sems = refs[8:13], refs[13]
    copies = [pltpu.make_async_copy(ref, here, sems.at[at]) for at, (ref, here) in enumerate(zip(late, here_refs))]

    @pl.when(pl.program_id(0) == 0)
    def _():
        for copy in copies:
            copy.start()

    ffn_back_chunk(low_ref, low_first_ref, act_ref, slope_ref, w1, w2, both_ref, total_ref, hidden_ref, pre_ref)

    @pl.when(pl.program_id(0) == pl.num_programs(0) - 1)
    def _():
        for copy in copies:
            copy.wait()
        grad_second_ref, other_ref, mixed_ref, wo_a, wo_b = here_refs
        vec_ref[...] = jnp.zeros_like(vec_ref)
        head_width = wo_a.shape[0]
        for at in range(0, mixed_ref.shape[0], SUB):
            here = slice(at, at + SUB)
            normed_one, inverse_one = normalise(mixed_ref[here])
            grad_first = total_ref[here] + other_ref[here] + grad_second_ref[here]
            grad_mixed = norm_back(grad_first, normed_one, inverse_one, weights_ref[GAIN_ONE])
            mixed_grad_ref[here] = grad_mixed
            low_mixed_ref[here] = grad_mixed.astype(bf16)
            valid = as_column(valid_ref[at // SUB].astype(f32))
            add_rows(
                vec_ref,
                (
                    grad_first * normed_one,
                    grad_first,
                    grad_mixed,
                    grad_first * grad_first * valid,
                    grad_mixed * grad_mixed * valid,
                ),
            )
        ctx_grad_ref[:, :head_width] = dot(low_mixed_ref[...], wo_a[...], 1, 1).astype(bf16)
        ctx_grad_ref[:, head_width:] = dot(low_mixed_ref[...], wo_b[...], 1, 1).astype(bf16)


def attend_back_kernel(
    side, q_ref, k_ref, v_ref, p_ref, ctx_ref, ctx_grad_ref, x_ref, low_mixed_ref, out_ref, vec_ref, other_ref, sum_ref
):
    lane = lax.broadcasted_iota(jnp.int32, (1, PAIR), 1)
    for pair in range(q_ref.shape[1] // PAIR):
        here = slice(pair * PAIR, (pair + 1) * PAIR)
        masked = by_head(ctx_grad_ref[:, here], lane)
        ctx = ctx_ref[:, here].astype(f32)
        inner = jnp.sum(masked.astype(f32) * jnp.concatenate([ctx, ctx], 0), axis=-1, keepdims=True)
        probs = p_ref[0, 2 * pair : 2 * pair + 2].reshape(2 * SEQ_LEN, SEQ_LEN)
        grad_scores = (probs.astype(f32) * (dot(masked, v_ref[:, here], 1, 1) - inner)).astype(bf16)
        dq = dot(grad_scores, k_ref[:, here])
        dk = dot(by_head(q_ref[:, here], lane), grad_scores, 0, 0)
        dv = dot(masked, probs, 0, 0)
        dq = jnp.where(lane < HEAD_DIM, dq[:SEQ_LEN], dq[SEQ_LEN:]) * HEAD_DIM ** -0.5
        for at, rows in enumerate((dq, dk.T, dv.T)):
            out_ref[0, :, (3 * pair + at) * PAIR : (3 * pair + at + 1) * PAIR] = rows.astype(bf16)

    @pl.when(pl.program_id(1) == 0)
    def _():
        vec_ref[...] = jnp.zeros_like(vec_ref)

    width = ctx_ref.shape[1]
    other = pl.program_id(0) == 0
    last = pl.program_id(1) == pl.num_programs(1) - 1

    @pl.when(other & (pl.program_id(1) == 0))
    def _():
        sum_ref[:width] = dot(ctx_ref[...], low_mixed_ref[...], 0, 0)
        sum_ref[width:] = dot(out_ref[0], x_ref[...], 0, 0)

    @pl.when(other & (pl.program_id(1) > 0))
    def _():
        sum_ref[:width] += dot(ctx_ref[...], low_mixed_ref[...], 0, 0)
        sum_ref[width:] += dot(out_ref[0], x_ref[...], 0, 0)

    @pl.when(other & last)
    def _():
        other_ref[...] = sum_ref[...].astype(bf16)

    vec_ref[0, 0:1, :] += jnp.sum(out_ref[0].astype(f32), axis=0, keepdims=True)


def attend_weights_kernel(side, three_ref, x_ref, ctx_ref, low_mixed_ref, out_ref):
    width = ctx_ref.shape[1]
    out_ref[:width] = dot(ctx_ref[...], low_mixed_ref[...], 0, 0).astype(bf16)
    out_ref[width:] = dot(three_ref[0], x_ref[...], 0, 0).astype(bf16)


def input_grad_kernel(side, mixed_grad_ref, valid_ref, *refs):
    three_ref, wq_a, wq_b, wk_a, wk_b, wv_a, wv_b, out_ref, vec_ref = refs
    grad_in = mixed_grad_ref[...]
    for half, weights in enumerate(((wq_a, wk_a, wv_a), (wq_b, wk_b, wv_b))):
        for pair in range(wq_a.shape[1] // PAIR):
            here = slice(pair * PAIR, (pair + 1) * PAIR)
            weight = jnp.concatenate([w[:, here] for w in weights], 1)
            grad_in += dot(three_ref[half, :, 3 * pair * PAIR : 3 * (pair + 1) * PAIR], weight, 1, 1)
    out_ref[...] = grad_in.astype(bf16)

    @pl.when(pl.program_id(0) == 0)
    def _():
        vec_ref[...] = jnp.zeros_like(vec_ref)

    add_rows(vec_ref, (grad_in * grad_in * as_column(valid_ref[0].astype(f32)),))


def meet_kernel(places, own, moved, *refs):
    *outs, own_rows, moved_rows, total_rows, in_sems, out_sems = refs
    count = places.shape[0] // 2
    rows = own_rows.shape[0]
    pieces = in_sems.shape[0]
    arriving = []
    for piece in range(pieces):
        here = pl.ds(piece * rows // pieces, rows // pieces)
        copies = [
            pltpu.make_async_copy(ref.at[here], held.at[here], in_sems.at[piece, which])
            for which, (ref, held) in enumerate(((own, own_rows), (moved, moved_rows)))
        ]
        for copy in copies:
            copy.start()
        arriving.append(copies)
    start, leaving = 0, []
    for part in range(2):
        half = outs[2 * part].shape[0]
        size = 2 * half // count
        for block in range(count):
            at = start + block * size
            while pieces - len(arriving) <= (at + size - 1) * pieces // rows:
                for copy in arriving.pop(0):
                    copy.wait()
            here = slice(at, at + size)
            place = pl.multiple_of(start + places[part * count + block] * size, size)
            total_rows[pl.ds(place, size)] = (own_rows[here].astype(f32) + moved_rows[here].astype(f32)).astype(bf16)
        for which in range(2):
            here = pl.ds(start + which * half, half)
            leaving.append(pltpu.make_async_copy(total_rows.at[here], outs[2 * part + which], out_sems.at[len(leaving)]))
            leaving[-1].start()
        start += count * size
    for copy in leaving:
        copy.wait()


def ordered_blocks(places, pieces):
    count = places.shape[0] // 2
    start = 0
    for part in range(2):
        low, high = pieces[2 * part], pieces[2 * part + 1]
        size = 2 * low.shape[0] // count
        for block in range(count):
            place = places[part * count + block]
            below = place < count // 2
            at = pl.multiple_of(jnp.where(below, place, 0) * size, size)
            after = pl.multiple_of(jnp.where(below, 0, place - count // 2) * size, size)
            rows = jnp.where(below, low[pl.ds(at, size)], high[pl.ds(after, size)])
            yield start + block * size, rows.astype(f32)
        start += count * size


def place_ffn_kernel(places, *refs):
    *pieces, w2_ref, w1_ref = refs
    for row, rows in ordered_blocks(places, pieces):
        size = rows.shape[0]
        if row < w2_ref.shape[0]:
            w2_ref[row : row + size] = rows
        else:
            chunk, row = divmod(row - w2_ref.shape[0], D)
            w1_ref[row : row + size, chunk * D : (chunk + 1) * D] = rows


def place_attend_kernel(places, *refs):
    *pieces, wo_ref, wq_ref, wk_ref, wv_ref, sorted_ref = refs
    for row, rows in ordered_blocks(places, pieces):
        sorted_ref[row : row + rows.shape[0]] = rows
    width = wo_ref.shape[0]
    wo_ref[...] = sorted_ref[:width]
    for pair in range(width // PAIR):
        for at, ref in enumerate((wq_ref, wk_ref, wv_ref)):
            start = width + (3 * pair + at) * PAIR
            ref[:, pair * PAIR : (pair + 1) * PAIR] = sorted_ref[start : start + PAIR].T


def lines_kernel(side, two_ref, one_ref, in_ref, three_ref, hidden_own, hidden_other, own_ref, sent_ref):
    pairs = three_ref.shape[2] // (3 * PAIR)
    for half, (out, hidden) in enumerate(((own_ref, hidden_own), (sent_ref, hidden_other))):
        out[12:16] = jnp.zeros((4, D), f32)
        out[0:5] = two_ref[0:5]
        out[5:10] = one_ref[0:5]
        out[10:11] = in_ref[0:1]
        for at, which in enumerate((0, 2)):
            for pair in range(pairs):
                to, start = (at * pairs + pair) * PAIR, (3 * pair + which) * PAIR
                out[11:12, to : to + PAIR] = three_ref[half, 0:1, start : start + PAIR]
        out[12:14] = hidden[0:2]


def run_kernel(kernel, grid, token, operands, outs, scratch=()):
    steps = grid if isinstance(grid, tuple) else (grid,)

    def spec(block, kind):
        rest = (0,) * (len(block) - 1)
        if kind == "late":
            return pl.BlockSpec(memory_space=pl.ANY)
        if callable(kind):
            return pl.BlockSpec(block, kind)
        if kind == "all":
            return pl.BlockSpec(block, lambda *i: (0,) + rest, pipeline_mode=pl.Buffered(1))
        if kind == "side":
            return pl.BlockSpec(block, lambda *i: (i[-1][0],) + rest, pipeline_mode=pl.Buffered(1))
        if kind == "sum":
            return pl.BlockSpec(block, lambda *i: (0,) + rest)
        if kind == "shared":
            return pl.BlockSpec(block, lambda i, s: (s[0] * grid + i,) + rest)
        return pl.BlockSpec(block, lambda i, s: (i,) + rest)

    return pl.pallas_call(
        kernel,
        grid_spec=pltpu.PrefetchScalarGridSpec(
            num_scalar_prefetch=1,
            grid=steps,
            in_specs=[spec(block, kind) for _, block, kind in operands],
            out_specs=[spec(block, kind) for _, block, kind in outs],
            scratch_shapes=list(scratch),
        ),
        out_shape=[shape for shape, _, _ in outs],
        compiler_params=pltpu.CompilerParams(vmem_limit_bytes=VMEM_BYTES),
        cost_estimate=LIGHT,
    )(token, *[array for array, _, _ in operands])


def like(shape, dtype):
    return jax.ShapeDtypeStruct(shape, dtype)


def whole(array):
    return (array, array.shape, "all")


def swap_narrow(values):
    return lax.ppermute(values, "narrow", [(0, 1), (1, 0)])


class WideSum:
    def __init__(self, own, moved, size):
        bits = size.bit_length() - 1
        late = list(range(3, bits))
        first = [0, 1, 2][:bits]
        turned = [first[i:] + first[:i] + late for i in range(3)]
        self.size, self.bits = size, bits
        self.orders = [(turned[0], turned[1]), (turned[2], turned[2])]
        self.step = 0
        me, core = lax.axis_index("wide"), lax.axis_index("narrow")
        place = jnp.arange(size, dtype=jnp.int32)

        def gather(value, order):
            return sum(((value >> bit) & 1) << (bits - 1 - at) for at, bit in enumerate(order))

        def both(change, value):
            return jnp.concatenate([jnp.where(core == 0, *(change(value, o) for o in pair)) for pair in self.orders])

        self.places = both(gather, place ^ me)
        rows = own.shape[0]
        halves = (rows // 3, rows // 6)
        self.parts = pl.pallas_call(
            meet_kernel,
            in_specs=[pl.BlockSpec(memory_space=pltpu.SMEM)] + [pl.BlockSpec(memory_space=pl.ANY)] * 2,
            out_specs=[pl.BlockSpec(memory_space=pl.ANY)] * 4,
            out_shape=[like((half, D), bf16) for half in halves for _ in range(2)],
            scratch_shapes=[pltpu.VMEM((rows, D), bf16)] * 3
            + [pltpu.SemaphoreType.DMA((6, 2)), pltpu.SemaphoreType.DMA((4,))],
            compiler_params=pltpu.CompilerParams(vmem_limit_bytes=VMEM_BYTES),
            cost_estimate=LIGHT,
        )(self.places, own, moved)

    def start(self):
        halving = self.step < self.bits
        at = self.step if halving else 2 * self.bits - 1 - self.step
        moving = []
        for part, orders in enumerate(self.orders):
            masks = [1 << order[at] for order in orders]
            pairs = [(w * 2 + c, (w ^ masks[c]) * 2 + c) for w in range(self.size) for c in range(2)]
            moving.append(lax.ppermute(self.parts[2 * part + 1] if halving else self.parts[part], ("wide", "narrow"), pairs))
        return moving

    def finish(self, moved):
        parts = []
        for part, got in enumerate(moved):
            if self.step < self.bits:
                kept = self.parts[2 * part]
                half = kept.shape[0] // 2
                cuts = ((0, half), (half, 2 * half)) if self.step < self.bits - 1 else ((0, 2 * half),)
                parts += [(kept[a:b].astype(f32) + got[a:b].astype(f32)).astype(bf16) for a, b in cuts]
            elif self.step < 2 * self.bits - 1:
                parts.append(jnp.concatenate([self.parts[part], got], 0))
            else:
                parts += [self.parts[part], got]
        self.parts = parts
        self.step += 1

    @property
    def done(self):
        return self.step == 2 * self.bits

    def result(self, kernel, outs, scratch=()):
        return pl.pallas_call(
            kernel,
            in_specs=[pl.BlockSpec(memory_space=pltpu.SMEM)] + [pl.BlockSpec(memory_space=pltpu.VMEM)] * 4,
            out_specs=[pl.BlockSpec(memory_space=pltpu.VMEM)] * len(outs),
            out_shape=[like(shape, f32) for shape in outs],
            scratch_shapes=list(scratch),
            compiler_params=pltpu.CompilerParams(vmem_limit_bytes=VMEM_BYTES),
            cost_estimate=LIGHT,
        )(self.places, *self.parts)


class SmallSum:
    def __init__(self, values, size):
        self.parts, self.size, self.step = [values], size, 0
        self.bits = size.bit_length() - 1

    def start(self):
        return [lax.ppermute(self.parts[0], "wide", [(i, i ^ (1 << self.step)) for i in range(self.size)])]

    def finish(self, moved):
        self.parts = [self.parts[0] + moved[0]]
        self.step += 1

    @property
    def done(self):
        return self.step == self.bits


def slot(sums, compute, token):
    live = [s for s in sums if not s.done]
    parts, token = lax.optimization_barrier(([s.parts for s in live], token))
    for one, held in zip(live, parts):
        one.parts = held
    moving = [s.start() for s in live]
    outs = compute(token) if compute else ()
    moving, outs, token = lax.optimization_barrier((moving, outs, token))
    for one, moved in zip(live, moving):
        one.finish(moved)
    return outs, token


def body(size, *arrays):
    (
        inputs, segments, valid, w_query, w_key, w_value, b_query, b_value, w_attn_out, b_attn_out,
        gain_one, shift_one, w_ffn_in, b_ffn_in, w_ffn_out, b_ffn_out, gain_two, shift_two, out_grad,
    ) = arrays
    side = lax.axis_index("narrow")
    rows = inputs.shape[0] // 2
    seqs = rows // SEQ_LEN
    head_width = w_query.shape[1]
    hidden = w_ffn_in.shape[1]
    pairs = head_width // PAIR
    token = side.astype(jnp.int32).reshape(1)
    row_block = 256
    blocks = rows // row_block

    def pair_of(array):
        return (array, swap_narrow(array))

    def join_rows(array, other):
        return jnp.where(
            side == 0,
            jnp.concatenate([array, other], 0),
            jnp.concatenate([other, array], 0),
        )

    wq, wk, wv = pair_of(w_query), pair_of(w_key), pair_of(w_value)
    wo = pair_of(w_attn_out)
    def packed(pieces, length):
        total = 0.0
        for at, vector in pieces:
            total += jnp.pad(vector.astype(f32), (at, length - at - vector.shape[0]))
        return total

    own_vectors = packed([(0, b_query), (head_width, b_value), (2 * head_width, b_ffn_in)], 3 * D)
    rest = [b_attn_out, b_ffn_out, gain_one, shift_one, gain_two, shift_two]
    vectors = packed(
        [(0, own_vectors), (3 * D, swap_narrow(own_vectors))] + [((6 + at) * D, v) for at, v in enumerate(rest)], 16 * D
    ).reshape(16, D)
    _, ffn_in, ffn_out = lax.optimization_barrier(((wq, wk, wv, wo, vectors), w_ffn_in, w_ffn_out))
    w1, w2 = (w_ffn_in, swap_narrow(ffn_in)), (w_ffn_out, swap_narrow(ffn_out))
    seg_rows = segments.reshape(-1, 1, SEQ_LEN)
    valid_seq = valid.reshape(-1, 1, SEQ_LEN)
    valid_block = valid.reshape(-1, 1, row_block)
    seq = (SEQ_LEN, D)
    blk = (row_block, D)
    low_rows = like((rows, D), bf16)
    full_rows = like((rows, D), f32)
    sums_shape = (like((8, D), f32), (8, D), "sum")

    queries, keys, values, probs, context, mixed = run_kernel(
        attend_kernel,
        seqs,
        token,
        [(inputs, seq, "shared"), (seg_rows, (1, 1, SEQ_LEN), "shared"), (valid_seq, (1, 1, SEQ_LEN), "shared")]
        + [whole(w) for w in wq + wk + wv + wo]
        + [whole(vectors)],
        [(low_rows, seq, "own")] * 3
        + [(like((seqs, 4 * pairs, SEQ_LEN, SEQ_LEN), bf16), (1, 4 * pairs, SEQ_LEN, SEQ_LEN), "own")]
        + [(low_rows, seq, "own"), (full_rows, seq, "own")],
        [pltpu.VMEM((SEQ_LEN, SEQ_LEN), f32)],
    )
    chunks = hidden // D
    row_shape = (rows, D)
    hidden_rows = like((rows, 2 * hidden), bf16)
    low_first, activated, slope, final, grad_second, low_second, vec_two = run_kernel(
        ffn_kernel,
        blocks,
        token,
        [(mixed, blk, "own"), (valid_block, (1, 1, row_block), "shared"), (out_grad, blk, "shared")]
        + [whole(w) for w in w1 + w2]
        + [whole(vectors)],
        [
            (low_rows, blk, "own"),
            (hidden_rows, (row_block, 2 * hidden), "own"),
            (hidden_rows, (row_block, 2 * hidden), "own"),
            (low_rows, blk, "own"),
            (full_rows, blk, "own"),
            (low_rows, blk, "own"),
            sums_shape,
        ],
        (),
    )

    def ffn_back(kernel, half, extra, outs, scratch, late=()):
        return run_kernel(
            kernel,
            chunks,
            token,
            [whole(a) for a in (low_second, low_first)]
            + [(a, (rows, D), lambda i, s: (0, half * chunks + i)) for a in (activated, slope)]
            + [(w1[half], (D, D), lambda i, s: (0, i)), (w2[half], (D, D), lambda i, s: (i, 0))]
            + extra
            + [(a, a.shape, "late") for a in late],
            [(like((2, chunks, D, D), bf16), (2, 1, D, D), lambda i, s: (0, i, 0, 0))] + outs,
            scratch
            + [pltpu.VMEM(row_shape, bf16)]
            + [pltpu.VMEM(a.shape, a.dtype) for a in late]
            + [pltpu.SemaphoreType.DMA((len(late),)) for _ in late[:1]],
        )

    valid_part = (valid_block, (blocks, 1, row_block), "side")
    sent, total, hidden_other = ffn_back(
        ffn_back_other_kernel, 1, [], [(full_rows, row_shape, "sum"), sums_shape], []
    )
    moved = swap_narrow(sent)
    own, grad_mixed, low_mixed, grad_context, hidden_own, vec_one = ffn_back(
        ffn_back_own_kernel,
        0,
        [valid_part, whole(vectors)],
        [(full_rows, row_shape, "sum"), (low_rows, row_shape, "sum"), (low_rows, row_shape, "sum"), sums_shape, sums_shape],
        [pltpu.VMEM(row_shape, f32)],
        (grad_second, total, mixed) + wo,
    )
    sum_ffn = WideSum(own.reshape(-1, D), moved.reshape(-1, D), size)

    def attend_back(token):
        def column(h, i, s):
            return (i, 1 - h)

        half_weights = like((4 * head_width, D), bf16)
        return tuple(
            run_kernel(
                attend_back_kernel,
                (2, seqs),
                token,
                [(a, (SEQ_LEN, head_width), column) for a in (queries, keys, values)]
                + [(probs, (1, 2 * pairs, SEQ_LEN, SEQ_LEN), lambda h, i, s: (i, 1 - h, 0, 0))]
                + [(a, (SEQ_LEN, head_width), column) for a in (context, grad_context)]
                + [(inputs, seq, lambda h, i, s: (s[0] * seqs + i, 0)), (low_mixed, seq, lambda h, i, s: (i, 0))],
                [
                    (
                        like((2, rows, 3 * head_width), bf16),
                        (1, SEQ_LEN, 3 * head_width),
                        lambda h, i, s: (1 - h, i, 0),
                    ),
                    (like((2, 8, 3 * head_width), f32), (1, 8, 3 * head_width), lambda h, i, s: (1 - h, 0, 0)),
                    (half_weights, half_weights.shape, "sum"),
                ],
                [pltpu.VMEM(half_weights.shape, f32)],
            )
        )

    def own_weights(token):
        return run_kernel(
            attend_weights_kernel,
            1,
            token,
            [
                (three, (1, rows, 3 * head_width), lambda i, s: (0, 0, 0)),
                (inputs, row_shape, "side"),
                (context, (rows, head_width), lambda i, s: (0, 0)),
                whole(low_mixed),
            ],
            [(like((4 * head_width, D), bf16), (4 * head_width, D), "sum")],
        )[0]

    (three, vec_three, sent), token = slot([sum_ffn], attend_back, token)
    (moved, own), token = slot([sum_ffn], lambda token: (swap_narrow(sent), own_weights(token)), token)
    sum_attn = WideSum(own, moved, size)

    def last(token):
        grad_in, vec_in = run_kernel(
            input_grad_kernel,
            seqs,
            token,
            [(grad_mixed, seq, "own"), (valid_seq, (1, 1, SEQ_LEN), "shared")]
            + [(three, (2, SEQ_LEN, 3 * head_width), lambda i, s: (0, i, 0))]
            + [whole(w) for w in wq + wk + wv],
            [(low_rows, seq, "own"), sums_shape],
        )
        lines = run_kernel(
            lines_kernel,
            1,
            token,
            [whole(v) for v in (vec_two, vec_one, vec_in, vec_three, hidden_own, hidden_other)],
            [(like((16, D), f32), (16, D), "sum")] * 2,
        )
        return (grad_in, *lines)

    (grad_in, lines_own, lines_sent, final_other), token = slot(
        [sum_ffn, sum_attn], lambda token: last(token) + (swap_narrow(final),), token
    )

    def place_ffn(token):
        return tuple(sum_ffn.result(place_ffn_kernel, [(hidden, D), (D, hidden)]))

    (output, grad_other, lines_moved), token = slot(
        [sum_ffn, sum_attn],
        lambda token: (join_rows(final, final_other), swap_narrow(grad_in), swap_narrow(lines_sent)),
        token,
    )
    small = SmallSum(lines_own + lines_moved, size)
    sums = [sum_ffn, sum_attn, small]
    (input_grad,), token = slot(sums, lambda token: (join_rows(grad_in, grad_other),), token)
    placed = None
    while not all(s.done for s in sums):
        late = sum_ffn.done and placed is None
        outs, token = slot(sums, place_ffn if late else None, token)
        placed = outs if late else placed
    d_w_out, d_w_in = placed
    small = small.parts[0]
    total = jnp.sum(jnp.stack([small[10], small[3], small[8], small[9]]), axis=1)
    rms = jnp.sqrt(total / (small[4, 0] * D))
    d_w_attn, *d_w_three = sum_attn.result(
        place_attend_kernel, [(head_width, D)] + [(D, head_width)] * 3, [pltpu.VMEM((4 * head_width, D), f32)]
    )
    return (
        output,
        input_grad,
        *d_w_three,
        small[11, :head_width],
        small[11, head_width:],
        d_w_attn,
        small[7],
        small[5],
        small[6],
        d_w_in,
        small[12 : 12 + chunks].reshape(-1),
        d_w_out,
        small[2],
        small[0],
        small[1],
        rms,
    )


def solution(mesh):
    row, col = P("narrow", None), P(None, "narrow")
    one, rows = P("narrow"), P("wide", None)
    in_specs = (
        rows, P("wide"), P("wide"), col, col, col, one, one, row, P(), P(), P(), col, one, row, P(), P(), P(), rows,
    )
    out_specs = (
        rows, rows, col, col, col, one, one, row, P(), P(), P(), col, one, row, P(), P(), P(), P(),
    )
    return jax.shard_map(
        partial(body, mesh.shape["wide"]), mesh=mesh, in_specs=in_specs, out_specs=out_specs, check_vma=False
    )
```
